32 devices in a mesh: head: 4 (over y, x), blk: 8 (over z, core).
Axes of the slice: x: 2, y: 2, z: 4, core: 2. Of those that a mesh axis runs over, the one named last changes fastest.
Arguments:
- tokens: bfloat16 [8192, 768], P(('blk', 'head')), may hold values from -6 to 6
- segment_ids: int32 [8192], P(('blk', 'head')), may hold values from 0 to 12, never falling along the last dimension, each value on 1 to 2000 neighbouring positions
- gains: float32 [1536], P(('head', 'blk')), may hold values from 0.5 to 1.5
- biases: float32 [7680], P(('head', 'blk')), may hold values from -0.6 to 0.6
- w_qkv: float32 [1769472], P(('head', 'blk')), may hold values from -0.21875 to 0.21875
- w_score: float32 [9216], P(('head', 'blk')), may hold values from -0.21875 to 0.21875
- w_out: float32 [589824], P(('head', 'blk')), may hold values from -1.75 to 1.75
- w_up: float32 [2359296], P(('head', 'blk')), may hold values from -0.21875 to 0.21875
- w_down: float32 [2359296], P(('head', 'blk')), may hold values from -0.109375 to 0.109375
- cotangent: bfloat16 [8192, 768], P(('blk', 'head')), may hold values from -6 to 6
Outputs:
- result: bfloat16 [8192, 768], P(('blk', 'head'))
- grad_tokens: bfloat16 [8192, 768], P(('blk', 'head'))
- grad_gains: float32 [1536], P(('head', 'blk'))
- grad_biases: float32 [7680], P(('head', 'blk'))
- grad_w_qkv: float32 [1769472], P(('head', 'blk'))
- grad_w_score: float32 [9216], P(('head', 'blk'))
- grad_w_out: float32 [589824], P(('head', 'blk'))
- grad_w_up: float32 [2359296], P(('head', 'blk'))
- grad_w_down: float32 [2359296], P(('head', 'blk'))
The draws below stay inside these ranges and needn't reach their ends.
Inputs may be any that keep to these rules, and one draw needn't show every extreme that they name: `segment_ids`: document ids never fall along the tokens; each document holds 1 to 2000 tokens, and one holds exactly 2000.
All inputs are finite; a program needn't handle non-finite values.
Results may differ from the reference program's by a relative error of at most 0.014.
Values may be sent and summed in bfloat16 or wider, within the bound.
No kernel may reach another device: no remote copies, remote signals or barrier semaphores. Data moves between devices by JAX's collectives and lax.ppermute only.
A program may use at most 192 MiB of HBM per device.

```python
import math
from functools import partial
import jax
import jax.numpy as jnp
import numpy as np
from jax import lax

D = 768
HEADS = 12
HDIM = 64
FF = 3072
WINDOW = 64
KEEP = 64
MOST = 2000
SEQS = 1
TOKENS = 8192
LENGTH = 8192
DOCS = 13


def shard_levels(stream_key, dims, pieces, low, high):
    loudness, own = 1.0, jax.random.fold_in(stream_key, 6)
    for dim, blocks in pieces:
        steps = jnp.exp(jax.random.uniform(jax.random.fold_in(own, dim), (blocks,), jnp.float32, low / len(pieces), high / len(pieces)))
        loudness = loudness * jnp.repeat(steps, dims[dim] // blocks).reshape([-1 if axis == dim else 1 for axis in range(len(dims))])
    return loudness


def split_up(count, total, most, lean):
    weights = [(1 << 20) // math.isqrt(standing ** lean) + 1 for standing in range(2, count + 1)]
    surplus, given = total - most - (count - 1), [1] * (count - 1)
    while surplus > 0:
        candidates = [i for i in range(count - 1) if given[i] < most]
        whole, remaining = sum([weights[i] for i in candidates]), surplus
        for i in candidates:
            extra = min(most - given[i], max(1, remaining * weights[i] // whole), surplus)
            given[i] = given[i] + extra
            surplus = surplus - extra
    return np.array([most] + given)


def ragged(rng, count, total, limit, lean):
    if count == 2:
        one = jax.random.randint(rng, (), max(1, total - limit), min(limit, total - 1) + 1)
        return jnp.stack([one, total - one])
    sizes = jnp.asarray(split_up(count, total, limit, lean), jnp.int32)
    pairs = (count - 1) // 2
    donor, taker = sizes[1:1 + 2 * pairs:2], sizes[2:2 + 2 * pairs:2]
    margin = jnp.minimum(donor - 1, limit - taker)
    passed = jax.random.randint(jax.random.fold_in(rng, 1), (pairs,), 0, 1 << 20) % (margin + 1)
    sizes = sizes.at[1:1 + 2 * pairs:2].set(donor - passed).at[2:2 + 2 * pairs:2].set(taker + passed)
    return sizes[jax.random.permutation(jax.random.fold_in(rng, 2), count)]


def bell_draw(stream_key, dims, scale, limit, pieces=(), held_as=jnp.bfloat16):
    result = scale * jax.random.normal(stream_key, dims, jnp.float32)
    if pieces:
        result = result * shard_levels(stream_key, dims, pieces, -0.22, 0.18)
    return jnp.clip(result, -limit, limit).astype(held_as)


def setup_inputs(seed: int = 0) -> dict:
    key_list = jax.random.split(jax.random.key(seed), 11)
    return {
        "tokens": bell_draw(key_list[0], (TOKENS, D), 1.0, 6.0, ((0, 32),)),
        "segment_ids": jnp.searchsorted(jnp.cumsum(ragged(key_list[1], DOCS, TOKENS, MOST, 1)), jnp.arange(TOKENS), side="right").astype(jnp.int32),
        "gains": jnp.clip(1.0 + 0.1 * jax.random.normal(key_list[2], (2 * D,), jnp.float32), 0.5, 1.5),
        "biases": bell_draw(key_list[3], (6 * D + FF,), 0.1, 0.6, ((0, 32),), jnp.float32),
        "w_qkv": bell_draw(key_list[4], (3 * D * D,), D ** -0.5, 0.21875, ((0, 32),), jnp.float32),
        "w_score": bell_draw(key_list[5], (D * HEADS,), D ** -0.5, 0.21875, ((0, 32),), jnp.float32),
        "w_out": bell_draw(key_list[6], (D * D,), (D // 64) ** -0.5, 1.75, ((0, 32),), jnp.float32),
        "w_up": bell_draw(key_list[7], (D * FF,), D ** -0.5, 0.21875, ((0, 32),), jnp.float32),
        "w_down": bell_draw(key_list[8], (FF * D,), FF ** -0.5, 0.109375, ((0, 32),), jnp.float32),
        "cotangent": bell_draw(key_list[9], (TOKENS, D), 1.0, 6.0, ((0, 32),)),
    }


EPS = 1e-05
HIGH = lax.Precision.HIGHEST

@jax.custom_vjp
def low(v):
    return lax.optimization_barrier(v.astype(jnp.bfloat16)).astype(jnp.float32)

@jax.custom_vjp
def low_back(v):
    return v

def low_keep(v):
    return (low(v), None)

def low_pass(kept, grad):
    return (grad,)

def back_keep(v):
    return (v, None)

def back_low(kept, grad):
    return (low(grad),)
low.defvjp(low_keep, low_pass)
low_back.defvjp(back_keep, back_low)

def layer_norm(row_values, gain_vec, shift_vec):
    centred = row_values - lax.optimization_barrier(jnp.mean(row_values, axis=-1, keepdims=True))
    spread = lax.optimization_barrier(jnp.mean(centred * centred, axis=-1, keepdims=True))
    return centred * lax.rsqrt(spread + EPS) * gain_vec + shift_vec

def tail_join(earlier, later):
    tail_a, sum_a = earlier
    tail_b, sum_b = later
    joined = (tail_a == tail_b)[..., None]
    return (tail_b, jnp.where(joined, sum_a + sum_b, sum_b))

def attend_block(qkv_one, score_one, threshold, keys_one, offset):
    block_rows = min(LENGTH, 512)
    span = min(LENGTH, block_rows + (MOST + block_rows - 1) // block_rows * block_rows)
    inv_root = 1.0 / math.sqrt(HDIM)
    begin = jnp.minimum(jnp.maximum(offset + block_rows - span, 0), LENGTH - span).astype(jnp.int32)
    queries = lax.dynamic_slice_in_dim(qkv_one[:, 0], offset, block_rows, 0)
    tau_rows = lax.dynamic_slice_in_dim(threshold, offset, block_rows, 0)
    query_keys = lax.dynamic_slice_in_dim(keys_one, offset, block_rows, 0)
    key_rows = lax.dynamic_slice_in_dim(qkv_one[:, 1], begin, span, 0)
    value_rows = lax.dynamic_slice_in_dim(qkv_one[:, 2], begin, span, 0)
    score_rows = lax.dynamic_slice_in_dim(score_one, begin, span, 0)
    key_ids = lax.dynamic_slice_in_dim(keys_one, begin, span, 0)
    positions = begin + jnp.arange(span, dtype=jnp.int32)
    query_pos = offset + jnp.arange(block_rows, dtype=jnp.int32)
    logits = jnp.einsum('qhd,khd->hqk', queries, key_rows, precision=HIGH) * inv_root
    sparse = jax.nn.log_sigmoid(score_rows.T[:, None, :] - tau_rows.T[:, :, None])
    nearby = query_pos[:, None] - positions[None, :] < WINDOW
    allowed = (key_ids[None, :] == query_keys[:, None]) & (positions[None, :] <= query_pos[:, None])
    scores_all = logits + jnp.where(nearby[None], jnp.zeros_like(sparse), sparse)
    scores_all = jnp.where(allowed[None], scores_all, -1e+30)
    attn_prob = jax.nn.softmax(scores_all, axis=-1)
    return jnp.einsum('hqk,khd->qhd', attn_prob, value_rows, precision=HIGH)

def one_sequence(packed):
    qkv_one, score_one, keys_one = packed
    _, totals = lax.associative_scan(tail_join, (keys_one, jnp.exp(score_one)), axis=0)
    threshold = jnp.log(totals) - math.log(KEEP)
    block_rows = min(LENGTH, 512)
    offsets = jnp.arange(LENGTH // block_rows, dtype=jnp.int32) * block_rows
    block_fn = jax.checkpoint(partial(attend_block, qkv_one, score_one, threshold, keys_one))
    outputs = lax.map(block_fn, offsets)
    return outputs.reshape(LENGTH, D)

def attention(mixed, scores, seg_keys):
    qkv_seq = mixed.reshape(SEQS, LENGTH, 3, HEADS, HDIM)
    score_seq = scores.reshape(SEQS, LENGTH, HEADS)
    key_seq = seg_keys.reshape(SEQS, LENGTH)
    return lax.map(one_sequence, (qkv_seq, score_seq, key_seq)).reshape(TOKENS, D)

def forward(seg_keys, tokens, gains, biases, w_qkv, w_score, w_out, w_up, w_down):
    gains = low(gains)
    biases = low(biases)
    mat_qkv = low(w_qkv).reshape(D, 3 * D)
    mat_score = low(w_score).reshape(D, HEADS)
    mat_out = low(w_out).reshape(D, D)
    mat_up = low(w_up).reshape(D, FF)
    mat_down = low(w_down).reshape(FF, D)
    gain_one = gains[:D]
    gain_two = gains[D:]
    shift_one = biases[:D]
    q_bias = biases[D:2 * D]
    v_bias = biases[2 * D:3 * D]
    out_bias = biases[3 * D:4 * D]
    shift_two = biases[4 * D:5 * D]
    up_bias = biases[5 * D:5 * D + FF]
    down_bias = biases[5 * D + FF:]
    normed = low(layer_norm(tokens, gain_one, shift_one))
    qkv_bias = jnp.concatenate([q_bias, jnp.zeros((D,), dtype=q_bias.dtype), v_bias])
    mixed = low(low_back(jnp.dot(normed, mat_qkv, precision=HIGH) + qkv_bias))
    scores = low(low_back(jnp.dot(normed, mat_score, precision=HIGH)))
    heads_out = attention(mixed, scores, seg_keys)
    attn_sent = low(low_back(heads_out))
    branch = low_back(jnp.dot(attn_sent, mat_out, precision=HIGH) + out_bias)
    middle = tokens + branch
    normed_two = low(layer_norm(middle, gain_two, shift_two))
    hidden_pre = low_back(jnp.dot(normed_two, mat_up, precision=HIGH) + up_bias)
    hidden = low(jax.nn.gelu(hidden_pre, approximate=True))
    return middle + jnp.dot(hidden, mat_down, precision=HIGH) + down_bias

def reference(tokens, segment_ids, gains, biases, w_qkv, w_score, w_out, w_up, w_down, cotangent):
    seq_index = jnp.arange(TOKENS, dtype=jnp.int32) // LENGTH
    seg_keys = (segment_ids * SEQS + seq_index).astype(jnp.int32)
    output, pull = jax.vjp(partial(forward, seg_keys), tokens.astype(jnp.float32), gains, biases, w_qkv, w_score, w_out, w_up, w_down)
    grads = pull(cotangent.astype(jnp.float32))
    return (output.astype(jnp.bfloat16), grads[0].astype(jnp.bfloat16), grads[1], grads[2], grads[3], grads[4], grads[5], grads[6], grads[7])
```

```python
import functools
import math

import jax
import jax.numpy as jnp
from jax import lax
from jax.experimental import pallas as pl
from jax.experimental.pallas import tpu as pltpu
from jax.sharding import Mesh
from jax.sharding import PartitionSpec as P

D = 768
HEADS = 12
HDIM = 64
FF = 3072
WINDOW = 64
KEEP = 64
MOST = 2000

EPS = 1e-05
NEGATIVE = -1e30
TINY = 1e-37
TILE = 256
ROOT = 1.0 / math.sqrt(HDIM)
F32 = jnp.float32
BF16 = jnp.bfloat16
ALL = ("head", "pair", "core")
SAME = ("head", "pair")


def dot_nn(a, b):
    return lax.dot_general(a, b, (((1,), (0,)), ((), ())), preferred_element_type=F32)


def dot_nt(a, b):
    return lax.dot_general(a, b, (((1,), (1,)), ((), ())), preferred_element_type=F32)


def dot_tn(a, b):
    return lax.dot_general(a, b, (((0,), (0,)), ((), ())), preferred_element_type=F32)


def tile_place(core, rel, k, count):
    return k + count * ((core + rel + k) & 1)


def fill_window(core, count, kv_refs, s_refs, kvw, kvt, ew, first):
    eye = (
        lax.broadcasted_iota(jnp.int32, (128, 128), 0)
        == lax.broadcasted_iota(jnp.int32, (128, 128), 1)
    ).astype(BF16)
    for part in range(2):
        for rel in range(2):
            for k in range(count):
                place = 2 * count * part + tile_place(core, rel, k, count)

                @pl.when(place >= first)
                def _(part=part, rel=rel, k=k, place=place):
                    block = kv_refs[2 * part + rel][k]
                    kvw[place] = block
                    rows = s_refs[2 * part + rel][:, k * TILE : (k + 1) * TILE].astype(F32)
                    cols = jnp.transpose(jnp.exp(rows))
                    for h in range(3):
                        kvt[place, h * 128 : (h + 1) * 128, :] = dot_nt(
                            eye, block[:, h * 128 : (h + 1) * 128]
                        ).astype(BF16)
                        ew[place * 3 + h] = jnp.broadcast_to(cols[:, h : h + 1], (TILE, 128))


def twice(x):
    return jnp.concatenate([x, x], axis=1)


def key_iota():
    return lax.broadcasted_iota(jnp.int32, (TILE, TILE), 0)


def query_iota():
    return lax.broadcasted_iota(jnp.int32, (1, TILE), 1)


def fwd_kernel(count, sc, q_ref, kv0, kv1, kv2, kv3, s0, s1, s2, s3, ds_ref,
               o_ref, ot_ref, st_ref, kvw, kvt, ew, acc):
    core = sc[0]
    fill_window(core, count, (kv2, kv3, kv0, kv1), (s2, s3, s0, s1), kvw, kvt, ew, sc[1])

    def one_tile(k, unused):
        place = 2 * count + k + count * ((core + k) & 1)
        low = sc[2 + k]
        ds_row = ds_ref[k][0:1, :]
        q_all = q_ref[k]
        lane = lax.broadcasted_iota(jnp.int32, (TILE, 128), 1)
        zero = jnp.zeros((TILE, 64), BF16)
        q_pad = [
            jnp.concatenate([q_all[:, 64 * h : 64 * h + 64], zero], axis=1) * BF16(ROOT)
            for h in range(3)
        ]
        tile_start = place * TILE
        k_io = key_iota()
        inside = (k_io >= ds_row - tile_start) & (k_io <= query_iota())
        ds_first = jnp.broadcast_to(jnp.min(ds_row, axis=1, keepdims=True), (1, 128))

        def carry_step(j, sums):
            keep = lax.broadcasted_iota(jnp.int32, (TILE, 128), 0) >= ds_first - j * TILE
            return tuple(
                sums[h] + jnp.sum(jnp.where(keep, ew[j * 3 + h], 0.0), axis=0, keepdims=True)
                for h in range(3)
            )

        carried = lax.fori_loop(low, place, carry_step, (jnp.zeros((1, 128), F32),) * 3)
        starts_before = ds_row < tile_start
        p_rows = []
        for h in range(3):
            local = jnp.sum(jnp.where(inside, twice(ew[place * 3 + h]), 0.0), axis=0, keepdims=True)
            prefix = local + jnp.where(starts_before, twice(carried[h]), 0.0)
            p_rows.append(jnp.maximum(prefix * (1.0 / KEEP), TINY))

        acc[...] = jnp.zeros_like(acc)

        def chunk(j, state, edge):
            k_io = key_iota()
            mask = k_io >= ds_row - j * TILE
            if edge:
                ahead = query_iota() + (place - j) * TILE
                mask = mask & (k_io <= ahead)
                near = k_io > ahead - WINDOW
            out = []
            for h in range(3):
                m_old, l_old = state[2 * h], state[2 * h + 1]
                z = dot_nt(kvw[j, :, h * 128 : (h + 1) * 128], q_pad[h])
                z = jnp.where(mask, z, NEGATIVE)
                m_new = jnp.maximum(m_old, jnp.max(z, axis=0, keepdims=True))
                e = twice(ew[j * 3 + h])
                sig = e / (e + p_rows[h])
                if edge:
                    sig = jnp.where(near, 1.0, sig)
                prob = jnp.exp(z - m_new) * sig
                alpha = jnp.exp(m_old - m_new)
                l_new = l_old * alpha + jnp.sum(prob, axis=0, keepdims=True)
                acc[h] = acc[h] * alpha + dot_nn(
                    kvt[j, h * 128 + 64 : (h + 1) * 128, :], prob.astype(BF16)
                )
                out += [m_new, l_new]
            return tuple(out)

        state = (jnp.full((1, TILE), NEGATIVE, F32), jnp.zeros((1, TILE), F32)) * 3
        edge_low = jnp.maximum(place - 1, low)
        state = lax.fori_loop(low, edge_low, lambda j, s: chunk(j, s, False), state)
        state = lax.fori_loop(edge_low, place + 1, lambda j, s: chunk(j, s, True), state)
        outs = []
        for h in range(3):
            outs.append(acc[h] / state[2 * h + 1])
        stacked = jnp.concatenate(outs, axis=0)
        ot_ref[k] = stacked
        o_ref[k] = jnp.transpose(stacked).astype(BF16)
        lse = [state[2 * h] + jnp.log(state[2 * h + 1]) for h in range(3)]
        st_ref[k] = jnp.concatenate(lse + p_rows + [jnp.zeros((2, TILE), F32)], axis=0)
        return unused

    lax.fori_loop(0, count, one_tile, 0)


def bwd_kernel(count, sc, q_ref, do_ref, ot_ref, st_ref, kv0, kv1, kv2, kv3, s0, s1, s2, s3, ds_ref,
               dq_ref, own_ref, sib_ref, prev_ref, cross_ref, sown_ref, ssib_ref, sprev_ref, scross_ref,
               kvw, kvt, ew, dkv, dsl, dqt):
    core = sc[0]
    first = sc[1]
    fill_window(core, count, (kv2, kv3, kv0, kv1), (s2, s3, s0, s1), kvw, kvt, ew, first)
    dkv[...] = jnp.zeros_like(dkv)
    dsl[...] = jnp.zeros_like(dsl)
    eye = (
        lax.broadcasted_iota(jnp.int32, (64, 64), 0) == lax.broadcasted_iota(jnp.int32, (64, 64), 1)
    ).astype(BF16)

    def one_tile(k, unused):
        place = 2 * count + k + count * ((core + k) & 1)
        low = sc[2 + k]
        ds_row = ds_ref[k][0:1, :]
        tile_start = place * TILE
        q_all = q_ref[k]
        do_all = do_ref[k]
        stats = st_ref[k]
        ot = ot_ref[k]
        zero = jnp.zeros((TILE, 64), BF16)
        qd, q_pad, do_pad, delta = [], [], [], []
        for h in range(3):
            qh = q_all[:, 64 * h : 64 * h + 64] * BF16(ROOT)
            dh = do_all[:, 64 * h : 64 * h + 64]
            q_pad.append(jnp.concatenate([qh, zero], axis=1))
            do_pad.append(jnp.concatenate([zero, dh], axis=1))
            qd.append(jnp.concatenate([q_pad[h], do_pad[h]], axis=0))
            dht = dot_nt(eye, dh)
            delta.append(jnp.sum(dht * ot[64 * h : 64 * h + 64, :], axis=0, keepdims=True))
        dqt[...] = jnp.zeros_like(dqt)

        def chunk(j, state, edge):
            k_io = key_iota()
            mask = k_io >= ds_row - j * TILE
            if edge:
                ahead = query_iota() + (place - j) * TILE
                mask = mask & (k_io <= ahead)
                near = k_io > ahead - WINDOW
            out = []
            for h in range(3):
                kv = kvw[j, :, h * 128 : (h + 1) * 128]
                z = dot_nt(kv, q_pad[h])
                dp = dot_nt(kv, do_pad[h])
                p_row = stats[3 + h : 4 + h, :]
                e = twice(ew[j * 3 + h])
                r = 1.0 / (e + p_row)
                sig = e * r
                if edge:
                    sig = jnp.where(near, 1.0, sig)
                prob = jnp.exp(jnp.where(mask, z - stats[h : h + 1, :], NEGATIVE)) * sig
                dz = prob * (dp - delta[h])
                far = dz * (p_row * r)
                if edge:
                    far = jnp.where(near, 0.0, far)
                out.append(state[h] - jnp.sum(far, axis=0, keepdims=True))
                dsl[j * 3 + h] += far[:, :128] + far[:, 128:]
                dz_low = dz.astype(BF16)
                dqt[h] += dot_nn(kvt[j, h * 128 : h * 128 + 64, :], dz_low)
                dkv[j, :, h * 128 : (h + 1) * 128] += dot_nn(
                    jnp.concatenate([dz_low, prob.astype(BF16)], axis=1), qd[h]
                )
            return tuple(out)

        state = (jnp.zeros((1, TILE), F32),) * 3
        edge_low = jnp.maximum(place - 1, low)
        state = lax.fori_loop(low, edge_low, lambda j, s: chunk(j, s, False), state)
        state = lax.fori_loop(edge_low, place + 1, lambda j, s: chunk(j, s, True), state)
        dq_ref[k] = (
            jnp.transpose(jnp.concatenate([dqt[0], dqt[1], dqt[2]], axis=0)) * ROOT
        ).astype(BF16)

        k_io = key_iota()
        inside = (k_io >= ds_row - tile_start) & (k_io <= query_iota())
        starts_before = ds_row < tile_start
        ds_first = jnp.broadcast_to(jnp.min(ds_row, axis=1, keepdims=True), (1, 128))
        w_row, w_lane = [], []
        for h in range(3):
            w = state[h] / (stats[3 + h : 4 + h, :] * float(KEEP))
            w_row.append(w)
            before = jnp.where(starts_before, w, 0.0)
            w_lane.append(before[:, :128] + before[:, 128:])
            here = jnp.where(inside, w, 0.0)
            dsl[place * 3 + h] += ew[place * 3 + h] * (here[:, :128] + here[:, 128:])

        def later(j, unused):
            keep = lax.broadcasted_iota(jnp.int32, (TILE, 128), 0) >= ds_first - j * TILE
            for h in range(3):
                dsl[j * 3 + h] += jnp.where(keep, ew[j * 3 + h] * w_lane[h], 0.0)
            return unused

        lax.fori_loop(low, place, later, 0)
        return unused

    lax.fori_loop(0, count, one_tile, 0)

    outs = ((prev_ref, sprev_ref), (cross_ref, scross_ref), (own_ref, sown_ref), (sib_ref, ssib_ref))
    for part in range(2):
        for rel in range(2):
            big, small = outs[2 * part + rel]
            for k in range(count):
                place = 2 * count * part + tile_place(core, rel, k, count)
                big[k] = dkv[place].astype(big.dtype)
                cols = [jnp.sum(dsl[place * 3 + h], axis=1, keepdims=True) for h in range(3)]
                cols = jnp.concatenate([jnp.broadcast_to(c, (TILE, 128)) for c in cols], axis=1)
                rows = jnp.concatenate(
                    [jnp.transpose(cols[:, 128 * h : 128 * h + 128])[0:1, :] for h in range(3)]
                    + [jnp.zeros((5, TILE), F32)],
                    axis=0,
                )
                small[:, k * TILE : (k + 1) * TILE] = rows.astype(small.dtype)


VM = pl.BlockSpec(memory_space=pltpu.VMEM)
SM = pl.BlockSpec(memory_space=pltpu.SMEM)
LIMIT = 60 * 1024 * 1024


def attend_forward(count, scal, q, kvs, ss, ds):
    shapes = (
        jax.ShapeDtypeStruct((count, TILE, 192), BF16),
        jax.ShapeDtypeStruct((count, 192, TILE), F32),
        jax.ShapeDtypeStruct((count, 8, TILE), F32),
    )
    return pl.pallas_call(
        functools.partial(fwd_kernel, count),
        out_shape=shapes,
        in_specs=[SM] + [VM] * 10,
        out_specs=(VM,) * 3,
        scratch_shapes=[
            pltpu.VMEM((4 * count, TILE, 384), BF16),
            pltpu.VMEM((4 * count, 384, TILE), BF16),
            pltpu.VMEM((4 * count * 3, TILE, 128), F32),
            pltpu.VMEM((3, 64, TILE), F32),
        ],
        compiler_params=pltpu.CompilerParams(vmem_limit_bytes=LIMIT),
        name="attend_forward",
    )(scal, q, *kvs, *ss, ds)


def attend_backward(count, scal, q, do, ot, st, kvs, ss, ds):
    rows = count * TILE
    shapes = (
        jax.ShapeDtypeStruct((count, TILE, 192), BF16),
        jax.ShapeDtypeStruct((count, TILE, 384), F32),
        jax.ShapeDtypeStruct((count, TILE, 384), BF16),
        jax.ShapeDtypeStruct((count, TILE, 384), F32),
        jax.ShapeDtypeStruct((count, TILE, 384), BF16),
        jax.ShapeDtypeStruct((8, rows), F32),
        jax.ShapeDtypeStruct((8, rows), BF16),
        jax.ShapeDtypeStruct((8, rows), F32),
        jax.ShapeDtypeStruct((8, rows), BF16),
    )
    return pl.pallas_call(
        functools.partial(bwd_kernel, count),
        out_shape=shapes,
        in_specs=[SM] + [VM] * 13,
        out_specs=(VM,) * 9,
        scratch_shapes=[
            pltpu.VMEM((4 * count, TILE, 384), BF16),
            pltpu.VMEM((4 * count, 384, TILE), BF16),
            pltpu.VMEM((4 * count * 3, TILE, 128), F32),
            pltpu.VMEM((4 * count, TILE, 384), F32),
            pltpu.VMEM((4 * count * 3, TILE, 128), F32),
            pltpu.VMEM((3, 64, TILE), F32),
        ],
        compiler_params=pltpu.CompilerParams(vmem_limit_bytes=LIMIT),
        name="attend_backward",
    )(scal, q, do, ot, st, *kvs, *ss, ds)


def other_core(x):
    return lax.ppermute(x, "core", [(0, 1), (1, 0)])


def next_chip(x, step):
    n = lax.axis_size("pair")
    return lax.ppermute(x, "pair", [(i, i + step) for i in range(n) if 0 <= i + step < n])


def spread(x, axes):
    n = lax.axis_size(axes)
    return lax.all_to_all(jnp.broadcast_to(x[None], (n,) + x.shape), axes, 0, 0)


def both_cores(mine, theirs, core, axis):
    return jnp.where(
        core == 0, jnp.stack([mine, theirs], axis), jnp.stack([theirs, mine], axis)
    )


def normalize(rows):
    centred = rows - jnp.mean(rows, axis=-1, keepdims=True)
    scale = lax.rsqrt(jnp.mean(centred * centred, axis=-1, keepdims=True) + EPS)
    return centred * scale, scale


def norm_pull(grad, unit, scale, gain):
    inner = grad * gain
    return scale * (
        inner
        - jnp.mean(inner, axis=-1, keepdims=True)
        - unit * jnp.mean(inner * unit, axis=-1, keepdims=True)
    )


def shards(tokens, segment_ids, gains, biases, w_qkv, w_score, w_out, w_up, w_down, cotangent):
    groups = lax.axis_size("head")
    pairs = lax.axis_size("pair")
    devices = groups * pairs * 2
    same = groups * pairs
    h = lax.axis_index("head")
    p = lax.axis_index("pair")
    c = lax.axis_index("core")
    tok = tokens.shape[0]
    block = groups * tok
    count = groups
    super_rows = 2 * block
    total = super_rows * pairs
    rows_l = D // devices
    down_l = FF // devices
    swaps = (h & 1) == 1

    x_other = other_core(tokens)
    dy_other = other_core(cotangent)
    x_mine = jnp.where(swaps, x_other, tokens)
    dy_mine = jnp.where(swaps, dy_other, cotangent)
    dy_sib = jnp.where(swaps, cotangent, dy_other)

    n_gain, n_bias, n_score = gains.shape[0], biases.shape[0], w_score.shape[0]
    aux = jnp.concatenate(
        [gains.astype(BF16), biases.astype(BF16), segment_ids.astype(BF16), w_score.astype(BF16)]
    )
    aux_n = -(-aux.shape[0] // 1024) * 1024
    aux = jnp.pad(aux, (0, aux_n - aux.shape[0])).reshape(-1, 128)
    aux_same = spread(aux, SAME)
    x_all = spread(x_mine, "head")

    part = w_qkv.astype(BF16).reshape(rows_l, 3, groups, 3, HDIM)
    part_q = part[:, 0].reshape(rows_l, groups, 192)
    part_kv = part[:, 1:].transpose(0, 2, 3, 1, 4).reshape(rows_l, groups, 384)
    part = jnp.concatenate([part_q, part_kv], axis=-1).transpose(1, 0, 2)
    part = jnp.broadcast_to(part[:, None], (groups, pairs, rows_l, 576)).reshape(same, rows_l, 576)
    w_same = lax.all_to_all(part, SAME, 0, 0)
    w_both = both_cores(w_same, other_core(w_same), c, 1)
    w_slice = w_both.reshape(D, 576)
    w_q, w_kv = w_slice[:, :192], w_slice[:, 192:]

    aux_all = both_cores(aux_same, other_core(aux_same), c, 1).reshape(devices, aux_n)
    gain_all = aux_all[:, :n_gain].reshape(-1).astype(F32)
    bias_all = aux_all[:, n_gain : n_gain + n_bias].reshape(-1).astype(F32)
    n_ids = n_gain + n_bias + tok
    ids_all = aux_all[:, n_gain + n_bias : n_ids].astype(jnp.int32)
    score_all = aux_all[:, n_ids : n_ids + n_score].reshape(D, HEADS)
    ids_all = ids_all.reshape(groups, pairs, 2, tok).transpose(1, 2, 0, 3).reshape(total)
    gain_one, gain_two = gain_all[:D], gain_all[D:]
    shift_one, q_bias, v_bias, out_bias, shift_two = (
        bias_all[i * D : (i + 1) * D] for i in range(5)
    )
    up_bias = bias_all[5 * D : 5 * D + FF]
    down_bias = bias_all[5 * D + FF :]

    up_rows = w_up.astype(BF16).reshape(rows_l, same, 2, down_l)
    up_mine = jnp.where(c == 0, up_rows[:, :, 0], up_rows[:, :, 1]).reshape(rows_l, FF // 2)
    up_send = jnp.where(c == 0, up_rows[:, :, 1], up_rows[:, :, 0]).reshape(rows_l, FF // 2)
    up_both = both_cores(up_mine, other_core(up_send), c, 0).reshape(2 * rows_l, FF // 2)
    down_mine = w_down.astype(BF16).reshape(down_l, D)
    out_mine = w_out.astype(BF16).reshape(rows_l, D)
    pack = jnp.concatenate([down_mine, up_both[:, :D], up_both[:, D:], out_mine], axis=0)
    packed = lax.all_gather(pack, SAME, axis=0, tiled=False)
    a, b, e = down_l, down_l + 2 * rows_l, down_l + 4 * rows_l
    m_down = packed[:, :a].reshape(FF // 2, D)
    m_up0 = packed[:, a:b].reshape(D, D)
    m_up1 = packed[:, b:e].reshape(D, D)
    out_same = packed[:, e:]
    m_out = both_cores(out_same, other_core(out_same), c, 1).reshape(D, D)

    padded = jnp.concatenate([jnp.full((super_rows,), -1, jnp.int32), ids_all])
    ids_win = lax.dynamic_slice_in_dim(padded, p * super_rows, 2 * super_rows)
    ids_super = ids_win[super_rows:].reshape(2, count, TILE)
    upper = ((jnp.arange(count) + c) & 1 == 1)[:, None]
    ids_q = jnp.where(upper, ids_super[1], ids_super[0])
    starts = jnp.sum(
        (ids_win[None, :, None] < ids_q[:, None, :]).astype(jnp.int32), axis=1
    )
    lows = jnp.min(starts, axis=1) // TILE
    scal = jnp.concatenate([c[None], jnp.min(lows)[None], lows]).astype(jnp.int32)
    ds = jnp.broadcast_to(starts[:, None, :], (count, 8, TILE))

    x_rows = x_all.reshape(block, D).astype(F32)
    unit_one, scale_one = normalize(x_rows)
    normed = (unit_one * gain_one + shift_one).astype(BF16)
    w_s = lax.dynamic_slice_in_dim(score_all.T, 3 * h, 3, axis=0)
    w_s = jnp.pad(w_s, ((0, 5), (0, 0)))
    scores = dot_nt(w_s, normed).astype(BF16)
    s_sib = other_core(scores)
    s_prev = next_chip(jnp.stack([scores, s_sib]), 1)
    bias_q = lax.dynamic_slice_in_dim(q_bias, 192 * h, 192)
    bias_v = lax.dynamic_slice_in_dim(v_bias, 192 * h, 192).reshape(3, 1, HDIM)
    bias_kv = jnp.concatenate([jnp.zeros_like(bias_v), bias_v], axis=1).reshape(384)
    kv = (dot_nn(normed, w_kv) + bias_kv).astype(BF16).reshape(count, TILE, 384)
    q = (dot_nn(normed, w_q) + bias_q).astype(BF16).reshape(count, TILE, 192)
    kv_prev = next_chip(kv, 1)
    kv_sib = other_core(kv)
    kv_cross = other_core(kv_prev)
    kvs = (kv, kv_sib, kv_prev, kv_cross)
    ss = (scores, s_sib, s_prev[0], s_prev[1])
    o, ot, st = attend_forward(count, scal, q, kvs, ss, ds)

    attn = lax.all_to_all(o, "head", 0, 0)
    attn = attn.transpose(1, 0, 2).reshape(tok, D)
    middle = x_mine.astype(F32) + dot_nn(attn, m_out) + out_bias
    unit_two, scale_two = normalize(middle)
    n_two = (unit_two * gain_two + shift_two).astype(BF16)
    n_pair = jnp.concatenate([n_two, other_core(n_two)], axis=0)
    dy_pair = jnp.concatenate([dy_mine, dy_sib], axis=0)
    stripes = up_bias.reshape(same, 2, down_l)
    up_half = jnp.where(c == 0, stripes[:, 0], stripes[:, 1]).reshape(FF // 2)
    d_hidden = dot_nt(dy_pair, m_down)
    up_pre = jnp.concatenate([dot_nn(n_pair, m_up0), dot_nn(n_pair, m_up1)], axis=1) + up_half
    c0 = math.sqrt(2.0 / math.pi)
    squared = up_pre * up_pre
    th = jnp.tanh(c0 * up_pre * (1.0 + 0.044715 * squared))
    hidden = (0.5 * up_pre * (1.0 + th)).astype(BF16)
    slope = 0.5 * (1.0 + th) + 0.5 * up_pre * (1.0 - th * th) * c0 * (1.0 + 3 * 0.044715 * squared)
    d_up_f = d_hidden * slope
    d_up = d_up_f.astype(BF16)
    d_two_part = dot_nt(d_up[:, :D], m_up0) + dot_nt(d_up[:, D:], m_up1)
    d_two = d_two_part[:tok] + other_core(d_two_part[tok:].astype(BF16)).astype(F32)
    y_part = dot_nn(hidden, m_down)
    y = y_part[:tok] + other_core(y_part[tok:])
    result_mine = (middle + y + down_bias).astype(BF16)
    result = jnp.where(swaps, other_core(result_mine), result_mine)

    g_down = dot_tn(hidden, dy_pair)
    g_up0 = dot_tn(n_pair, d_up[:, :D])
    g_up1 = dot_tn(n_pair, d_up[:, D:])
    g_up_bias = jnp.sum(d_up.astype(F32), axis=0)
    g_gain_two = jnp.sum(d_two * unit_two, axis=0)
    g_shift_two = jnp.sum(d_two, axis=0)
    dy_f = dy_mine.astype(F32)
    g_down_bias = jnp.sum(dy_f, axis=0)

    d_middle = dy_f + norm_pull(d_two, unit_two, scale_two, gain_two)
    d_branch = d_middle.astype(BF16)
    g_out_bias = jnp.sum(d_branch.astype(F32), axis=0)
    d_sent = dot_nt(d_branch, m_out).astype(BF16)
    d_heads = lax.all_to_all(d_sent.reshape(tok, groups, 192).transpose(1, 0, 2), "head", 0, 0)
    g_out = dot_tn(attn, d_branch)

    g_out_rows = g_out.reshape(same, 2, rows_l, D)
    g_out_keep = jnp.where(c == 0, g_out_rows[:, 0], g_out_rows[:, 1])
    g_out_send = jnp.where(c == 0, g_out_rows[:, 1], g_out_rows[:, 0]).astype(BF16)
    g_out_same = (g_out_keep + other_core(g_out_send).astype(F32)).astype(BF16)
    g_pack = jnp.concatenate(
        [
            g_down.astype(BF16).reshape(same, down_l, D),
            g_up0.astype(BF16).reshape(same, 2 * rows_l, D),
            g_up1.astype(BF16).reshape(same, 2 * rows_l, D),
            g_out_same,
        ],
        axis=1,
    ).reshape(groups, pairs, e + rows_l, D)
    g_pack = lax.psum_scatter(g_pack, "head", scatter_dimension=0, tiled=False)
    g_pack = lax.psum_scatter(g_pack, "pair", scatter_dimension=0, tiled=False).astype(F32)
    grad_w_down = g_pack[:a].reshape(-1)
    grad_w_out = g_pack[e:].reshape(-1)
    g_up_rows = jnp.concatenate([g_pack[a:b], g_pack[b:e]], axis=1).reshape(2, rows_l, FF // 2)
    g_up_keep = jnp.where(c == 0, g_up_rows[0], g_up_rows[1])
    g_up_came = other_core(jnp.where(c == 0, g_up_rows[1], g_up_rows[0]))
    grad_w_up = both_cores(
        g_up_keep.reshape(rows_l, same, down_l), g_up_came.reshape(rows_l, same, down_l), c, 2
    ).reshape(-1)

    dq, own, to_sib, prev, to_cross, s_own, s_to_sib, s_back, s_to_cross = attend_backward(
        count, scal, q, d_heads, ot, st, kvs, ss, ds
    )
    back = next_chip((prev + other_core(to_cross).astype(F32)).astype(BF16), -1)
    s_back = next_chip((s_back + other_core(s_to_cross).astype(F32)).astype(BF16), -1)
    d_kv = own + other_core(to_sib).astype(F32) + back.astype(F32)
    d_s = s_own + other_core(s_to_sib).astype(F32) + s_back.astype(F32)
    d_kv = d_kv.astype(BF16).reshape(block, 384)
    d_q = dq.reshape(block, 192)
    d_s = d_s.astype(BF16)

    d_normed = dot_nt(d_q, w_q) + dot_nt(d_kv, w_kv) + dot_tn(d_s, w_s)
    d_norm_parts = lax.all_to_all(d_normed.astype(BF16).reshape(groups, tok, D), "head", 0, 0)
    g_q = dot_tn(normed, d_q)
    g_kv = dot_tn(normed, d_kv)
    g_s = dot_nn(d_s, normed)
    g_gain_one = jnp.sum(d_normed * unit_one, axis=0)
    g_shift_one = jnp.sum(d_normed, axis=0)
    g_q_bias = jnp.sum(d_q.astype(F32), axis=0)
    g_v_bias = jnp.sum(d_kv.astype(F32), axis=0).reshape(3, 2, HDIM)[:, 1].reshape(192)

    g_slice = jnp.concatenate([g_q, g_kv], axis=1).reshape(same, 2, rows_l, 576)
    g_keep = jnp.where(c == 0, g_slice[:, 0], g_slice[:, 1])
    g_send = jnp.where(c == 0, g_slice[:, 1], g_slice[:, 0]).astype(BF16)
    g_same = (g_keep + other_core(g_send).astype(F32)).astype(BF16)
    g_rows = lax.all_to_all(g_same, SAME, 0, 0).reshape(groups, pairs, rows_l, 576)
    g_rows = jnp.sum(g_rows.astype(F32), axis=1)
    grad_q = g_rows[:, :, :192].transpose(1, 0, 2).reshape(rows_l, 1, D)
    grad_kv = g_rows[:, :, 192:].reshape(groups, rows_l, 3, 2, HDIM)
    grad_kv = grad_kv.transpose(1, 3, 0, 2, 4).reshape(rows_l, 2, D)
    grad_w_qkv = jnp.concatenate([grad_q, grad_kv], axis=1).reshape(-1)

    zeros_d = jnp.zeros((D,), F32)
    halves = jnp.stack([g_up_bias.reshape(same, down_l), jnp.zeros((same, down_l), F32)], axis=1)
    halves = jnp.where(c == 0, halves, halves[:, ::-1]).reshape(FF)
    score_cols = lax.dynamic_update_slice_in_dim(jnp.zeros((HEADS, D), F32), g_s[:3], 3 * h, 0).T
    small = jnp.concatenate(
        [
            jnp.concatenate([g_gain_one, g_gain_two]).reshape(devices, n_gain),
            jnp.concatenate(
                [
                    g_shift_one,
                    lax.dynamic_update_slice_in_dim(zeros_d, g_q_bias, 192 * h, 0),
                    lax.dynamic_update_slice_in_dim(zeros_d, g_v_bias, 192 * h, 0),
                    g_out_bias,
                    g_shift_two,
                    halves,
                    g_down_bias,
                ]
            ).reshape(devices, n_bias),
            score_cols.reshape(devices, n_score),
        ],
        axis=1,
    )
    width = -(-small.shape[1] // 128) * 128
    small = jnp.pad(small, ((0, 0), (0, width - small.shape[1])))
    small = jnp.sum(lax.all_to_all(small, ALL, 0, 0, tiled=True), axis=0)
    grad_gains = small[:n_gain]
    grad_biases = small[n_gain : n_gain + n_bias]
    grad_w_score = small[n_gain + n_bias : n_gain + n_bias + n_score]

    d_norm_sum = jnp.sum(d_norm_parts.astype(F32), axis=0)
    unit_mine, scale_mine = normalize(x_mine.astype(F32))
    grad_mine = (d_middle + norm_pull(d_norm_sum, unit_mine, scale_mine, gain_one)).astype(BF16)
    grad_tokens = jnp.where(swaps, other_core(grad_mine), grad_mine)
    return (
        result,
        grad_tokens,
        grad_gains,
        grad_biases,
        grad_w_qkv,
        grad_w_score,
        grad_w_out,
        grad_w_up,
        grad_w_down,
    )


def solution(mesh):
    groups = mesh.devices.shape[0]
    fine = Mesh(mesh.devices.reshape(groups, -1, 2), ALL)
    rows = P(("pair", "core", "head"), None)
    flat = P(ALL)
    in_specs = (rows, P(("pair", "core", "head"))) + (flat,) * 7 + (rows,)
    out_specs = (rows, rows) + (flat,) * 7
    return jax.shard_map(shards, mesh=fine, in_specs=in_specs, out_specs=out_specs, check_vma=False)
```

```python
import functools
import math

import jax
import jax.numpy as jnp
from jax import lax
from jax.experimental import pallas as pl
from jax.experimental.pallas import tpu as pltpu
from jax.sharding import Mesh
from jax.sharding import PartitionSpec as P

D = 768
HEADS = 12
HDIM = 64
FF = 3072
WINDOW = 64
KEEP = 64
MOST = 2000

EPS = 1e-05
NEGATIVE = -1e30
TINY = 1e-37
TILE = 256
ROOT = 1.0 / math.sqrt(HDIM)
F32 = jnp.float32
BF16 = jnp.bfloat16
ALL = ("head", "pair", "core")
SAME = ("head", "pair")


def dot_nn(a, b):
    return lax.dot_general(a, b, (((1,), (0,)), ((), ())), preferred_element_type=F32)


def dot_nt(a, b):
    return lax.dot_general(a, b, (((1,), (1,)), ((), ())), preferred_element_type=F32)


def dot_tn(a, b):
    return lax.dot_general(a, b, (((0,), (0,)), ((), ())), preferred_element_type=F32)


def tile_place(sc, r, rel, count):
    k = sc[1] ^ r
    return k + count * ((sc[0] + rel + k) & 1)


def fill_window(sc, count, base, kv_refs, s_refs, kvw, kvt, ew):
    eye = (
        lax.broadcasted_iota(jnp.int32, (128, 128), 0)
        == lax.broadcasted_iota(jnp.int32, (128, 128), 1)
    ).astype(BF16)
    for rel in range(2):
        for r in range(count):
            place = tile_place(sc, r, rel, count)

            @pl.when(base + place >= sc[2])
            def _(rel=rel, r=r, place=place):
                block = kv_refs[rel][r * TILE : (r + 1) * TILE, :]
                kvw[place] = block
                rows = s_refs[rel][:, r * TILE : (r + 1) * TILE]
                for h in range(3):
                    kvt[place, h * 128 : (h + 1) * 128, :] = dot_nt(
                        eye, block[:, h * 128 : (h + 1) * 128]
                    ).astype(BF16)
                    pick = (lax.broadcasted_iota(jnp.int32, (8, 128), 0) == h).astype(BF16)
                    ew[place * 3 + h] = jnp.exp(dot_tn(rows, pick))


def twice(x):
    return jnp.concatenate([x, x], axis=1)


def key_iota():
    return lax.broadcasted_iota(jnp.int32, (TILE, TILE), 0)


def query_iota():
    return lax.broadcasted_iota(jnp.int32, (1, TILE), 1)


def column(r):
    return pl.ds(pl.multiple_of(r * TILE, TILE), TILE)


def padded_queries(q_ref, r):
    zero = jnp.zeros((64, TILE), BF16)
    q_all = q_ref[:, column(r)] * BF16(ROOT)
    return [
        jnp.concatenate([q_all[64 * h : 64 * h + 64, :], zero], axis=0) for h in range(3)
    ]


def chunk_masks(ds_row, place, j, edge):
    k_io = key_iota()
    mask = k_io >= ds_row - j * TILE
    near = None
    if edge:
        ahead = query_iota() + (place - j) * TILE
        mask = mask & (k_io <= ahead)
        near = k_io > ahead - WINDOW
    return mask, near


def fwd_chunk(state, j, slot, edge, place, ds_row, q_pad, p_rows, kvw, kvt, ew, acc):
    mask, near = chunk_masks(ds_row, place, j, edge)
    zs = [dot_nn(kvw[slot, :, h * 128 : (h + 1) * 128], q_pad[h]) for h in range(3)]
    out, probs, alphas = [], [], []
    for h in range(3):
        m_old, l_old = state[2 * h], state[2 * h + 1]
        z = jnp.where(mask, zs[h], NEGATIVE)
        m_new = jnp.maximum(m_old, jnp.max(z, axis=0, keepdims=True))
        e = twice(ew[slot * 3 + h])
        sig = e / (e + p_rows[h])
        if edge:
            sig = jnp.where(near, 1.0, sig)
        prob = jnp.exp(z - m_new) * sig
        alphas.append(jnp.exp(m_old - m_new))
        out += [m_new, l_old * alphas[h] + jnp.sum(prob, axis=0, keepdims=True)]
        probs.append(prob.astype(BF16))
    for h in range(3):
        acc[h] = acc[h] * alphas[h] + dot_nn(kvt[slot, h * 128 + 64 : (h + 1) * 128, :], probs[h])
    return tuple(out)


def fwd_own_kernel(count, sc, q_ref, kv0, kv1, s0, s1, s2, s3, ds_ref, acc_ref, ml_ref, p_ref,
                   kvw, kvt, ew, er, acc):
    base = 2 * count
    fill_window(sc, count, base, (kv0, kv1), (s0, s1), kvw, kvt, ew)
    for part, refs in enumerate(((s2, s3), (s0, s1))):
        for rel in range(2):
            for r in range(count):
                place = part * base + tile_place(sc, r, rel, count)
                er[place] = jnp.exp(refs[rel][:, r * TILE : (r + 1) * TILE].astype(F32))

    def one_tile(r, unused):
        place = base + tile_place(sc, r, 0, count)
        low = sc[3 + r]
        ds_row = ds_ref[r][0:1, :]
        tile_start = place * TILE
        q_pad = padded_queries(q_ref, r)
        k_io = key_iota()
        inside = (k_io >= ds_row - tile_start) & (k_io <= query_iota())
        ds_first = jnp.min(ds_row, axis=1, keepdims=True)
        lane = lax.broadcasted_iota(jnp.int32, (8, TILE), 1)

        def carry_step(j, sums):
            return sums + jnp.where(lane >= ds_first - j * TILE, er[j], 0.0)

        carried = lax.fori_loop(low, place, carry_step, jnp.zeros((8, TILE), F32))
        carried = jnp.sum(carried, axis=1, keepdims=True)
        starts_before = ds_row < tile_start
        p_rows = []
        for h in range(3):
            local = jnp.sum(
                jnp.where(inside, twice(ew[(place - base) * 3 + h]), 0.0), axis=0, keepdims=True
            )
            prefix = local + jnp.where(starts_before, carried[h : h + 1, :], 0.0)
            p_rows.append(jnp.maximum(prefix * (1.0 / KEEP), TINY))
        acc[...] = jnp.zeros_like(acc)

        def chunk(j, state, edge):
            return fwd_chunk(
                state, j, j - base, edge, place, ds_row, q_pad, p_rows, kvw, kvt, ew, acc
            )

        state = (jnp.full((1, TILE), NEGATIVE, F32), jnp.zeros((1, TILE), F32)) * 3
        low = jnp.maximum(low, base)
        edge_low = jnp.maximum(place - 1, low)
        state = lax.fori_loop(low, edge_low, lambda j, s: chunk(j, s, False), state)
        state = lax.fori_loop(edge_low, place + 1, lambda j, s: chunk(j, s, True), state)
        zero = jnp.zeros((2, TILE), F32)
        acc_ref[r] = jnp.concatenate([acc[0], acc[1], acc[2]], axis=0)
        ml_ref[r] = jnp.concatenate(list(state[0::2]) + list(state[1::2]) + [zero], axis=0)
        p_ref[r] = jnp.concatenate(p_rows + p_rows + [zero], axis=0)
        return unused

    lax.fori_loop(0, count, one_tile, 0)


def fwd_prev_kernel(count, sc, q_ref, kv0, kv1, s0, s1, ds_ref, acc_ref, ml_ref, p_ref,
                    o_ref, of_ref, lse_ref, kvw, kvt, ew, acc):
    base = 2 * count
    fill_window(sc, count, 0, (kv0, kv1), (s0, s1), kvw, kvt, ew)

    def one_tile(r, unused):
        place = base + tile_place(sc, r, 0, count)
        low = sc[3 + r]
        ds_row = ds_ref[r][0:1, :]
        q_pad = padded_queries(q_ref, r)
        ml = ml_ref[r]
        p_all = p_ref[r]
        p_rows = [p_all[h : h + 1, :] for h in range(3)]
        before = acc_ref[r]
        for h in range(3):
            acc[h] = before[64 * h : 64 * h + 64, :]

        def chunk(j, state, edge):
            return fwd_chunk(state, j, j, edge, place, ds_row, q_pad, p_rows, kvw, kvt, ew, acc)

        state = ()
        for h in range(3):
            state += (ml[h : h + 1, :], ml[3 + h : 4 + h, :])
        edge_low = jnp.maximum(place - 1, low)
        state = lax.fori_loop(
            low, jnp.minimum(edge_low, base), lambda j, s: chunk(j, s, False), state
        )
        state = lax.fori_loop(edge_low, base, lambda j, s: chunk(j, s, True), state)
        stacked = jnp.concatenate([acc[h] / state[2 * h + 1] for h in range(3)], axis=0)
        of_ref[r] = stacked
        o_ref[sc[1] ^ r] = stacked.astype(BF16)
        lse = [state[2 * h] + jnp.log(state[2 * h + 1]) for h in range(3)]
        lse_ref[r] = jnp.concatenate(lse + lse + [jnp.zeros((2, TILE), F32)], axis=0)
        return unused

    lax.fori_loop(0, count, one_tile, 0)


def bwd_chunk(state, j, slot, edge, place, ds_row, q_pad, do_pad, both, lse, p_rows, delta,
              kvw, kvt, ew, dkv, dsl, dqt):
    mask, near = chunk_masks(ds_row, place, j, edge)
    kv = [kvw[slot, :, h * 128 : (h + 1) * 128] for h in range(3)]
    zs = [dot_nn(kv[h], q_pad[h]) for h in range(3)]
    dps = [dot_nn(kv[h], do_pad[h]) for h in range(3)]
    out, lows, pairs, fars = [], [], [], []
    for h in range(3):
        e = twice(ew[slot * 3 + h])
        r = 1.0 / (e + p_rows[h])
        sig = e * r
        if edge:
            sig = jnp.where(near, 1.0, sig)
        prob = jnp.exp(jnp.where(mask, zs[h] - lse[h], NEGATIVE)) * sig
        dz = prob * (dps[h] - delta[h])
        far = dz * (p_rows[h] * r)
        if edge:
            far = jnp.where(near, 0.0, far)
        out.append(state[h] - jnp.sum(far, axis=0, keepdims=True))
        fars.append(far[:, :128] + far[:, 128:])
        lows.append(dz.astype(BF16))
        pairs.append(jnp.concatenate([lows[h], prob.astype(BF16)], axis=1))
    for h in range(3):
        dqt[h] += dot_nn(kvt[slot, h * 128 : h * 128 + 64, :], lows[h])
    grads = [dot_nt(pairs[h], both[h]) for h in range(3)]
    dkv[slot] += jnp.concatenate(grads, axis=1)
    for h in range(3):
        dsl[slot * 3 + h] += fars[h]
    return tuple(out)


def bwd_rows(r, sc, q_ref, do_ref, of_ref, lse_ref, p_ref):
    q_pad = padded_queries(q_ref, r)
    do_all = do_ref[sc[1] ^ r]
    lse_all, p_all, of = lse_ref[r], p_ref[r], of_ref[r]
    zero = jnp.zeros((64, TILE), BF16)
    do_pad, both, lse, p_rows, delta = [], [], [], [], []
    for h in range(3):
        dh = do_all[64 * h : 64 * h + 64, :]
        do_pad.append(jnp.concatenate([zero, dh], axis=0))
        both.append(jnp.concatenate([q_pad[h], do_pad[h]], axis=1))
        lse.append(lse_all[h : h + 1, :])
        p_rows.append(p_all[h : h + 1, :])
        delta.append(
            jnp.sum(dh.astype(F32) * of[64 * h : 64 * h + 64, :], axis=0, keepdims=True)
        )
    return q_pad, do_pad, both, lse, p_rows, delta


def write_keys(sc, count, dkv, dsl, outs):
    for rel in range(2):
        big, small = outs[rel]
        for r in range(count):
            place = tile_place(sc, r, rel, count)
            big[r * TILE : (r + 1) * TILE, :] = dkv[place].astype(big.dtype)
            rows = []
            for h in range(3):
                summed = jnp.sum(dsl[place * 3 + h], axis=1, keepdims=True)
                rows.append(jnp.transpose(jnp.broadcast_to(summed, (TILE, 128)))[0:1, :])
            rows = jnp.concatenate(rows + [jnp.zeros((5, TILE), F32)], axis=0)
            small[:, r * TILE : (r + 1) * TILE] = rows.astype(small.dtype)


def bwd_prev_kernel(count, sc, q_ref, do_ref, of_ref, lse_ref, p_ref, kv0, kv1, s0, s1, ds_ref,
                    dq_ref, tau_ref, big0, big1, small0, small1, kvw, kvt, ew, dkv, dsl, dqt):
    base = 2 * count
    fill_window(sc, count, 0, (kv0, kv1), (s0, s1), kvw, kvt, ew)
    dkv[...] = jnp.zeros_like(dkv)
    dsl[...] = jnp.zeros_like(dsl)

    def one_tile(r, unused):
        place = base + tile_place(sc, r, 0, count)
        low = sc[3 + r]
        ds_row = ds_ref[r][0:1, :]
        dqt[...] = jnp.zeros_like(dqt)

        @pl.when(low >= base)
        def _():
            tau_ref[r] = jnp.zeros((8, TILE), F32)

        @pl.when(low < base)
        def _():
            rows = bwd_rows(r, sc, q_ref, do_ref, of_ref, lse_ref, p_ref)

            def chunk(j, state, edge):
                return bwd_chunk(
                    state, j, j, edge, place, ds_row, *rows, kvw, kvt, ew, dkv, dsl, dqt
                )

            state = (jnp.zeros((1, TILE), F32),) * 3
            edge_low = jnp.maximum(place - 1, low)
            state = lax.fori_loop(
                low, jnp.minimum(edge_low, base), lambda j, s: chunk(j, s, False), state
            )
            state = lax.fori_loop(edge_low, base, lambda j, s: chunk(j, s, True), state)
            tau_ref[r] = jnp.concatenate(list(state) + [jnp.zeros((5, TILE), F32)], axis=0)

        dq_ref[r] = jnp.concatenate([dqt[0], dqt[1], dqt[2]], axis=0)
        return unused

    lax.fori_loop(0, count, one_tile, 0)
    write_keys(sc, count, dkv, dsl, ((big0, small0), (big1, small1)))


def bwd_own_kernel(count, sc, q_ref, do_ref, of_ref, lse_ref, p_ref, kv0, kv1, s0, s1, ds_ref,
                   dqp_ref, tau_ref, dq_ref, big0, big1, small0, small1, carry_ref,
                   kvw, kvt, ew, dkv, dsl, dqt):
    base = 2 * count
    fill_window(sc, count, base, (kv0, kv1), (s0, s1), kvw, kvt, ew)
    dkv[...] = jnp.zeros_like(dkv)
    dsl[...] = jnp.zeros_like(dsl)
    carry_ref[...] = jnp.zeros_like(carry_ref)

    def one_tile(r, unused):
        place = base + tile_place(sc, r, 0, count)
        low = sc[3 + r]
        ds_row = ds_ref[r][0:1, :]
        tile_start = place * TILE
        rows = bwd_rows(r, sc, q_ref, do_ref, of_ref, lse_ref, p_ref)
        p_rows = rows[4]
        before = dqp_ref[r]
        for h in range(3):
            dqt[h] = before[64 * h : 64 * h + 64, :]

        def chunk(j, state, edge):
            return bwd_chunk(
                state, j, j - base, edge, place, ds_row, *rows, kvw, kvt, ew, dkv, dsl, dqt
            )

        tau = tau_ref[r]
        state = tuple(tau[h : h + 1, :] for h in range(3))
        low = jnp.maximum(low, base)
        edge_low = jnp.maximum(place - 1, low)
        state = lax.fori_loop(low, edge_low, lambda j, s: chunk(j, s, False), state)
        state = lax.fori_loop(edge_low, place + 1, lambda j, s: chunk(j, s, True), state)
        dq_ref[:, column(r)] = (
            jnp.concatenate([dqt[0], dqt[1], dqt[2]], axis=0) * ROOT
        ).astype(BF16)

        k_io = key_iota()
        inside = (k_io >= ds_row - tile_start) & (k_io <= query_iota())
        ds_first = jnp.min(ds_row, axis=1, keepdims=True)
        slot = place - base
        w_lane = []
        for h in range(3):
            w = state[h] / (p_rows[h] * float(KEEP))
            earlier = jnp.where(ds_row < tile_start, w, 0.0)
            w_lane.append(earlier[:, :128] + earlier[:, 128:])
            here = jnp.where(inside, w, 0.0)
            dsl[slot * 3 + h] += ew[slot * 3 + h] * (here[:, :128] + here[:, 128:])
            further = jnp.where(ds_row < base * TILE, w, 0.0)
            carry_ref[h : h + 1, :] += further[:, :128] + further[:, 128:]

        def later(j, unused):
            keep = lax.broadcasted_iota(jnp.int32, (TILE, 128), 0) >= ds_first - j * TILE
            for h in range(3):
                dsl[(j - base) * 3 + h] += jnp.where(keep, ew[(j - base) * 3 + h] * w_lane[h], 0.0)
            return unused

        lax.fori_loop(low, place, later, 0)
        return unused

    lax.fori_loop(0, count, one_tile, 0)
    write_keys(sc, count, dkv, dsl, ((big0, small0), (big1, small1)))


VM = pl.BlockSpec(memory_space=pltpu.VMEM)
SM = pl.BlockSpec(memory_space=pltpu.SMEM)
MIB = 1024 * 1024


def window_scratch(count):
    return [
        pltpu.VMEM((2 * count, TILE, 384), BF16),
        pltpu.VMEM((2 * count, 384, TILE), BF16),
        pltpu.VMEM((2 * count * 3, TILE, 128), F32),
    ]


def grad_scratch(count):
    return [
        pltpu.VMEM((2 * count, TILE, 384), F32),
        pltpu.VMEM((2 * count * 3, TILE, 128), F32),
        pltpu.VMEM((3, 64, TILE), F32),
    ]


def call(body, count, name, args, outs, scratch, work, room):
    return pl.pallas_call(
        functools.partial(body, count),
        out_shape=tuple(jax.ShapeDtypeStruct(s, t) for s, t in outs),
        in_specs=[SM] + [VM] * (len(args) - 1),
        out_specs=(VM,) * len(outs),
        scratch_shapes=scratch,
        compiler_params=pltpu.CompilerParams(vmem_limit_bytes=room * MIB),
        cost_estimate=pl.CostEstimate(flops=work, bytes_accessed=work // 400, transcendentals=0),
        name=name,
    )(*args)


def forward_own(count, scal, q, kvs, ss, ds):
    outs = (((count, 192, TILE), F32), ((count, 8, TILE), F32), ((count, 8, TILE), F32))
    scratch = window_scratch(count) + [
        pltpu.VMEM((4 * count, 8, TILE), F32),
        pltpu.VMEM((3, 64, TILE), F32),
    ]
    return call(fwd_own_kernel, count, "forward_own", (scal, q, *kvs, *ss, ds), outs, scratch, 20 * 10**9, 24)


def forward_prev(count, scal, q, kvs, ss, ds, acc, ml, p):
    outs = (((count, 192, TILE), BF16), ((count, 192, TILE), F32), ((count, 8, TILE), F32))
    scratch = window_scratch(count) + [pltpu.VMEM((3, 64, TILE), F32)]
    args = (scal, q, *kvs, *ss, ds, acc, ml, p)
    return call(fwd_prev_kernel, count, "forward_prev", args, outs, scratch, 8 * 10**9, 24)


def key_outs(count):
    rows = count * TILE
    return (((rows, 384), F32), ((rows, 384), BF16), ((8, rows), F32), ((8, rows), BF16))


def backward_prev(count, scal, q, do, of, lse, p, kvs, ss, ds):
    outs = (((count, 192, TILE), F32), ((count, 8, TILE), F32)) + key_outs(count)
    scratch = window_scratch(count) + grad_scratch(count)
    args = (scal, q, do, of, lse, p, *kvs, *ss, ds)
    return call(bwd_prev_kernel, count, "backward_prev", args, outs, scratch, 12 * 10**9, 32)


def backward_own(count, scal, q, do, of, lse, p, kvs, ss, ds, dq, tau):
    outs = (((192, count * TILE), BF16),) + key_outs(count) + (((8, 128), F32),)
    scratch = window_scratch(count) + grad_scratch(count)
    args = (scal, q, do, of, lse, p, *kvs, *ss, ds, dq, tau)
    return call(bwd_own_kernel, count, "backward_own", args, outs, scratch, 24 * 10**9, 32)


def hidden_kernel(n0, n1, dy0, dy1, bias, down, up, y0, y1, dt0, dt1, g_ref, gb_ref, n_all, dy_all, y_acc, d_acc):
    step = pl.program_id(0)
    tok = n0.shape[0]

    @pl.when(step == 0)
    def _():
        n_all[:tok, :] = n0[...]
        n_all[tok:, :] = n1[...]
        dy_all[:tok, :] = dy0[...]
        dy_all[tok:, :] = dy1[...]
        y_acc[...] = jnp.zeros_like(y_acc)
        d_acc[...] = jnp.zeros_like(d_acc)

    w_up = up[...].reshape(D, -1)
    w_down = down[...].reshape(-1, D)
    n = n_all[...]
    dy = dy_all[...]
    pre = dot_nn(n, w_up) + bias[0:1, :]
    d_hidden = dot_nt(dy, w_down)
    c0 = math.sqrt(2.0 / math.pi)
    squared = pre * pre
    th = jnp.tanh(c0 * pre * (1.0 + 0.044715 * squared))
    half = 0.5 * (1.0 + th)
    hidden = (pre * half).astype(BF16)
    slope = half + 0.5 * pre * (1.0 - th * th) * c0 * (1.0 + 3 * 0.044715 * squared)
    d_up = (d_hidden * slope).astype(BF16)
    y_acc[...] += dot_nn(hidden, w_down)
    d_acc[...] += dot_nt(d_up, w_up)
    gb_ref[...] = jnp.broadcast_to(jnp.sum(d_up.astype(F32), axis=0, keepdims=True), gb_ref.shape)
    g_down = dot_tn(hidden, dy).astype(BF16).reshape(down.shape)
    g_up = dot_tn(n, d_up).astype(BF16).reshape(up.shape)
    groups, height = down.shape[0], down.shape[1]
    g_ref[pl.ds(step * groups, groups), 0:height, :] = g_down
    rows, cols = up.shape[1], up.shape[2]
    per = D // cols
    top = pl.multiple_of(height + (step // per) * rows, 16)
    left = pl.multiple_of(lax.rem(step, per) * cols, 128)
    g_ref[:, pl.ds(top, rows), pl.ds(left, cols)] = g_up

    @pl.when(step == pl.num_programs(0) - 1)
    def _():
        y0[...] = y_acc[:tok, :]
        y1[...] = y_acc[tok:, :]
        dt0[...] = d_acc[:tok, :]
        dt1[...] = d_acc[tok:, :].astype(BF16)


def hidden_passes(n0, n1, dy0, dy1, bias, packed):
    tok = n0.shape[0]
    parts, height, rows, cols = packed.shape[0], 96, 48, 384
    steps = 4
    whole = pl.BlockSpec((tok, D), lambda i: (0, 0))
    outs = (
        jax.ShapeDtypeStruct((tok, D), F32),
        jax.ShapeDtypeStruct((tok, D), F32),
        jax.ShapeDtypeStruct((tok, D), F32),
        jax.ShapeDtypeStruct((tok, D), BF16),
        jax.ShapeDtypeStruct((parts, 192, D), BF16),
        jax.ShapeDtypeStruct((8, FF // 2), F32),
    )
    return pl.pallas_call(
        hidden_kernel,
        grid=(steps,),
        out_shape=outs,
        in_specs=[
            whole,
            whole,
            whole,
            whole,
            pl.BlockSpec((8, cols), lambda i: (0, i)),
            pl.BlockSpec((parts // steps, height, D), lambda i: (i, 0, 0)),
            pl.BlockSpec((parts, rows, cols), lambda i: (0, 2 + i // 2, lax.rem(i, 2))),
        ],
        out_specs=(
            whole,
            whole,
            whole,
            whole,
            pl.BlockSpec((parts, 192, D), lambda i: (0, 0, 0)),
            pl.BlockSpec((8, cols), lambda i: (0, i)),
        ),
        scratch_shapes=[
            pltpu.VMEM((2 * tok, D), BF16),
            pltpu.VMEM((2 * tok, D), BF16),
            pltpu.VMEM((2 * tok, D), F32),
            pltpu.VMEM((2 * tok, D), F32),
        ],
        compiler_params=pltpu.CompilerParams(vmem_limit_bytes=56 * MIB),
        cost_estimate=pl.CostEstimate(flops=7 * 10**9, bytes_accessed=10**7, transcendentals=0),
        name="hidden_passes",
    )(n0, n1, dy0, dy1, bias, packed, packed)


def project_kernel(count, sc, own, sib, back, dq, s0, s1, s2, scores, cond, carry, x, w,
                   cat_ref, dn0_ref, dn_ref, sums_ref, cols_ref):
    place = (
        lax.broadcasted_iota(jnp.int32, (8, 64), 1)
        == lax.broadcasted_iota(jnp.int32, (8, 64), 0) + 3 * sc[1]
    ).astype(BF16)
    real = lax.broadcasted_iota(jnp.int32, (8, TILE), 0) < 3
    sums_ref[...] = jnp.zeros_like(sums_ref)
    cols_ref[...] = jnp.zeros_like(cols_ref)
    weights = w[...]
    for r in range(count):
        at = slice(r * TILE, (r + 1) * TILE)
        d_kv = own[at, :] + sib[at, :].astype(F32) + back[at, :].astype(F32)
        d_q = jnp.transpose(dq[:, at].astype(F32))
        after = jnp.exp(scores[:, at].astype(F32)) * jnp.sum(carry[...], axis=1, keepdims=True)
        d_s = s0[:, at] + s1[:, at].astype(F32) + s2[:, at].astype(F32)
        d_s = d_s + jnp.where(cond[0:1, at] > 0, after, 0.0)
        d_s = jnp.transpose(jnp.where(real, d_s, 0.0)).astype(BF16)
        d_s = dot_nn(d_s, place)
        cat = jnp.concatenate([d_kv, d_q, d_s], axis=1).astype(BF16)
        cat_ref[at, :] = cat
        d_n = dot_nt(cat, weights)
        if r == 0:
            dn0_ref[...] = d_n
        else:
            dn_ref[(r - 1) * TILE : r * TILE, :] = d_n.astype(BF16)
        unit, _ = normalize(x[at, :].astype(F32))
        sums_ref[0:1, :] += jnp.sum(d_n * unit, axis=0, keepdims=True)
        sums_ref[1:2, :] += jnp.sum(d_n, axis=0, keepdims=True)
        cols_ref[0:1, :] += jnp.sum(cat.astype(F32), axis=0, keepdims=True)


def project_back(count, *args):
    rows = count * TILE
    outs = (
        ((rows, 640), BF16),
        ((TILE, D), F32),
        ((rows - TILE, D), BF16),
        ((8, D), F32),
        ((8, 640), F32),
    )
    return call(project_kernel, count, "project_back", args, outs, [], 10**9, 56)


def other_core(x):
    return lax.ppermute(x, "core", [(0, 1), (1, 0)])


def next_chip(x, step):
    n = lax.axis_size("pair")
    return lax.ppermute(x, "pair", [(i, i + step) for i in range(n) if 0 <= i + step < n])


def spread(x, axes):
    n = lax.axis_size(axes)
    return lax.all_to_all(jnp.broadcast_to(x[None], (n,) + x.shape), axes, 0, 0)


def both_cores(mine, theirs, core, axis):
    return jnp.where(
        core == 0, jnp.stack([mine, theirs], axis), jnp.stack([theirs, mine], axis)
    )


def normalize(rows):
    centred = rows - jnp.mean(rows, axis=-1, keepdims=True)
    scale = lax.rsqrt(jnp.mean(centred * centred, axis=-1, keepdims=True) + EPS)
    return centred * scale, scale


def norm_pull(grad, unit, scale, gain):
    inner = grad * gain
    return scale * (
        inner
        - jnp.mean(inner, axis=-1, keepdims=True)
        - unit * jnp.mean(inner * unit, axis=-1, keepdims=True)
    )


def across(x, r):
    return lax.ppermute(x, "head", [(i, i ^ r) for i in range(lax.axis_size("head"))])


def shards(tokens, segment_ids, gains, biases, w_qkv, w_score, w_out, w_up, w_down, cotangent):
    groups = lax.axis_size("head")
    pairs = lax.axis_size("pair")
    devices = groups * pairs * 2
    same = groups * pairs
    h = lax.axis_index("head")
    p = lax.axis_index("pair")
    c = lax.axis_index("core")
    tok = tokens.shape[0]
    block = groups * tok
    count = groups
    super_rows = 2 * block
    total = super_rows * pairs
    rows_l = D // devices
    down_l = FF // devices
    swaps = (h & 1) == 1

    x_other = other_core(tokens)
    dy_other = other_core(cotangent)
    x_mine = jnp.where(swaps, x_other, tokens)
    x_parts = [x_mine] + [across(x_mine, r) for r in range(1, groups)]

    part = w_qkv.astype(BF16).reshape(rows_l, 3, groups, 3, HDIM)
    part_q = part[:, 0].reshape(rows_l, groups, 192)
    part_kv = part[:, 1:].transpose(0, 2, 3, 1, 4).reshape(rows_l, groups, 384)
    id_lanes = -(-tok // rows_l)
    own_ids = jnp.pad(segment_ids.astype(BF16), (0, id_lanes * rows_l - tok))
    small = jnp.concatenate(
        [
            w_score.astype(BF16).reshape(rows_l, HEADS),
            gains.astype(BF16).reshape(rows_l, 2),
            biases.astype(BF16).reshape(rows_l, 10),
            own_ids.reshape(rows_l, id_lanes),
        ],
        axis=1,
    )
    small = jnp.broadcast_to(small[:, None], (rows_l, groups, small.shape[1]))
    part = jnp.concatenate([part_kv, part_q, small], axis=-1).transpose(1, 0, 2)
    filled = part.shape[2]
    width = -(-filled // 128) * 128
    part = jnp.pad(part, ((0, 0), (0, 0), (0, width - filled)))
    part = jnp.broadcast_to(part[:, None], (groups, pairs, rows_l, width))
    w_same = lax.all_to_all(part.reshape(same, rows_l, width), SAME, 0, 0)
    up_rows = w_up.astype(BF16).reshape(rows_l, same, 2, down_l)
    up_mine = jnp.where(c == 0, up_rows[:, :, 0], up_rows[:, :, 1]).reshape(rows_l, FF // 2)
    up_send = jnp.where(c == 0, up_rows[:, :, 1], up_rows[:, :, 0]).reshape(rows_l, FF // 2)
    up_both = both_cores(up_mine, other_core(up_send), c, 0).reshape(2 * rows_l, FF // 2)
    down_mine = w_down.astype(BF16).reshape(down_l, D)
    out_mine = w_out.astype(BF16).reshape(rows_l, D)
    a, b, e = down_l, down_l + 2 * rows_l, down_l + 4 * rows_l
    pack = jnp.concatenate([down_mine, up_both[:, :D], up_both[:, D:]], axis=0)
    packed = lax.all_gather(pack, "pair", axis=0, tiled=False)
    packed, out_mine, w_same = lax.optimization_barrier((packed, out_mine, w_same))
    packed = lax.all_gather(packed, "head", axis=0, tiled=False).reshape((same,) + pack.shape)
    out_same = spread(out_mine, SAME)
    tall = down_l
    if tall != 96:
        packed = jnp.concatenate(
            [
                packed[:, :a].reshape(16, 96, D),
                packed[:, a:b].reshape(16, 48, D),
                packed[:, b:e].reshape(16, 48, D),
            ],
            axis=1,
        )

    w_both = both_cores(w_same, other_core(w_same), c, 1).reshape(D, width)
    w_kv, w_q = w_both[:, :384], w_both[:, 384:576]
    gain_rows = w_both[:, 588:590].reshape(2, D).astype(F32)
    bias_rows = w_both[:, 590:600].reshape(10, D).astype(F32)
    ids_all = w_both[:, 600 : 600 + id_lanes].reshape(devices, rows_l * id_lanes)[:, :tok]
    ids_all = ids_all.astype(jnp.int32).reshape(groups, pairs, 2, tok)
    ids_all = ids_all.transpose(1, 2, 0, 3).reshape(total)

    x_low = jnp.concatenate(x_parts, axis=0)
    x_rows = x_low.astype(F32)
    unit_one, scale_one = normalize(x_rows)
    normed = (unit_one * gain_rows[0] + bias_rows[0]).astype(BF16)
    w_s = lax.dynamic_slice_in_dim(w_both[:, 576:588], 3 * h, 3, axis=1)
    w_s = jnp.pad(w_s, ((0, 0), (0, 5)))
    scores = lax.dot_general(
        w_s, normed, (((0,), (1,)), ((), ())), preferred_element_type=F32
    ).astype(BF16)
    s_sib = other_core(scores)
    s_prev = next_chip(jnp.stack([scores, s_sib]), 1)
    bias_v = lax.dynamic_slice_in_dim(bias_rows[2:3], 192 * h, 192, axis=1).reshape(1, 3, 1, HDIM)
    bias_kv = jnp.concatenate([jnp.zeros_like(bias_v), bias_v], axis=2).reshape(1, 384)
    kv = (dot_nn(normed, w_kv) + bias_kv).astype(BF16)
    kv, s_prev, out_same = lax.optimization_barrier((kv, s_prev, out_same))
    m_out = both_cores(out_same, other_core(out_same), c, 1).reshape(D, D)
    kv_prev = next_chip(kv, 1)
    kv_sib = other_core(kv)
    bias_q = lax.dynamic_slice_in_dim(bias_rows[1:2], 192 * h, 192, axis=1).reshape(192, 1)
    q = lax.dot_general(w_q, normed, (((0,), (1,)), ((), ())), preferred_element_type=F32)
    q = (q + bias_q).astype(BF16)

    padded = jnp.concatenate([jnp.full((super_rows,), -1, jnp.int32), ids_all])
    ids_win = lax.dynamic_slice_in_dim(padded, p * super_rows, 2 * super_rows)
    k_of = h ^ jnp.arange(count)
    tile_of = k_of + count * ((c + k_of) & 1)
    ids_super = ids_win[super_rows:].reshape(1, 2 * count, TILE)
    picked = tile_of[:, None, None] == jnp.arange(2 * count)[None, :, None]
    ids_q = jnp.sum(jnp.where(picked, ids_super, 0), axis=1)
    starts = jnp.sum((ids_win[None, :, None] < ids_q[:, None, :]).astype(jnp.int32), axis=1)
    lows = jnp.min(starts, axis=1) // TILE
    scal = jnp.concatenate([jnp.stack([c, h]), jnp.min(lows)[None], lows]).astype(jnp.int32)
    ds = jnp.broadcast_to(starts[:, None, :], (count, 8, TILE))

    own_kvs, own_ss = (kv, kv_sib), (scores, s_sib)
    prev_ss = (s_prev[0], s_prev[1])
    acc, ml, pr = forward_own(count, scal, q, own_kvs, own_ss + prev_ss, ds)
    kv_prev, acc = lax.optimization_barrier((kv_prev, acc))
    prev_kvs = (kv_prev, other_core(kv_prev))
    o, of, lse = forward_prev(count, scal, q, prev_kvs, prev_ss, ds, acc, ml, pr)

    attn = lax.all_to_all(o, "head", 0, 0).reshape(D, tok)
    middle = x_mine.astype(F32) + dot_tn(attn, m_out) + bias_rows[3]
    unit_two, scale_two = normalize(middle)
    n_two = (unit_two * gain_rows[1] + bias_rows[4]).astype(BF16)
    n_sib = other_core(n_two)
    dy_mine = jnp.where(swaps, dy_other, cotangent)
    dy_sib = jnp.where(swaps, cotangent, dy_other)
    stripes = bias_rows[5:9].reshape(same, 2, down_l)
    up_half = jnp.where(c == 0, stripes[:, 0], stripes[:, 1]).reshape(1, FF // 2)
    up_half = jnp.broadcast_to(up_half, (8, FF // 2))
    y0, y1, d_two_0, d_two_1, g_pack, g_up_bias = hidden_passes(
        n_two, n_sib, dy_mine, dy_sib, up_half, packed
    )
    d_two = d_two_0 + other_core(d_two_1).astype(F32)
    y = y0 + other_core(y1)
    result_mine = (middle + y + bias_rows[9]).astype(BF16)
    result = jnp.where(swaps, other_core(result_mine), result_mine)

    g_up_bias = g_up_bias[0]
    g_gain_two = jnp.sum(d_two * unit_two, axis=0)
    g_shift_two = jnp.sum(d_two, axis=0)
    dy_f = dy_mine.astype(F32)
    g_down_bias = jnp.sum(dy_f, axis=0)

    d_middle = dy_f + norm_pull(d_two, unit_two, scale_two, gain_rows[1])
    d_branch = d_middle.astype(BF16)
    g_out_bias = jnp.sum(d_branch.astype(F32), axis=0)
    d_sent = dot_nt(m_out, d_branch).astype(BF16)
    d_heads = lax.all_to_all(d_sent.reshape(groups, 192, tok), "head", 0, 0)
    g_out = dot_nn(attn, d_branch)

    if tall != 96:
        g_pack = jnp.concatenate(
            [
                g_pack[:, :96].reshape(same, a, D),
                g_pack[:, 96:144].reshape(same, b - a, D),
                g_pack[:, 144:].reshape(same, e - b, D),
            ],
            axis=1,
        )
    g_out_rows = g_out.reshape(same, 2, rows_l, D)
    g_out_keep = jnp.where(c == 0, g_out_rows[:, 0], g_out_rows[:, 1])
    g_out_send = jnp.where(c == 0, g_out_rows[:, 1], g_out_rows[:, 0]).astype(BF16)
    g_out_same = (g_out_keep + other_core(g_out_send).astype(F32)).astype(BF16)
    g_pack = jnp.concatenate([g_pack, g_out_same], axis=1)
    g_half = lax.psum_scatter(
        g_pack.reshape(groups, pairs, e + rows_l, D), "head", scatter_dimension=0, tiled=False
    )

    rows = (q, d_heads, of, lse, pr)
    dq_part, tau, prev, to_cross, s_prev_part, s_to_cross = backward_prev(
        count, scal, *rows, prev_kvs, prev_ss, ds
    )
    to_prev = (prev + other_core(to_cross).astype(F32)).astype(BF16)
    to_prev, tau = lax.optimization_barrier((to_prev, tau))
    back = next_chip(to_prev, -1)
    s_back = next_chip((s_prev_part + other_core(s_to_cross).astype(F32)).astype(BF16), -1)
    dq, own, to_sib, s_own, s_to_sib, carry = backward_own(
        count, scal, *rows, own_kvs, own_ss, ds, dq_part, tau
    )
    carry = next_chip(carry + other_core(carry), -1)
    back, s_back, to_sib, s_to_sib = lax.optimization_barrier((back, s_back, to_sib, s_to_sib))
    sib_kv, sib_s = other_core(to_sib), other_core(s_to_sib)

    continued = (ids_q == ids_win[-1]).astype(jnp.int32).reshape(1, block)
    continued = jnp.broadcast_to(continued, (8, block))
    cat, d_norm_sum, d_norm_low, sums, cols = project_back(
        count, scal, own, sib_kv, back, dq, s_own, sib_s, s_back, scores, continued, carry, x_low, w_both[:, :640]
    )
    cat, d_norm_low = lax.optimization_barrier((cat, d_norm_low))
    for r in range(1, groups):
        d_norm_sum = d_norm_sum + across(d_norm_low[(r - 1) * tok : r * tok], r).astype(F32)

    mine = jnp.arange(D) // 192 == h
    g_q_bias = jnp.where(mine, jnp.tile(cols[0, 384:576], groups), 0.0)
    g_v_bias = cols[0, :384].reshape(3, 2, HDIM)[:, 1].reshape(192)
    g_v_bias = jnp.where(mine, jnp.tile(g_v_bias, groups), 0.0)
    halves = jnp.stack([g_up_bias.reshape(same, down_l)] * 2, axis=1)
    halves = jnp.where(jnp.arange(2)[None, :, None] == c, halves, 0.0).reshape(4, D)
    g_bias_rows = jnp.concatenate(
        [
            jnp.stack([sums[1], g_q_bias, g_v_bias, g_out_bias, g_shift_two]),
            halves,
            g_down_bias[None],
        ],
        axis=0,
    )
    small = jnp.concatenate(
        [jnp.stack([sums[0], g_gain_two]).reshape(D, 2), g_bias_rows.reshape(D, 10)], axis=1
    )
    g_all = dot_tn(normed, cat) + jnp.pad(small, ((0, 0), (588, 40)))
    g_all, g_half = lax.optimization_barrier((g_all.astype(BF16), g_half))
    came = lax.all_to_all(g_all, ALL, 0, 0, tiled=True).astype(F32)
    came = jnp.sum(came.reshape(groups, 2 * pairs, rows_l, 640), axis=1)
    grad_kv = came[:, :, :384].reshape(groups, rows_l, 3, 2, HDIM)
    grad_kv = grad_kv.transpose(1, 3, 0, 2, 4).reshape(rows_l, 2, D)
    grad_q = came[:, :, 384:576].transpose(1, 0, 2).reshape(rows_l, 1, D)
    grad_w_qkv = jnp.concatenate([grad_q, grad_kv], axis=1).reshape(-1)
    small_sum = jnp.sum(came[:, :, 576:600], axis=0)
    grad_w_score = small_sum[:, :12].reshape(-1)
    grad_gains = small_sum[:, 12:14].reshape(-1)
    grad_biases = small_sum[:, 14:24].reshape(-1)

    g_pack = lax.psum_scatter(g_half, "pair", scatter_dimension=0, tiled=False).astype(F32)
    grad_w_down = g_pack[:a].reshape(-1)
    grad_w_out = g_pack[e:].reshape(-1)
    g_up_rows = jnp.concatenate([g_pack[a:b], g_pack[b:e]], axis=1).reshape(2, rows_l, FF // 2)
    g_up_keep = jnp.where(c == 0, g_up_rows[0], g_up_rows[1])
    g_up_came = other_core(jnp.where(c == 0, g_up_rows[1], g_up_rows[0]))
    grad_w_up = both_cores(
        g_up_keep.reshape(rows_l, same, down_l), g_up_came.reshape(rows_l, same, down_l), c, 2
    ).reshape(-1)

    unit_mine, scale_mine = unit_one[:tok], scale_one[:tok]
    grad_mine = d_middle + norm_pull(d_norm_sum, unit_mine, scale_mine, gain_rows[0])
    grad_mine = grad_mine.astype(BF16)
    grad_tokens = jnp.where(swaps, other_core(grad_mine), grad_mine)
    return (
        result,
        grad_tokens,
        grad_gains,
        grad_biases,
        grad_w_qkv,
        grad_w_score,
        grad_w_out,
        grad_w_up,
        grad_w_down,
    )


def solution(mesh):
    groups = mesh.devices.shape[0]
    fine = Mesh(mesh.devices.reshape(groups, -1, 2), ALL)
    rows = P(("pair", "core", "head"), None)
    flat = P(ALL)
    in_specs = (rows, P(("pair", "core", "head"))) + (flat,) * 7 + (rows,)
    out_specs = (rows, rows) + (flat,) * 7
    return jax.shard_map(shards, mesh=fine, in_specs=in_specs, out_specs=out_specs, check_vma=False)
```

```python
import functools
import math

import jax
import jax.numpy as jnp
from jax import lax
from jax.experimental import pallas as pl
from jax.experimental.pallas import tpu as pltpu
from jax.sharding import Mesh
from jax.sharding import PartitionSpec as P

D = 768
HEADS = 12
HDIM = 64
FF = 3072
WINDOW = 64
KEEP = 64
MOST = 2000

EPS = 1e-05
NEGATIVE = -1e30
TINY = 1e-37
TILE = 256
ROOT = 1.0 / math.sqrt(HDIM)
F32 = jnp.float32
BF16 = jnp.bfloat16
ALL = ("head", "pair", "core")
SAME = ("head", "pair")


def dot_nn(a, b):
    return lax.dot_general(a, b, (((1,), (0,)), ((), ())), preferred_element_type=F32)


def dot_nt(a, b):
    return lax.dot_general(a, b, (((1,), (1,)), ((), ())), preferred_element_type=F32)


def dot_tn(a, b):
    return lax.dot_general(a, b, (((0,), (0,)), ((), ())), preferred_element_type=F32)


def tile_place(sc, r, rel, count):
    k = sc[1] ^ r
    return k + count * ((sc[0] + rel + k) & 1)


def fill_window(sc, count, base, kv_refs, s_refs, kvw, kvt, ew):
    eye = (
        lax.broadcasted_iota(jnp.int32, (128, 128), 0)
        == lax.broadcasted_iota(jnp.int32, (128, 128), 1)
    ).astype(BF16)
    for rel in range(2):
        for r in range(count):
            place = tile_place(sc, r, rel, count)

            @pl.when(base + place >= sc[2])
            def _(rel=rel, r=r, place=place):
                block = kv_refs[rel][r * TILE : (r + 1) * TILE, :]
                kvw[place] = block
                rows = s_refs[rel][:, r * TILE : (r + 1) * TILE]
                for h in range(3):
                    kvt[place, h * 128 : (h + 1) * 128, :] = dot_nt(
                        eye, block[:, h * 128 : (h + 1) * 128]
                    ).astype(BF16)
                    pick = (lax.broadcasted_iota(jnp.int32, (8, 128), 0) == h).astype(BF16)
                    ew[place * 3 + h] = jnp.exp(dot_tn(rows, pick))


def twice(x):
    return jnp.concatenate([x, x], axis=1)


def key_iota():
    return lax.broadcasted_iota(jnp.int32, (TILE, TILE), 0)


def query_iota():
    return lax.broadcasted_iota(jnp.int32, (1, TILE), 1)


def column(r):
    return pl.ds(pl.multiple_of(r * TILE, TILE), TILE)


def padded_queries(q_ref, r):
    zero = jnp.zeros((64, TILE), BF16)
    q_all = q_ref[:, column(r)] * BF16(ROOT)
    return [
        jnp.concatenate([q_all[64 * h : 64 * h + 64, :], zero], axis=0) for h in range(3)
    ]


def chunk_masks(ds_row, place, j, edge):
    k_io = key_iota()
    mask = k_io >= ds_row - j * TILE
    near = None
    if edge:
        ahead = query_iota() + (place - j) * TILE
        mask = mask & (k_io <= ahead)
        near = k_io > ahead - WINDOW
    return mask, near


def fwd_chunk(state, j, slot, edge, place, ds_row, q_pad, p_rows, kvw, kvt, ew, acc):
    mask, near = chunk_masks(ds_row, place, j, edge)
    zs = [dot_nn(kvw[slot, :, h * 128 : (h + 1) * 128], q_pad[h]) for h in range(3)]
    out, probs, alphas = [], [], []
    for h in range(3):
        m_old, l_old = state[2 * h], state[2 * h + 1]
        z = jnp.where(mask, zs[h], NEGATIVE)
        m_new = jnp.maximum(m_old, jnp.max(z, axis=0, keepdims=True))
        e = twice(ew[slot * 3 + h])
        sig = e / (e + p_rows[h])
        if edge:
            sig = jnp.where(near, 1.0, sig)
        prob = jnp.exp(z - m_new) * sig
        alphas.append(jnp.exp(m_old - m_new))
        out += [m_new, l_old * alphas[h] + jnp.sum(prob, axis=0, keepdims=True)]
        probs.append(prob.astype(BF16))
    for h in range(3):
        acc[h] = acc[h] * alphas[h] + dot_nn(kvt[slot, h * 128 + 64 : (h + 1) * 128, :], probs[h])
    return tuple(out)


def fwd_own_kernel(count, sc, q_ref, kv0, kv1, s0, s1, s2, s3, ds_ref, acc_ref, ml_ref, p_ref,
                   kvw, kvt, ew, er, acc):
    base = 2 * count
    fill_window(sc, count, base, (kv0, kv1), (s0, s1), kvw, kvt, ew)
    for part, refs in enumerate(((s2, s3), (s0, s1))):
        for rel in range(2):
            for r in range(count):
                place = part * base + tile_place(sc, r, rel, count)
                er[place] = jnp.exp(refs[rel][:, r * TILE : (r + 1) * TILE].astype(F32))

    def one_tile(r, unused):
        place = base + tile_place(sc, r, 0, count)
        low = sc[3 + r]
        ds_row = ds_ref[r][0:1, :]
        tile_start = place * TILE
        q_pad = padded_queries(q_ref, r)
        k_io = key_iota()
        inside = (k_io >= ds_row - tile_start) & (k_io <= query_iota())
        ds_first = jnp.min(ds_row, axis=1, keepdims=True)
        lane = lax.broadcasted_iota(jnp.int32, (8, TILE), 1)

        def carry_step(j, sums):
            return sums + jnp.where(lane >= ds_first - j * TILE, er[j], 0.0)

        carried = lax.fori_loop(low, place, carry_step, jnp.zeros((8, TILE), F32))
        carried = jnp.sum(carried, axis=1, keepdims=True)
        starts_before = ds_row < tile_start
        p_rows = []
        for h in range(3):
            local = jnp.sum(
                jnp.where(inside, twice(ew[(place - base) * 3 + h]), 0.0), axis=0, keepdims=True
            )
            prefix = local + jnp.where(starts_before, carried[h : h + 1, :], 0.0)
            p_rows.append(jnp.maximum(prefix * (1.0 / KEEP), TINY))
        acc[...] = jnp.zeros_like(acc)

        def chunk(j, state, edge):
            return fwd_chunk(
                state, j, j - base, edge, place, ds_row, q_pad, p_rows, kvw, kvt, ew, acc
            )

        state = (jnp.full((1, TILE), NEGATIVE, F32), jnp.zeros((1, TILE), F32)) * 3
        low = jnp.maximum(low, base)
        edge_low = jnp.maximum(place - 1, low)
        state = lax.fori_loop(low, edge_low, lambda j, s: chunk(j, s, False), state)
        state = lax.fori_loop(edge_low, place + 1, lambda j, s: chunk(j, s, True), state)
        zero = jnp.zeros((2, TILE), F32)
        acc_ref[r] = jnp.concatenate([acc[0], acc[1], acc[2]], axis=0)
        ml_ref[r] = jnp.concatenate(list(state[0::2]) + list(state[1::2]) + [zero], axis=0)
        p_ref[r] = jnp.concatenate(p_rows + p_rows + [zero], axis=0)
        return unused

    lax.fori_loop(0, count, one_tile, 0)


def fwd_prev_kernel(count, sc, q_ref, kv0, kv1, s0, s1, ds_ref, acc_ref, ml_ref, p_ref,
                    o_ref, of_ref, lse_ref, kvw, kvt, ew, acc):
    base = 2 * count
    fill_window(sc, count, 0, (kv0, kv1), (s0, s1), kvw, kvt, ew)

    def one_tile(r, unused):
        place = base + tile_place(sc, r, 0, count)
        low = sc[3 + r]
        ds_row = ds_ref[r][0:1, :]
        q_pad = padded_queries(q_ref, r)
        ml = ml_ref[r]
        p_all = p_ref[r]
        p_rows = [p_all[h : h + 1, :] for h in range(3)]
        before = acc_ref[r]
        for h in range(3):
            acc[h] = before[64 * h : 64 * h + 64, :]

        def chunk(j, state, edge):
            return fwd_chunk(state, j, j, edge, place, ds_row, q_pad, p_rows, kvw, kvt, ew, acc)

        state = ()
        for h in range(3):
            state += (ml[h : h + 1, :], ml[3 + h : 4 + h, :])
        edge_low = jnp.maximum(place - 1, low)
        state = lax.fori_loop(
            low, jnp.minimum(edge_low, base), lambda j, s: chunk(j, s, False), state
        )
        state = lax.fori_loop(edge_low, base, lambda j, s: chunk(j, s, True), state)
        stacked = jnp.concatenate([acc[h] / state[2 * h + 1] for h in range(3)], axis=0)
        of_ref[r] = stacked
        o_ref[sc[1] ^ r] = stacked.astype(BF16)
        lse = [state[2 * h] + jnp.log(state[2 * h + 1]) for h in range(3)]
        lse_ref[r] = jnp.concatenate(lse + lse + [jnp.zeros((2, TILE), F32)], axis=0)
        return unused

    lax.fori_loop(0, count, one_tile, 0)


def bwd_chunk(state, j, slot, edge, place, ds_row, q_pad, do_pad, both, lse, p_rows, delta,
              kvw, kvt, ew, dkv, dsl, dqt):
    mask, near = chunk_masks(ds_row, place, j, edge)
    kv = [kvw[slot, :, h * 128 : (h + 1) * 128] for h in range(3)]
    zs = [dot_nn(kv[h], q_pad[h]) for h in range(3)]
    dps = [dot_nn(kv[h], do_pad[h]) for h in range(3)]
    out, lows, pairs, fars = [], [], [], []
    for h in range(3):
        e = twice(ew[slot * 3 + h])
        r = 1.0 / (e + p_rows[h])
        sig = e * r
        if edge:
            sig = jnp.where(near, 1.0, sig)
        prob = jnp.exp(jnp.where(mask, zs[h] - lse[h], NEGATIVE)) * sig
        dz = prob * (dps[h] - delta[h])
        far = dz * (p_rows[h] * r)
        if edge:
            far = jnp.where(near, 0.0, far)
        out.append(state[h] - jnp.sum(far, axis=0, keepdims=True))
        fars.append(far[:, :128] + far[:, 128:])
        lows.append(dz.astype(BF16))
        pairs.append(jnp.concatenate([lows[h], prob.astype(BF16)], axis=1))
    for h in range(3):
        dqt[h] += dot_nn(kvt[slot, h * 128 : h * 128 + 64, :], lows[h])
    grads = [dot_nt(pairs[h], both[h]) for h in range(3)]
    dkv[slot] += jnp.concatenate(grads, axis=1)
    for h in range(3):
        dsl[slot * 3 + h] += fars[h]
    return tuple(out)


def bwd_rows(r, sc, q_ref, do_ref, of_ref, lse_ref, p_ref):
    q_pad = padded_queries(q_ref, r)
    do_all = do_ref[sc[1] ^ r]
    lse_all, p_all, of = lse_ref[r], p_ref[r], of_ref[r]
    zero = jnp.zeros((64, TILE), BF16)
    do_pad, both, lse, p_rows, delta = [], [], [], [], []
    for h in range(3):
        dh = do_all[64 * h : 64 * h + 64, :]
        do_pad.append(jnp.concatenate([zero, dh], axis=0))
        both.append(jnp.concatenate([q_pad[h], do_pad[h]], axis=1))
        lse.append(lse_all[h : h + 1, :])
        p_rows.append(p_all[h : h + 1, :])
        delta.append(
            jnp.sum(dh.astype(F32) * of[64 * h : 64 * h + 64, :], axis=0, keepdims=True)
        )
    return q_pad, do_pad, both, lse, p_rows, delta


def write_keys(sc, count, dkv, dsl, outs):
    for rel in range(2):
        big, small = outs[rel]
        for r in range(count):
            place = tile_place(sc, r, rel, count)
            big[r * TILE : (r + 1) * TILE, :] = dkv[place].astype(big.dtype)
            rows = []
            for h in range(3):
                summed = jnp.sum(dsl[place * 3 + h], axis=1, keepdims=True)
                rows.append(jnp.transpose(jnp.broadcast_to(summed, (TILE, 128)))[0:1, :])
            rows = jnp.concatenate(rows + [jnp.zeros((5, TILE), F32)], axis=0)
            small[:, r * TILE : (r + 1) * TILE] = rows.astype(small.dtype)


def bwd_prev_kernel(count, sc, q_ref, do_ref, of_ref, lse_ref, p_ref, kv0, kv1, s0, s1, ds_ref,
                    dq_ref, tau_ref, big0, big1, small0, small1, kvw, kvt, ew, dkv, dsl, dqt):
    base = 2 * count
    fill_window(sc, count, 0, (kv0, kv1), (s0, s1), kvw, kvt, ew)
    dkv[...] = jnp.zeros_like(dkv)
    dsl[...] = jnp.zeros_like(dsl)

    def one_tile(r, unused):
        place = base + tile_place(sc, r, 0, count)
        low = sc[3 + r]
        ds_row = ds_ref[r][0:1, :]
        dqt[...] = jnp.zeros_like(dqt)

        @pl.when(low >= base)
        def _():
            tau_ref[r] = jnp.zeros((8, TILE), F32)

        @pl.when(low < base)
        def _():
            rows = bwd_rows(r, sc, q_ref, do_ref, of_ref, lse_ref, p_ref)

            def chunk(j, state, edge):
                return bwd_chunk(
                    state, j, j, edge, place, ds_row, *rows, kvw, kvt, ew, dkv, dsl, dqt
                )

            state = (jnp.zeros((1, TILE), F32),) * 3
            edge_low = jnp.maximum(place - 1, low)
            state = lax.fori_loop(
                low, jnp.minimum(edge_low, base), lambda j, s: chunk(j, s, False), state
            )
            state = lax.fori_loop(edge_low, base, lambda j, s: chunk(j, s, True), state)
            tau_ref[r] = jnp.concatenate(list(state) + [jnp.zeros((5, TILE), F32)], axis=0)

        dq_ref[r] = jnp.concatenate([dqt[0], dqt[1], dqt[2]], axis=0)
        return unused

    lax.fori_loop(0, count, one_tile, 0)
    write_keys(sc, count, dkv, dsl, ((big0, small0), (big1, small1)))


def bwd_own_kernel(count, sc, q_ref, do_ref, of_ref, lse_ref, p_ref, kv0, kv1, s0, s1, ds_ref,
                   dqp_ref, tau_ref, dq_ref, big0, big1, small0, small1, carry_ref,
                   kvw, kvt, ew, dkv, dsl, dqt):
    base = 2 * count
    fill_window(sc, count, base, (kv0, kv1), (s0, s1), kvw, kvt, ew)
    dkv[...] = jnp.zeros_like(dkv)
    dsl[...] = jnp.zeros_like(dsl)
    carry_ref[...] = jnp.zeros_like(carry_ref)

    def one_tile(r, unused):
        place = base + tile_place(sc, r, 0, count)
        low = sc[3 + r]
        ds_row = ds_ref[r][0:1, :]
        tile_start = place * TILE
        rows = bwd_rows(r, sc, q_ref, do_ref, of_ref, lse_ref, p_ref)
        p_rows = rows[4]
        before = dqp_ref[r]
        for h in range(3):
            dqt[h] = before[64 * h : 64 * h + 64, :]

        def chunk(j, state, edge):
            return bwd_chunk(
                state, j, j - base, edge, place, ds_row, *rows, kvw, kvt, ew, dkv, dsl, dqt
            )

        tau = tau_ref[r]
        state = tuple(tau[h : h + 1, :] for h in range(3))
        low = jnp.maximum(low, base)
        edge_low = jnp.maximum(place - 1, low)
        state = lax.fori_loop(low, edge_low, lambda j, s: chunk(j, s, False), state)
        state = lax.fori_loop(edge_low, place + 1, lambda j, s: chunk(j, s, True), state)
        dq_ref[:, column(r)] = (
            jnp.concatenate([dqt[0], dqt[1], dqt[2]], axis=0) * ROOT
        ).astype(BF16)

        k_io = key_iota()
        inside = (k_io >= ds_row - tile_start) & (k_io <= query_iota())
        ds_first = jnp.min(ds_row, axis=1, keepdims=True)
        slot = place - base
        w_lane = []
        for h in range(3):
            w = state[h] / (p_rows[h] * float(KEEP))
            earlier = jnp.where(ds_row < tile_start, w, 0.0)
            w_lane.append(earlier[:, :128] + earlier[:, 128:])
            here = jnp.where(inside, w, 0.0)
            dsl[slot * 3 + h] += ew[slot * 3 + h] * (here[:, :128] + here[:, 128:])
            further = jnp.where(ds_row < base * TILE, w, 0.0)
            carry_ref[h : h + 1, :] += further[:, :128] + further[:, 128:]

        def later(j, unused):
            keep = lax.broadcasted_iota(jnp.int32, (TILE, 128), 0) >= ds_first - j * TILE
            for h in range(3):
                dsl[(j - base) * 3 + h] += jnp.where(keep, ew[(j - base) * 3 + h] * w_lane[h], 0.0)
            return unused

        lax.fori_loop(low, place, later, 0)
        return unused

    lax.fori_loop(0, count, one_tile, 0)
    write_keys(sc, count, dkv, dsl, ((big0, small0), (big1, small1)))


VM = pl.BlockSpec(memory_space=pltpu.VMEM)
SM = pl.BlockSpec(memory_space=pltpu.SMEM)
MIB = 1024 * 1024


def window_scratch(count):
    return [
        pltpu.VMEM((2 * count, TILE, 384), BF16),
        pltpu.VMEM((2 * count, 384, TILE), BF16),
        pltpu.VMEM((2 * count * 3, TILE, 128), F32),
    ]


def grad_scratch(count):
    return [
        pltpu.VMEM((2 * count, TILE, 384), F32),
        pltpu.VMEM((2 * count * 3, TILE, 128), F32),
        pltpu.VMEM((3, 64, TILE), F32),
    ]


def call(body, count, name, args, outs, scratch, work, room):
    return pl.pallas_call(
        functools.partial(body, count),
        out_shape=tuple(jax.ShapeDtypeStruct(s, t) for s, t in outs),
        in_specs=[SM] + [VM] * (len(args) - 1),
        out_specs=(VM,) * len(outs),
        scratch_shapes=scratch,
        compiler_params=pltpu.CompilerParams(vmem_limit_bytes=room * MIB),
        cost_estimate=pl.CostEstimate(flops=work, bytes_accessed=work // 400, transcendentals=0),
        name=name,
    )(*args)


def forward_own(count, scal, q, kvs, ss, ds):
    outs = (((count, 192, TILE), F32), ((count, 8, TILE), F32), ((count, 8, TILE), F32))
    scratch = window_scratch(count) + [
        pltpu.VMEM((4 * count, 8, TILE), F32),
        pltpu.VMEM((3, 64, TILE), F32),
    ]
    return call(fwd_own_kernel, count, "forward_own", (scal, q, *kvs, *ss, ds), outs, scratch, 20 * 10**9, 24)


def forward_prev(count, scal, q, kvs, ss, ds, acc, ml, p):
    outs = (((count, 192, TILE), BF16), ((count, 192, TILE), F32), ((count, 8, TILE), F32))
    scratch = window_scratch(count) + [pltpu.VMEM((3, 64, TILE), F32)]
    args = (scal, q, *kvs, *ss, ds, acc, ml, p)
    return call(fwd_prev_kernel, count, "forward_prev", args, outs, scratch, 8 * 10**9, 24)


def key_outs(count):
    rows = count * TILE
    return (((rows, 384), F32), ((rows, 384), BF16), ((8, rows), F32), ((8, rows), BF16))


def backward_prev(count, scal, q, do, of, lse, p, kvs, ss, ds):
    outs = (((count, 192, TILE), F32), ((count, 8, TILE), F32)) + key_outs(count)
    scratch = window_scratch(count) + grad_scratch(count)
    args = (scal, q, do, of, lse, p, *kvs, *ss, ds)
    return call(bwd_prev_kernel, count, "backward_prev", args, outs, scratch, 12 * 10**9, 32)


def backward_own(count, scal, q, do, of, lse, p, kvs, ss, ds, dq, tau):
    outs = (((192, count * TILE), BF16),) + key_outs(count) + (((8, 128), F32),)
    scratch = window_scratch(count) + grad_scratch(count)
    args = (scal, q, do, of, lse, p, *kvs, *ss, ds, dq, tau)
    return call(bwd_own_kernel, count, "backward_own", args, outs, scratch, 24 * 10**9, 32)


def hidden_kernel(n0, n1, dy0, dy1, bias, down, up, y0, y1, dt0, dt1, gd_ref, gu_ref, gb_ref,
                  n_all, dy_all, y_acc, d_acc):
    step = pl.program_id(0)
    tok = n0.shape[0]

    @pl.when(step == 0)
    def _():
        n_all[:tok, :] = n0[...]
        n_all[tok:, :] = n1[...]
        dy_all[:tok, :] = dy0[...]
        dy_all[tok:, :] = dy1[...]
        y_acc[...] = jnp.zeros_like(y_acc)
        d_acc[...] = jnp.zeros_like(d_acc)

    n = n_all[...]
    dy = dy_all[...]
    c0 = math.sqrt(2.0 / math.pi)
    ways, wide = 2, 384
    w_up = [up[:, :, i * wide : (i + 1) * wide].reshape(D, wide) for i in range(ways)]
    w_down = [down[4 * i : 4 * i + 4].reshape(wide, D) for i in range(ways)]
    pres = [dot_nn(n, w_up[i]) + bias[0:1, i * wide : (i + 1) * wide] for i in range(ways)]
    backs = [dot_nt(dy, w_down[i]) for i in range(ways)]
    for i in range(ways):
        pre = pres[i]
        squared = pre * pre
        th = jnp.tanh(c0 * pre * (1.0 + 0.044715 * squared))
        half = 0.5 * (1.0 + th)
        hidden = (pre * half).astype(BF16)
        slope = half + 0.5 * pre * (1.0 - th * th) * c0 * (1.0 + 3 * 0.044715 * squared)
        d_up = (backs[i] * slope).astype(BF16)
        y_acc[...] += dot_nn(hidden, w_down[i])
        d_acc[...] += dot_nt(d_up, w_up[i])
        gb_ref[:, i * wide : (i + 1) * wide] = jnp.broadcast_to(
            jnp.sum(d_up.astype(F32), axis=0, keepdims=True), (8, wide)
        )
        gd_ref[4 * i : 4 * i + 4] = dot_tn(hidden, dy).astype(BF16).reshape(4, 96, D)
        gu_ref[:, :, i * wide : (i + 1) * wide] = dot_tn(n, d_up).astype(BF16).reshape(16, 48, wide)

    @pl.when(step == pl.num_programs(0) - 1)
    def _():
        y0[...] = y_acc[:tok, :]
        y1[...] = y_acc[tok:, :]
        dt0[...] = d_acc[:tok, :]
        dt1[...] = d_acc[tok:, :].astype(BF16)


def hidden_passes(n0, n1, dy0, dy1, bias, packed):
    tok = n0.shape[0]
    whole = pl.BlockSpec((tok, D), lambda i: (0, 0))
    lanes = pl.BlockSpec((8, D), lambda i: (0, i))
    outs = (
        jax.ShapeDtypeStruct((tok, D), F32),
        jax.ShapeDtypeStruct((tok, D), F32),
        jax.ShapeDtypeStruct((tok, D), F32),
        jax.ShapeDtypeStruct((tok, D), BF16),
        jax.ShapeDtypeStruct((16, 96, D), BF16),
        jax.ShapeDtypeStruct((16, 96, D), BF16),
        jax.ShapeDtypeStruct((8, FF // 2), F32),
    )
    return pl.pallas_call(
        hidden_kernel,
        grid=(2,),
        out_shape=outs,
        in_specs=[
            whole,
            whole,
            whole,
            whole,
            lanes,
            pl.BlockSpec((8, 96, D), lambda i: (i, 0, 0)),
            pl.BlockSpec((16, 48, D), lambda i: (0, 2 + i, 0)),
        ],
        out_specs=(
            whole,
            whole,
            whole,
            whole,
            pl.BlockSpec((8, 96, D), lambda i: (i, 0, 0)),
            pl.BlockSpec((16, 48, D), lambda i: (0, i, 0)),
            lanes,
        ),
        scratch_shapes=[
            pltpu.VMEM((2 * tok, D), BF16),
            pltpu.VMEM((2 * tok, D), BF16),
            pltpu.VMEM((2 * tok, D), F32),
            pltpu.VMEM((2 * tok, D), F32),
        ],
        compiler_params=pltpu.CompilerParams(vmem_limit_bytes=56 * MIB),
        cost_estimate=pl.CostEstimate(flops=7 * 10**9, bytes_accessed=10**7, transcendentals=0),
        name="hidden_passes",
    )(n0, n1, dy0, dy1, bias, packed, packed)


def project_kernel(count, sc, own, sib, back, dq, s0, s1, s2, scores, cond, carry, x, w,
                   cat_ref, dn0_ref, dn_ref, sums_ref, cols_ref):
    place = (
        lax.broadcasted_iota(jnp.int32, (8, 64), 1)
        == lax.broadcasted_iota(jnp.int32, (8, 64), 0) + 3 * sc[1]
    ).astype(BF16)
    real = lax.broadcasted_iota(jnp.int32, (8, TILE), 0) < 3
    sums_ref[...] = jnp.zeros_like(sums_ref)
    cols_ref[...] = jnp.zeros_like(cols_ref)
    weights = w[...]
    for r in range(count):
        at = slice(r * TILE, (r + 1) * TILE)
        d_kv = own[at, :] + sib[at, :].astype(F32) + back[at, :].astype(F32)
        d_q = jnp.transpose(dq[:, at].astype(F32))
        after = jnp.exp(scores[:, at].astype(F32)) * jnp.sum(carry[...], axis=1, keepdims=True)
        d_s = s0[:, at] + s1[:, at].astype(F32) + s2[:, at].astype(F32)
        d_s = d_s + jnp.where(cond[0:1, at] > 0, after, 0.0)
        d_s = jnp.transpose(jnp.where(real, d_s, 0.0)).astype(BF16)
        d_s = dot_nn(d_s, place)
        cat = jnp.concatenate([d_kv, d_q, d_s], axis=1).astype(BF16)
        cat_ref[at, :] = cat
        d_n = dot_nt(cat, weights)
        if r == 0:
            dn0_ref[...] = d_n
        else:
            dn_ref[(r - 1) * TILE : r * TILE, :] = d_n.astype(BF16)
        unit, _ = normalize(x[at, :].astype(F32))
        sums_ref[0:1, :] += jnp.sum(d_n * unit, axis=0, keepdims=True)
        sums_ref[1:2, :] += jnp.sum(d_n, axis=0, keepdims=True)
        cols_ref[0:1, :] += jnp.sum(cat.astype(F32), axis=0, keepdims=True)


def project_back(count, *args):
    rows = count * TILE
    outs = (
        ((rows, 640), BF16),
        ((TILE, D), F32),
        ((rows - TILE, D), BF16),
        ((8, D), F32),
        ((8, 640), F32),
    )
    return call(project_kernel, count, "project_back", args, outs, [], 10**9, 56)


def other_core(x):
    return lax.ppermute(x, "core", [(0, 1), (1, 0)])


def next_chip(x, step):
    n = lax.axis_size("pair")
    return lax.ppermute(x, "pair", [(i, i + step) for i in range(n) if 0 <= i + step < n])


def spread(x, axes):
    n = lax.axis_size(axes)
    return lax.all_to_all(jnp.broadcast_to(x[None], (n,) + x.shape), axes, 0, 0)


def both_cores(mine, theirs, core, axis):
    return jnp.where(
        core == 0, jnp.stack([mine, theirs], axis), jnp.stack([theirs, mine], axis)
    )


def normalize(rows):
    centred = rows - jnp.mean(rows, axis=-1, keepdims=True)
    scale = lax.rsqrt(jnp.mean(centred * centred, axis=-1, keepdims=True) + EPS)
    return centred * scale, scale


def norm_pull(grad, unit, scale, gain):
    inner = grad * gain
    return scale * (
        inner
        - jnp.mean(inner, axis=-1, keepdims=True)
        - unit * jnp.mean(inner * unit, axis=-1, keepdims=True)
    )


def across(x, r):
    return lax.ppermute(x, "head", [(i, i ^ r) for i in range(lax.axis_size("head"))])


def shards(tokens, segment_ids, gains, biases, w_qkv, w_score, w_out, w_up, w_down, cotangent):
    groups = lax.axis_size("head")
    pairs = lax.axis_size("pair")
    devices = groups * pairs * 2
    same = groups * pairs
    h = lax.axis_index("head")
    p = lax.axis_index("pair")
    c = lax.axis_index("core")
    tok = tokens.shape[0]
    block = groups * tok
    count = groups
    super_rows = 2 * block
    total = super_rows * pairs
    rows_l = D // devices
    down_l = FF // devices
    swaps = (h & 1) == 1

    x_other = other_core(tokens)
    dy_other = other_core(cotangent)
    x_mine = jnp.where(swaps, x_other, tokens)
    x_parts = [x_mine] + [across(x_mine, r) for r in range(1, groups)]

    part = w_qkv.astype(BF16).reshape(rows_l, 3, groups, 3, HDIM)
    part_q = part[:, 0].reshape(rows_l, groups, 192)
    part_kv = part[:, 1:].transpose(0, 2, 3, 1, 4).reshape(rows_l, groups, 384)
    id_lanes = -(-tok // rows_l)
    own_ids = jnp.pad(segment_ids.astype(BF16), (0, id_lanes * rows_l - tok))
    small = jnp.concatenate(
        [
            w_score.astype(BF16).reshape(rows_l, HEADS),
            gains.astype(BF16).reshape(rows_l, 2),
            biases.astype(BF16).reshape(rows_l, 10),
            own_ids.reshape(rows_l, id_lanes),
        ],
        axis=1,
    )
    small = jnp.broadcast_to(small[:, None], (rows_l, groups, small.shape[1]))
    part = jnp.concatenate([part_kv, part_q, small], axis=-1).transpose(1, 0, 2)
    filled = part.shape[2]
    width = -(-filled // 128) * 128
    part = jnp.pad(part, ((0, 0), (0, 0), (0, width - filled)))
    part = jnp.broadcast_to(part[:, None], (groups, pairs, rows_l, width))
    w_same = lax.all_to_all(part.reshape(same, rows_l, width), SAME, 0, 0)
    up_rows = w_up.astype(BF16).reshape(rows_l, same, 2, down_l)
    up_mine = jnp.where(c == 0, up_rows[:, :, 0], up_rows[:, :, 1]).reshape(rows_l, FF // 2)
    up_send = jnp.where(c == 0, up_rows[:, :, 1], up_rows[:, :, 0]).reshape(rows_l, FF // 2)
    up_both = both_cores(up_mine, other_core(up_send), c, 0).reshape(2 * rows_l, FF // 2)
    down_mine = w_down.astype(BF16).reshape(down_l, D)
    out_mine = w_out.astype(BF16).reshape(rows_l, D)
    a, b, e = down_l, down_l + 2 * rows_l, down_l + 4 * rows_l
    pack = jnp.concatenate([down_mine, up_both[:, :D], up_both[:, D:]], axis=0)
    packed = lax.all_gather(pack, "pair", axis=0, tiled=False)
    packed, _ = lax.optimization_barrier((packed, w_same))
    out_mine, _ = lax.optimization_barrier((out_mine, w_same))
    packed = lax.all_gather(packed, "head", axis=0, tiled=False).reshape((same,) + pack.shape)
    out_same = spread(out_mine, SAME)
    tall = down_l
    if tall != 96:
        packed = jnp.concatenate(
            [
                packed[:, :a].reshape(16, 96, D),
                packed[:, a:b].reshape(16, 48, D),
                packed[:, b:e].reshape(16, 48, D),
            ],
            axis=1,
        )

    w_both = both_cores(w_same, other_core(w_same), c, 1).reshape(D, width)
    w_kv, w_q = w_both[:, :384], w_both[:, 384:576]
    gain_rows = w_both[:, 588:590].reshape(2, D).astype(F32)
    bias_rows = w_both[:, 590:600].reshape(10, D).astype(F32)
    ids_all = w_both[:, 600 : 600 + id_lanes].reshape(devices, rows_l * id_lanes)[:, :tok]
    ids_all = ids_all.astype(jnp.int32).reshape(groups, pairs, 2, tok)
    ids_all = ids_all.transpose(1, 2, 0, 3).reshape(total)

    x_low = jnp.concatenate(x_parts, axis=0)
    x_rows = x_low.astype(F32)
    unit_one, scale_one = normalize(x_rows)
    normed = (unit_one * gain_rows[0] + bias_rows[0]).astype(BF16)
    w_s = lax.dynamic_slice_in_dim(w_both[:, 576:588], 3 * h, 3, axis=1)
    w_s = jnp.pad(w_s, ((0, 0), (0, 5)))
    scores = lax.dot_general(
        w_s, normed, (((0,), (1,)), ((), ())), preferred_element_type=F32
    ).astype(BF16)
    s_sib = other_core(scores)
    s_prev = next_chip(jnp.stack([scores, s_sib]), 1)
    bias_v = lax.dynamic_slice_in_dim(bias_rows[2:3], 192 * h, 192, axis=1).reshape(1, 3, 1, HDIM)
    bias_kv = jnp.concatenate([jnp.zeros_like(bias_v), bias_v], axis=2).reshape(1, 384)
    kv = (dot_nn(normed, w_kv) + bias_kv).astype(BF16)
    kv, s_prev, out_same = lax.optimization_barrier((kv, s_prev, out_same))
    m_out = both_cores(out_same, other_core(out_same), c, 1).reshape(D, D)
    kv_prev = next_chip(kv, 1)
    kv_sib = other_core(kv)
    bias_q = lax.dynamic_slice_in_dim(bias_rows[1:2], 192 * h, 192, axis=1).reshape(192, 1)
    q = lax.dot_general(w_q, normed, (((0,), (1,)), ((), ())), preferred_element_type=F32)
    q = (q + bias_q).astype(BF16)

    padded = jnp.concatenate([jnp.full((super_rows,), -1, jnp.int32), ids_all])
    ids_win = lax.dynamic_slice_in_dim(padded, p * super_rows, 2 * super_rows)
    k_of = h ^ jnp.arange(count)
    tile_of = k_of + count * ((c + k_of) & 1)
    ids_super = ids_win[super_rows:].reshape(1, 2 * count, TILE)
    picked = tile_of[:, None, None] == jnp.arange(2 * count)[None, :, None]
    ids_q = jnp.sum(jnp.where(picked, ids_super, 0), axis=1)
    starts = jnp.sum((ids_win[None, :, None] < ids_q[:, None, :]).astype(jnp.int32), axis=1)
    lows = jnp.min(starts, axis=1) // TILE
    scal = jnp.concatenate([jnp.stack([c, h]), jnp.min(lows)[None], lows]).astype(jnp.int32)
    ds = jnp.broadcast_to(starts[:, None, :], (count, 8, TILE))

    own_kvs, own_ss = (kv, kv_sib), (scores, s_sib)
    prev_ss = (s_prev[0], s_prev[1])
    acc, ml, pr = forward_own(count, scal, q, own_kvs, own_ss + prev_ss, ds)
    dy_mine = jnp.where(swaps, dy_other, cotangent)
    dy_sib = jnp.where(swaps, cotangent, dy_other)
    stripes = bias_rows[5:9].reshape(same, 2, down_l)
    up_half = jnp.where(c == 0, stripes[:, 0], stripes[:, 1]).reshape(1, FF // 2)
    up_half = jnp.broadcast_to(up_half, (8, FF // 2))
    kv_prev, acc, dy_mine, dy_sib, up_half = lax.optimization_barrier(
        (kv_prev, acc, dy_mine, dy_sib, up_half)
    )
    prev_kvs = (kv_prev, other_core(kv_prev))
    o, of, lse = forward_prev(count, scal, q, prev_kvs, prev_ss, ds, acc, ml, pr)

    attn = lax.all_to_all(o, "head", 0, 0).reshape(D, tok)
    middle = x_mine.astype(F32) + dot_tn(attn, m_out) + bias_rows[3]
    unit_two, scale_two = normalize(middle)
    n_two = (unit_two * gain_rows[1] + bias_rows[4]).astype(BF16)
    n_sib = other_core(n_two)
    y0, y1, d_two_0, d_two_1, g_down, g_up, g_up_bias = hidden_passes(
        n_two, n_sib, dy_mine, dy_sib, up_half, packed
    )
    d_two = d_two_0 + other_core(d_two_1).astype(F32)
    y = y0 + other_core(y1)
    result_mine = (middle + y + bias_rows[9]).astype(BF16)
    result = jnp.where(swaps, other_core(result_mine), result_mine)

    g_up_bias = g_up_bias[0]
    g_gain_two = jnp.sum(d_two * unit_two, axis=0)
    g_shift_two = jnp.sum(d_two, axis=0)
    dy_f = dy_mine.astype(F32)
    g_down_bias = jnp.sum(dy_f, axis=0)

    d_middle = dy_f + norm_pull(d_two, unit_two, scale_two, gain_rows[1])
    d_branch = d_middle.astype(BF16)
    g_out_bias = jnp.sum(d_branch.astype(F32), axis=0)
    d_sent = dot_nt(m_out, d_branch).astype(BF16)
    d_branch, d_sent = lax.optimization_barrier((d_branch, d_sent))
    d_heads = lax.all_to_all(d_sent.reshape(groups, 192, tok), "head", 0, 0)
    g_out = dot_nn(attn, d_branch)

    g_parts = [
        g_down.reshape(same, a, D),
        g_up[:, :48].reshape(same, b - a, D),
        g_up[:, 48:].reshape(same, e - b, D),
    ]
    g_out_rows = g_out.reshape(same, 2, rows_l, D)
    g_out_keep = jnp.where(c == 0, g_out_rows[:, 0], g_out_rows[:, 1])
    g_out_send = jnp.where(c == 0, g_out_rows[:, 1], g_out_rows[:, 0]).astype(BF16)
    g_out_same = (g_out_keep + other_core(g_out_send).astype(F32)).astype(BF16)
    g_pack = jnp.concatenate(g_parts + [g_out_same], axis=1)
    g_half = lax.psum_scatter(
        g_pack.reshape(groups, pairs, e + rows_l, D), "head", scatter_dimension=0, tiled=False
    )

    rows = (q, d_heads, of, lse, pr)
    dq_part, tau, prev, to_cross, s_prev_part, s_to_cross = backward_prev(
        count, scal, *rows, prev_kvs, prev_ss, ds
    )
    to_prev = (prev + other_core(to_cross).astype(F32)).astype(BF16)
    to_prev, tau = lax.optimization_barrier((to_prev, tau))
    back = next_chip(to_prev, -1)
    s_back = next_chip((s_prev_part + other_core(s_to_cross).astype(F32)).astype(BF16), -1)
    dq, own, to_sib, s_own, s_to_sib, carry = backward_own(
        count, scal, *rows, own_kvs, own_ss, ds, dq_part, tau
    )
    carry = next_chip(carry + other_core(carry), -1)
    back, s_back, to_sib, s_to_sib = lax.optimization_barrier((back, s_back, to_sib, s_to_sib))
    sib_kv, sib_s = other_core(to_sib), other_core(s_to_sib)

    sib_kv, g_half = lax.optimization_barrier((sib_kv, g_half))

    continued = (ids_q == ids_win[-1]).astype(jnp.int32).reshape(1, block)
    continued = jnp.broadcast_to(continued, (8, block))
    cat, d_norm_sum, d_norm_low, sums, cols = project_back(
        count, scal, own, sib_kv, back, dq, s_own, sib_s, s_back, scores, continued, carry, x_low, w_both[:, :640]
    )
    cat, d_norm_low = lax.optimization_barrier((cat, d_norm_low))
    for r in range(1, groups):
        d_norm_sum = d_norm_sum + across(d_norm_low[(r - 1) * tok : r * tok], r).astype(F32)

    mine = jnp.arange(D) // 192 == h
    g_q_bias = jnp.where(mine, jnp.tile(cols[0, 384:576], groups), 0.0)
    g_v_bias = cols[0, :384].reshape(3, 2, HDIM)[:, 1].reshape(192)
    g_v_bias = jnp.where(mine, jnp.tile(g_v_bias, groups), 0.0)
    halves = jnp.stack([g_up_bias.reshape(same, down_l)] * 2, axis=1)
    halves = jnp.where(jnp.arange(2)[None, :, None] == c, halves, 0.0).reshape(4, D)
    g_bias_rows = jnp.concatenate(
        [
            jnp.stack([sums[1], g_q_bias, g_v_bias, g_out_bias, g_shift_two]),
            halves,
            g_down_bias[None],
        ],
        axis=0,
    )
    small = jnp.concatenate(
        [jnp.stack([sums[0], g_gain_two]).reshape(D, 2), g_bias_rows.reshape(D, 10)], axis=1
    )
    g_all = dot_tn(normed, cat) + jnp.pad(small, ((0, 0), (588, 40)))
    g_all = g_all.astype(BF16)
    came = lax.all_to_all(g_all, ALL, 0, 0, tiled=True)
    g_pack = lax.psum_scatter(g_half, "pair", scatter_dimension=0, tiled=False).astype(F32)
    grad_w_down = g_pack[:a].reshape(-1)
    grad_w_out = g_pack[e:].reshape(-1)
    g_up_rows = jnp.concatenate([g_pack[a:b], g_pack[b:e]], axis=1).reshape(2, rows_l, FF // 2)
    g_up_keep = jnp.where(c == 0, g_up_rows[0], g_up_rows[1])
    g_up_came = other_core(jnp.where(c == 0, g_up_rows[1], g_up_rows[0]))
    grad_w_up = both_cores(
        g_up_keep.reshape(rows_l, same, down_l), g_up_came.reshape(rows_l, same, down_l), c, 2
    ).reshape(-1)
    came, grad_w_down, grad_w_out, grad_w_up = lax.optimization_barrier(
        (came, grad_w_down, grad_w_out, grad_w_up)
    )
    came = came.astype(F32)
    came = jnp.sum(came.reshape(groups, 2 * pairs, rows_l, 640), axis=1)
    grad_kv = came[:, :, :384].reshape(groups, rows_l, 3, 2, HDIM)
    grad_kv = grad_kv.transpose(1, 3, 0, 2, 4).reshape(rows_l, 2, D)
    grad_q = came[:, :, 384:576].transpose(1, 0, 2).reshape(rows_l, 1, D)
    grad_w_qkv = jnp.concatenate([grad_q, grad_kv], axis=1).reshape(-1)
    small_sum = jnp.sum(came[:, :, 576:600], axis=0)
    grad_w_score = small_sum[:, :12].reshape(-1)
    grad_gains = small_sum[:, 12:14].reshape(-1)
    grad_biases = small_sum[:, 14:24].reshape(-1)

    unit_mine, scale_mine = unit_one[:tok], scale_one[:tok]
    grad_mine = d_middle + norm_pull(d_norm_sum, unit_mine, scale_mine, gain_rows[0])
    grad_mine = grad_mine.astype(BF16)
    grad_tokens = jnp.where(swaps, other_core(grad_mine), grad_mine)
    return (
        result,
        grad_tokens,
        grad_gains,
        grad_biases,
        grad_w_qkv,
        grad_w_score,
        grad_w_out,
        grad_w_up,
        grad_w_down,
    )


def solution(mesh):
    groups = mesh.devices.shape[0]
    fine = Mesh(mesh.devices.reshape(groups, -1, 2), ALL)
    rows = P(("pair", "core", "head"), None)
    flat = P(ALL)
    in_specs = (rows, P(("pair", "core", "head"))) + (flat,) * 7 + (rows,)
    out_specs = (rows, rows) + (flat,) * 7
    return jax.shard_map(shards, mesh=fine, in_specs=in_specs, out_specs=out_specs, check_vma=False)
```

```python
import functools
import math

import jax
import jax.numpy as jnp
from jax import lax
from jax.experimental import pallas as pl
from jax.experimental.pallas import tpu as pltpu
from jax.sharding import Mesh
from jax.sharding import PartitionSpec as P

D = 768
HEADS = 12
HDIM = 64
FF = 3072
WINDOW = 64
KEEP = 64
MOST = 2000

EPS = 1e-05
NEGATIVE = -1e30
TINY = 1e-37
TILE = 256
ROOT = 1.0 / math.sqrt(HDIM)
F32 = jnp.float32
BF16 = jnp.bfloat16
ALL = ("head", "pair", "core")
SAME = ("head", "pair")


def dot_nn(a, b):
    return lax.dot_general(a, b, (((1,), (0,)), ((), ())), preferred_element_type=F32)


def dot_nt(a, b):
    return lax.dot_general(a, b, (((1,), (1,)), ((), ())), preferred_element_type=F32)


def dot_tn(a, b):
    return lax.dot_general(a, b, (((0,), (0,)), ((), ())), preferred_element_type=F32)


def tile_place(sc, r, rel, count):
    k = sc[1] ^ r
    return k + count * ((sc[0] + rel + k) & 1)


def fill_window(sc, count, base, kv_refs, s_refs, kvw, kvt, ew):
    eye = (
        lax.broadcasted_iota(jnp.int32, (128, 128), 0)
        == lax.broadcasted_iota(jnp.int32, (128, 128), 1)
    ).astype(BF16)
    for rel in range(2):
        for r in range(count):
            place = tile_place(sc, r, rel, count)

            @pl.when(base + place >= sc[2])
            def _(rel=rel, r=r, place=place):
                block = kv_refs[rel][r * TILE : (r + 1) * TILE, :]
                kvw[place] = block
                rows = s_refs[rel][:, r * TILE : (r + 1) * TILE]
                for h in range(3):
                    kvt[place, h * 128 : (h + 1) * 128, :] = dot_nt(
                        eye, block[:, h * 128 : (h + 1) * 128]
                    ).astype(BF16)
                    pick = (lax.broadcasted_iota(jnp.int32, (8, 128), 0) == h).astype(BF16)
                    ew[place * 3 + h] = jnp.exp(dot_tn(rows, pick))


def twice(x):
    return jnp.concatenate([x, x], axis=1)


def key_iota():
    return lax.broadcasted_iota(jnp.int32, (TILE, TILE), 0)


def query_iota():
    return lax.broadcasted_iota(jnp.int32, (1, TILE), 1)


def column(r):
    return pl.ds(pl.multiple_of(r * TILE, TILE), TILE)


def padded_queries(q_ref, r):
    zero = jnp.zeros((64, TILE), BF16)
    q_all = q_ref[:, column(r)] * BF16(ROOT)
    return [
        jnp.concatenate([q_all[64 * h : 64 * h + 64, :], zero], axis=0) for h in range(3)
    ]


def chunk_masks(ds_row, place, j, edge):
    k_io = key_iota()
    mask = k_io >= ds_row - j * TILE
    near = None
    if edge:
        ahead = query_iota() + (place - j) * TILE
        mask = mask & (k_io <= ahead)
        near = k_io > ahead - WINDOW
    return mask, near


def fwd_chunk(state, j, slot, edge, place, ds_row, q_pad, p_rows, kvw, kvt, ew, acc):
    mask, near = chunk_masks(ds_row, place, j, edge)
    zs = [dot_nn(kvw[slot, :, h * 128 : (h + 1) * 128], q_pad[h]) for h in range(3)]
    out, probs, alphas = [], [], []
    for h in range(3):
        m_old, l_old = state[2 * h], state[2 * h + 1]
        z = jnp.where(mask, zs[h], NEGATIVE)
        m_new = jnp.maximum(m_old, jnp.max(z, axis=0, keepdims=True))
        e = twice(ew[slot * 3 + h])
        sig = e / (e + p_rows[h])
        if edge:
            sig = jnp.where(near, 1.0, sig)
        prob = jnp.exp(z - m_new) * sig
        alphas.append(jnp.exp(m_old - m_new))
        out += [m_new, l_old * alphas[h] + jnp.sum(prob, axis=0, keepdims=True)]
        probs.append(prob.astype(BF16))
    for h in range(3):
        acc[h] = acc[h] * alphas[h] + dot_nn(kvt[slot, h * 128 + 64 : (h + 1) * 128, :], probs[h])
    return tuple(out)


def fwd_own_kernel(count, sc, q_ref, kv0, kv1, s0, s1, s2, s3, ds_ref, acc_ref, ml_ref, p_ref,
                   kvw, kvt, ew, er, acc):
    base = 2 * count
    fill_window(sc, count, base, (kv0, kv1), (s0, s1), kvw, kvt, ew)
    for part, refs in enumerate(((s2, s3), (s0, s1))):
        for rel in range(2):
            for r in range(count):
                place = part * base + tile_place(sc, r, rel, count)
                er[place] = jnp.exp(refs[rel][:, r * TILE : (r + 1) * TILE].astype(F32))

    def one_tile(r, unused):
        place = base + tile_place(sc, r, 0, count)
        low = sc[3 + r]
        ds_row = ds_ref[r][0:1, :]
        tile_start = place * TILE
        q_pad = padded_queries(q_ref, r)
        k_io = key_iota()
        inside = (k_io >= ds_row - tile_start) & (k_io <= query_iota())
        ds_first = jnp.min(ds_row, axis=1, keepdims=True)
        lane = lax.broadcasted_iota(jnp.int32, (8, TILE), 1)

        def carry_step(j, sums):
            return sums + jnp.where(lane >= ds_first - j * TILE, er[j], 0.0)

        carried = lax.fori_loop(low, place, carry_step, jnp.zeros((8, TILE), F32))
        carried = jnp.sum(carried, axis=1, keepdims=True)
        starts_before = ds_row < tile_start
        p_rows = []
        for h in range(3):
            local = jnp.sum(
                jnp.where(inside, twice(ew[(place - base) * 3 + h]), 0.0), axis=0, keepdims=True
            )
            prefix = local + jnp.where(starts_before, carried[h : h + 1, :], 0.0)
            p_rows.append(jnp.maximum(prefix * (1.0 / KEEP), TINY))
        acc[...] = jnp.zeros_like(acc)

        def chunk(j, state, edge):
            return fwd_chunk(
                state, j, j - base, edge, place, ds_row, q_pad, p_rows, kvw, kvt, ew, acc
            )

        state = (jnp.full((1, TILE), NEGATIVE, F32), jnp.zeros((1, TILE), F32)) * 3
        low = jnp.maximum(low, base)
        edge_low = jnp.maximum(place - 1, low)
        state = lax.fori_loop(low, edge_low, lambda j, s: chunk(j, s, False), state)
        state = lax.fori_loop(edge_low, place + 1, lambda j, s: chunk(j, s, True), state)
        zero = jnp.zeros((2, TILE), F32)
        acc_ref[r] = jnp.concatenate([acc[0], acc[1], acc[2]], axis=0)
        ml_ref[r] = jnp.concatenate(list(state[0::2]) + list(state[1::2]) + [zero], axis=0)
        p_ref[r] = jnp.concatenate(p_rows + p_rows + [zero], axis=0)
        return unused

    lax.fori_loop(0, count, one_tile, 0)


def fwd_prev_kernel(count, sc, q_ref, kv0, kv1, s0, s1, ds_ref, acc_ref, ml_ref, p_ref,
                    o_ref, of_ref, lse_ref, kvw, kvt, ew, acc):
    base = 2 * count
    fill_window(sc, count, 0, (kv0, kv1), (s0, s1), kvw, kvt, ew)

    def one_tile(r, unused):
        place = base + tile_place(sc, r, 0, count)
        low = sc[3 + r]
        ds_row = ds_ref[r][0:1, :]
        q_pad = padded_queries(q_ref, r)
        ml = ml_ref[r]
        p_all = p_ref[r]
        p_rows = [p_all[h : h + 1, :] for h in range(3)]
        before = acc_ref[r]
        for h in range(3):
            acc[h] = before[64 * h : 64 * h + 64, :]

        def chunk(j, state, edge):
            return fwd_chunk(state, j, j, edge, place, ds_row, q_pad, p_rows, kvw, kvt, ew, acc)

        state = ()
        for h in range(3):
            state += (ml[h : h + 1, :], ml[3 + h : 4 + h, :])
        edge_low = jnp.maximum(place - 1, low)
        state = lax.fori_loop(
            low, jnp.minimum(edge_low, base), lambda j, s: chunk(j, s, False), state
        )
        state = lax.fori_loop(edge_low, base, lambda j, s: chunk(j, s, True), state)
        stacked = jnp.concatenate([acc[h] / state[2 * h + 1] for h in range(3)], axis=0)
        of_ref[r] = stacked
        o_ref[sc[1] ^ r] = stacked.astype(BF16)
        lse = [state[2 * h] + jnp.log(state[2 * h + 1]) for h in range(3)]
        lse_ref[r] = jnp.concatenate(lse + lse + [jnp.zeros((2, TILE), F32)], axis=0)
        return unused

    lax.fori_loop(0, count, one_tile, 0)


def bwd_chunk(state, j, slot, edge, place, ds_row, q_pad, do_pad, both, lse, p_rows, delta,
              kvw, kvt, ew, dkv, dsl, dqt):
    mask, near = chunk_masks(ds_row, place, j, edge)
    kv = [kvw[slot, :, h * 128 : (h + 1) * 128] for h in range(3)]
    zds = [dot_nn(kv[h], both[h]) for h in range(3)]
    zs = [zd[:, :TILE] for zd in zds]
    dps = [zd[:, TILE:] for zd in zds]
    out, lows, pairs, fars = [], [], [], []
    for h in range(3):
        e = twice(ew[slot * 3 + h])
        r = 1.0 / (e + p_rows[h])
        sig = e * r
        if edge:
            sig = jnp.where(near, 1.0, sig)
        prob = jnp.exp(jnp.where(mask, zs[h] - lse[h], NEGATIVE)) * sig
        dz = prob * (dps[h] - delta[h])
        far = dz * (p_rows[h] * r)
        if edge:
            far = jnp.where(near, 0.0, far)
        out.append(state[h] - jnp.sum(far, axis=0, keepdims=True))
        fars.append(far[:, :128] + far[:, 128:])
        lows.append(dz.astype(BF16))
        pairs.append(jnp.concatenate([lows[h], prob.astype(BF16)], axis=1))
    grads = [dot_nt(pairs[h], both[h]) for h in range(3)]
    for h in range(3):
        dqt[h] += dot_nn(kvt[slot, h * 128 : h * 128 + 64, :], lows[h])
    dkv[slot] += jnp.concatenate(grads, axis=1)
    for h in range(3):
        dsl[slot * 3 + h] += fars[h]
    return tuple(out)


def bwd_rows(r, sc, q_ref, do_ref, of_ref, lse_ref, p_ref):
    q_pad = padded_queries(q_ref, r)
    do_all = do_ref[sc[1] ^ r]
    lse_all, p_all, of = lse_ref[r], p_ref[r], of_ref[r]
    zero = jnp.zeros((64, TILE), BF16)
    do_pad, both, lse, p_rows, delta = [], [], [], [], []
    for h in range(3):
        dh = do_all[64 * h : 64 * h + 64, :]
        do_pad.append(jnp.concatenate([zero, dh], axis=0))
        both.append(jnp.concatenate([q_pad[h], do_pad[h]], axis=1))
        lse.append(lse_all[h : h + 1, :])
        p_rows.append(p_all[h : h + 1, :])
        delta.append(
            jnp.sum(dh.astype(F32) * of[64 * h : 64 * h + 64, :], axis=0, keepdims=True)
        )
    return q_pad, do_pad, both, lse, p_rows, delta


def write_keys(sc, count, dkv, dsl, outs):
    for rel in range(2):
        big, small = outs[rel]
        for r in range(count):
            place = tile_place(sc, r, rel, count)
            big[r * TILE : (r + 1) * TILE, :] = dkv[place].astype(big.dtype)
            rows = []
            for h in range(3):
                summed = jnp.sum(dsl[place * 3 + h], axis=1, keepdims=True)
                rows.append(jnp.transpose(jnp.broadcast_to(summed, (TILE, 128)))[0:1, :])
            rows = jnp.concatenate(rows + [jnp.zeros((5, TILE), F32)], axis=0)
            small[:, r * TILE : (r + 1) * TILE] = rows.astype(small.dtype)


def bwd_prev_kernel(count, sc, q_ref, do_ref, of_ref, lse_ref, p_ref, kv0, kv1, s0, s1, ds_ref,
                    dq_ref, tau_ref, big0, big1, small0, small1, kvw, kvt, ew, dkv, dsl, dqt):
    base = 2 * count
    fill_window(sc, count, 0, (kv0, kv1), (s0, s1), kvw, kvt, ew)
    dkv[...] = jnp.zeros_like(dkv)
    dsl[...] = jnp.zeros_like(dsl)

    def one_tile(r, unused):
        place = base + tile_place(sc, r, 0, count)
        low = sc[3 + r]
        ds_row = ds_ref[r][0:1, :]
        dqt[...] = jnp.zeros_like(dqt)

        @pl.when(low >= base)
        def _():
            tau_ref[r] = jnp.zeros((8, TILE), F32)

        @pl.when(low < base)
        def _():
            rows = bwd_rows(r, sc, q_ref, do_ref, of_ref, lse_ref, p_ref)

            def chunk(j, state, edge):
                return bwd_chunk(
                    state, j, j, edge, place, ds_row, *rows, kvw, kvt, ew, dkv, dsl, dqt
                )

            state = (jnp.zeros((1, TILE), F32),) * 3
            edge_low = jnp.maximum(place - 1, low)
            state = lax.fori_loop(
                low, jnp.minimum(edge_low, base), lambda j, s: chunk(j, s, False), state
            )
            state = lax.fori_loop(edge_low, base, lambda j, s: chunk(j, s, True), state)
            tau_ref[r] = jnp.concatenate(list(state) + [jnp.zeros((5, TILE), F32)], axis=0)

        dq_ref[r] = jnp.concatenate([dqt[0], dqt[1], dqt[2]], axis=0)
        return unused

    lax.fori_loop(0, count, one_tile, 0)
    write_keys(sc, count, dkv, dsl, ((big0, small0), (big1, small1)))


def bwd_own_kernel(count, sc, q_ref, do_ref, of_ref, lse_ref, p_ref, kv0, kv1, s0, s1, ds_ref,
                   dqp_ref, tau_ref, dq_ref, big0, big1, small0, small1, carry_ref,
                   kvw, kvt, ew, dkv, dsl, dqt):
    base = 2 * count
    fill_window(sc, count, base, (kv0, kv1), (s0, s1), kvw, kvt, ew)
    dkv[...] = jnp.zeros_like(dkv)
    dsl[...] = jnp.zeros_like(dsl)
    carry_ref[...] = jnp.zeros_like(carry_ref)

    def one_tile(r, unused):
        place = base + tile_place(sc, r, 0, count)
        low = sc[3 + r]
        ds_row = ds_ref[r][0:1, :]
        tile_start = place * TILE
        rows = bwd_rows(r, sc, q_ref, do_ref, of_ref, lse_ref, p_ref)
        p_rows = rows[4]
        before = dqp_ref[r]
        for h in range(3):
            dqt[h] = before[64 * h : 64 * h + 64, :]

        def chunk(j, state, edge):
            return bwd_chunk(
                state, j, j - base, edge, place, ds_row, *rows, kvw, kvt, ew, dkv, dsl, dqt
            )

        tau = tau_ref[r]
        state = tuple(tau[h : h + 1, :] for h in range(3))
        low = jnp.maximum(low, base)
        edge_low = jnp.maximum(place - 1, low)
        state = lax.fori_loop(low, edge_low, lambda j, s: chunk(j, s, False), state)
        state = lax.fori_loop(edge_low, place + 1, lambda j, s: chunk(j, s, True), state)
        dq_ref[:, column(r)] = (
            jnp.concatenate([dqt[0], dqt[1], dqt[2]], axis=0) * ROOT
        ).astype(BF16)

        k_io = key_iota()
        inside = (k_io >= ds_row - tile_start) & (k_io <= query_iota())
        ds_first = jnp.min(ds_row, axis=1, keepdims=True)
        slot = place - base
        w_lane = []
        for h in range(3):
            w = state[h] / (p_rows[h] * float(KEEP))
            earlier = jnp.where(ds_row < tile_start, w, 0.0)
            w_lane.append(earlier[:, :128] + earlier[:, 128:])
            here = jnp.where(inside, w, 0.0)
            dsl[slot * 3 + h] += ew[slot * 3 + h] * (here[:, :128] + here[:, 128:])
            further = jnp.where(ds_row < base * TILE, w, 0.0)
            carry_ref[h : h + 1, :] += further[:, :128] + further[:, 128:]

        def later(j, unused):
            keep = lax.broadcasted_iota(jnp.int32, (TILE, 128), 0) >= ds_first - j * TILE
            for h in range(3):
                dsl[(j - base) * 3 + h] += jnp.where(keep, ew[(j - base) * 3 + h] * w_lane[h], 0.0)
            return unused

        lax.fori_loop(low, place, later, 0)
        return unused

    lax.fori_loop(0, count, one_tile, 0)
    write_keys(sc, count, dkv, dsl, ((big0, small0), (big1, small1)))


VM = pl.BlockSpec(memory_space=pltpu.VMEM)
SM = pl.BlockSpec(memory_space=pltpu.SMEM)
MIB = 1024 * 1024


def window_scratch(count):
    return [
        pltpu.VMEM((2 * count, TILE, 384), BF16),
        pltpu.VMEM((2 * count, 384, TILE), BF16),
        pltpu.VMEM((2 * count * 3, TILE, 128), F32),
    ]


def grad_scratch(count):
    return [
        pltpu.VMEM((2 * count, TILE, 384), F32),
        pltpu.VMEM((2 * count * 3, TILE, 128), F32),
        pltpu.VMEM((3, 64, TILE), F32),
    ]


def call(body, count, name, args, outs, scratch, work, room):
    return pl.pallas_call(
        functools.partial(body, count),
        out_shape=tuple(jax.ShapeDtypeStruct(s, t) for s, t in outs),
        in_specs=[SM] + [VM] * (len(args) - 1),
        out_specs=(VM,) * len(outs),
        scratch_shapes=scratch,
        compiler_params=pltpu.CompilerParams(vmem_limit_bytes=room * MIB),
        cost_estimate=pl.CostEstimate(flops=work, bytes_accessed=work // 400, transcendentals=0),
        name=name,
    )(*args)


def forward_own(count, scal, q, kvs, ss, ds):
    outs = (((count, 192, TILE), F32), ((count, 8, TILE), F32), ((count, 8, TILE), F32))
    scratch = window_scratch(count) + [
        pltpu.VMEM((4 * count, 8, TILE), F32),
        pltpu.VMEM((3, 64, TILE), F32),
    ]
    return call(fwd_own_kernel, count, "forward_own", (scal, q, *kvs, *ss, ds), outs, scratch, 20 * 10**9, 24)


def forward_prev(count, scal, q, kvs, ss, ds, acc, ml, p):
    outs = (((count, 192, TILE), BF16), ((count, 192, TILE), F32), ((count, 8, TILE), F32))
    scratch = window_scratch(count) + [pltpu.VMEM((3, 64, TILE), F32)]
    args = (scal, q, *kvs, *ss, ds, acc, ml, p)
    return call(fwd_prev_kernel, count, "forward_prev", args, outs, scratch, 8 * 10**9, 24)


def key_outs(count):
    rows = count * TILE
    return (((rows, 384), F32), ((rows, 384), BF16), ((8, rows), F32), ((8, rows), BF16))


def backward_prev(count, scal, q, do, of, lse, p, kvs, ss, ds):
    outs = (((count, 192, TILE), F32), ((count, 8, TILE), F32)) + key_outs(count)
    scratch = window_scratch(count) + grad_scratch(count)
    args = (scal, q, do, of, lse, p, *kvs, *ss, ds)
    return call(bwd_prev_kernel, count, "backward_prev", args, outs, scratch, 12 * 10**9, 32)


def backward_own(count, scal, q, do, of, lse, p, kvs, ss, ds, dq, tau):
    outs = (((192, count * TILE), BF16),) + key_outs(count) + (((8, 128), F32),)
    scratch = window_scratch(count) + grad_scratch(count)
    args = (scal, q, do, of, lse, p, *kvs, *ss, ds, dq, tau)
    return call(bwd_own_kernel, count, "backward_own", args, outs, scratch, 24 * 10**9, 32)


def hidden_kernel(n0, n1, dy0, dy1, bias, down, up, y0, y1, dt0, dt1, g_ref, gb_ref,
                  n_all, dy_all, y_acc, d_acc, n_t, gd, gu, sem):
    step = pl.program_id(0)
    tok = n0.shape[0]

    @pl.when(step == 0)
    def _():
        n_all[:tok, :] = n0[...]
        n_all[tok:, :] = n1[...]
        n_t[:, :tok] = jnp.transpose(n0[...].astype(F32)).astype(BF16)
        n_t[:, tok:] = jnp.transpose(n1[...].astype(F32)).astype(BF16)
        dy_all[:tok, :] = dy0[...]
        dy_all[tok:, :] = dy1[...]
        y_acc[...] = jnp.zeros_like(y_acc)
        d_acc[...] = jnp.zeros_like(d_acc)

    n = n_all[...]
    dy = dy_all[...]
    c0 = math.sqrt(2.0 / math.pi)
    ways, wide = 2, 384
    w_up = [up[:, :, i * wide : (i + 1) * wide].reshape(D, wide) for i in range(ways)]
    w_down = [down[4 * i : 4 * i + 4].reshape(wide, D) for i in range(ways)]
    pres = [dot_nn(n, w_up[i]) + bias[0:1, i * wide : (i + 1) * wide] for i in range(ways)]
    backs = [dot_nt(dy, w_down[i]) for i in range(ways)]
    hiddens, d_ups = [], []
    for i in range(ways):
        pre = pres[i]
        squared = pre * pre
        th = jnp.tanh(c0 * pre * (1.0 + 0.044715 * squared))
        half = 0.5 * (1.0 + th)
        hiddens.append((pre * half).astype(BF16))
        slope = half + 0.5 * pre * (1.0 - th * th) * c0 * (1.0 + 3 * 0.044715 * squared)
        d_ups.append((backs[i] * slope).astype(BF16))
        gb_ref[:, i * wide : (i + 1) * wide] = jnp.broadcast_to(
            jnp.sum(d_ups[i].astype(F32), axis=0, keepdims=True), (8, wide)
        )
    hid, dup = jnp.concatenate(hiddens, axis=1), jnp.concatenate(d_ups, axis=1)
    y_acc[...] += dot_nn(hid, down[...].reshape(-1, D))
    d_acc[...] += dot_nt(dup, up[...].reshape(D, -1))
    g_down = dot_tn(hid, dy).astype(BF16).reshape(8, 96, D)
    g_up = dot_nn(n_t[...], dup).astype(BF16).reshape(16, 48, D)
    for k in range(2):

        @pl.when(step == k)
        def _(k=k):
            gd[k] = g_down
            gu[k] = g_up
            pltpu.make_async_copy(gd.at[k], g_ref.at[8 * k : 8 * k + 8, 0:96, :], sem.at[k]).start()
            pltpu.make_async_copy(
                gu.at[k], g_ref.at[:, 96 + 48 * k : 144 + 48 * k, :], sem.at[2 + k]
            ).start()


    @pl.when(step == pl.num_programs(0) - 1)
    def _():
        y0[...] = y_acc[:tok, :]
        y1[...] = y_acc[tok:, :]
        dt0[...] = d_acc[:tok, :]
        dt1[...] = d_acc[tok:, :].astype(BF16)
        for k in range(2):
            pltpu.make_async_copy(gd.at[k], g_ref.at[8 * k : 8 * k + 8, 0:96, :], sem.at[k]).wait()
            pltpu.make_async_copy(
                gu.at[k], g_ref.at[:, 96 + 48 * k : 144 + 48 * k, :], sem.at[2 + k]
            ).wait()


def hidden_passes(n0, n1, dy0, dy1, bias, packed):
    tok = n0.shape[0]
    whole = pl.BlockSpec((tok, D), lambda i: (0, 0))
    lanes = pl.BlockSpec((8, D), lambda i: (0, i))
    outs = (
        jax.ShapeDtypeStruct((tok, D), F32),
        jax.ShapeDtypeStruct((tok, D), F32),
        jax.ShapeDtypeStruct((tok, D), F32),
        jax.ShapeDtypeStruct((tok, D), BF16),
        jax.ShapeDtypeStruct((16, 216, D), BF16),
        jax.ShapeDtypeStruct((8, FF // 2), F32),
    )
    return pl.pallas_call(
        hidden_kernel,
        grid=(2,),
        out_shape=outs,
        in_specs=[
            whole,
            whole,
            whole,
            whole,
            lanes,
            pl.BlockSpec((8, 96, D), lambda i: (i, 0, 0)),
            pl.BlockSpec((16, 48, D), lambda i: (0, 2 + i, 0)),
        ],
        out_specs=(
            whole,
            whole,
            whole,
            whole,
            pl.BlockSpec(memory_space=pl.ANY),
            lanes,
        ),
        scratch_shapes=[
            pltpu.VMEM((2 * tok, D), BF16),
            pltpu.VMEM((2 * tok, D), BF16),
            pltpu.VMEM((2 * tok, D), F32),
            pltpu.VMEM((2 * tok, D), F32),
            pltpu.VMEM((D, 2 * tok), BF16),
            pltpu.VMEM((2, 8, 96, D), BF16),
            pltpu.VMEM((2, 16, 48, D), BF16),
            pltpu.SemaphoreType.DMA((4,)),
        ],
        compiler_params=pltpu.CompilerParams(vmem_limit_bytes=56 * MIB),
        cost_estimate=pl.CostEstimate(flops=7 * 10**9, bytes_accessed=10**7, transcendentals=0),
        name="hidden_passes",
    )(n0, n1, dy0, dy1, bias, packed, packed)


def project_kernel(count, sc, own, sib, back, dq, s0, s1, s2, scores, cond, carry, x, w,
                   cat_ref, dn0_ref, dn1_ref, dn2_ref, dn3_ref, sums_ref, cols_ref):
    place = (
        lax.broadcasted_iota(jnp.int32, (8, 64), 1)
        == lax.broadcasted_iota(jnp.int32, (8, 64), 0) + 3 * sc[1]
    ).astype(BF16)
    real = lax.broadcasted_iota(jnp.int32, (8, TILE), 0) < 3
    sums_ref[...] = jnp.zeros_like(sums_ref)
    cols_ref[...] = jnp.zeros_like(cols_ref)
    weights = w[...]
    for r in range(count):
        at = slice(r * TILE, (r + 1) * TILE)
        d_kv = own[at, :] + sib[at, :].astype(F32) + back[at, :].astype(F32)
        d_q = jnp.transpose(dq[:, at].astype(F32))
        after = jnp.exp(scores[:, at].astype(F32)) * jnp.sum(carry[...], axis=1, keepdims=True)
        d_s = s0[:, at] + s1[:, at].astype(F32) + s2[:, at].astype(F32)
        d_s = d_s + jnp.where(cond[0:1, at] > 0, after, 0.0)
        d_s = jnp.transpose(jnp.where(real, d_s, 0.0)).astype(BF16)
        d_s = dot_nn(d_s, place)
        cat = jnp.concatenate([d_kv, d_q, d_s], axis=1).astype(BF16)
        cat_ref[at, :] = cat
        d_n = dot_nt(cat, weights)
        if r == 0:
            dn0_ref[...] = d_n
        else:
            (dn1_ref, dn2_ref, dn3_ref)[r - 1][...] = d_n.astype(BF16)
        unit, _ = normalize(x[at, :].astype(F32))
        sums_ref[0:1, :] += jnp.sum(d_n * unit, axis=0, keepdims=True)
        sums_ref[1:2, :] += jnp.sum(d_n, axis=0, keepdims=True)
        cols_ref[0:1, :] += jnp.sum(cat.astype(F32), axis=0, keepdims=True)


def project_back(count, *args):
    rows = count * TILE
    outs = (
        ((rows, 640), BF16),
        ((TILE, D), F32),
        ((TILE, D), BF16),
        ((TILE, D), BF16),
        ((TILE, D), BF16),
        ((8, D), F32),
        ((8, 640), F32),
    )
    return call(project_kernel, count, "project_back", args, outs, [], 10**9, 56)


def other_core(x):
    return lax.ppermute(x, "core", [(0, 1), (1, 0)])


def next_chip(x, step):
    n = lax.axis_size("pair")
    return lax.ppermute(x, "pair", [(i, i + step) for i in range(n) if 0 <= i + step < n])


def spread(x, axes):
    n = lax.axis_size(axes)
    return lax.all_to_all(jnp.broadcast_to(x[None], (n,) + x.shape), axes, 0, 0)


def both_cores(mine, theirs, core, axis):
    return jnp.where(
        core == 0, jnp.stack([mine, theirs], axis), jnp.stack([theirs, mine], axis)
    )


def normalize(rows):
    centred = rows - jnp.mean(rows, axis=-1, keepdims=True)
    scale = lax.rsqrt(jnp.mean(centred * centred, axis=-1, keepdims=True) + EPS)
    return centred * scale, scale


def norm_pull(grad, unit, scale, gain):
    inner = grad * gain
    return scale * (
        inner
        - jnp.mean(inner, axis=-1, keepdims=True)
        - unit * jnp.mean(inner * unit, axis=-1, keepdims=True)
    )


def across(x, r):
    return lax.ppermute(x, "head", [(i, i ^ r) for i in range(lax.axis_size("head"))])


def shards(tokens, segment_ids, gains, biases, w_qkv, w_score, w_out, w_up, w_down, cotangent):
    groups = lax.axis_size("head")
    pairs = lax.axis_size("pair")
    devices = groups * pairs * 2
    same = groups * pairs
    h = lax.axis_index("head")
    p = lax.axis_index("pair")
    c = lax.axis_index("core")
    tok = tokens.shape[0]
    block = groups * tok
    count = groups
    super_rows = 2 * block
    total = super_rows * pairs
    rows_l = D // devices
    down_l = FF // devices
    swaps = (h & 1) == 1

    x_other = other_core(tokens)
    dy_other = other_core(cotangent)
    x_mine = jnp.where(swaps, x_other, tokens)
    x_parts = [x_mine] + [across(x_mine, r) for r in range(1, groups)]

    part = w_qkv.astype(BF16).reshape(rows_l, 3, groups, 3, HDIM)
    part_q = part[:, 0].reshape(rows_l, groups, 192)
    part_kv = part[:, 1:].transpose(0, 2, 3, 1, 4).reshape(rows_l, groups, 384)
    id_lanes = -(-tok // rows_l)
    own_ids = jnp.pad(segment_ids.astype(BF16), (0, id_lanes * rows_l - tok))
    small = jnp.concatenate(
        [
            w_score.astype(BF16).reshape(rows_l, HEADS),
            gains.astype(BF16).reshape(rows_l, 2),
            biases.astype(BF16).reshape(rows_l, 10),
            own_ids.reshape(rows_l, id_lanes),
        ],
        axis=1,
    )
    small = jnp.broadcast_to(small[:, None], (rows_l, groups, small.shape[1]))
    part = jnp.concatenate([part_kv, part_q, small], axis=-1).transpose(1, 0, 2)
    filled = part.shape[2]
    width = -(-filled // 128) * 128
    part = jnp.pad(part, ((0, 0), (0, 0), (0, width - filled)))
    part = jnp.broadcast_to(part[:, None], (groups, pairs, rows_l, width))
    w_same = lax.all_to_all(part.reshape(same, rows_l, width), SAME, 0, 0)
    up_rows = w_up.astype(BF16).reshape(rows_l, same, 2, down_l)
    up_mine = jnp.where(c == 0, up_rows[:, :, 0], up_rows[:, :, 1]).reshape(rows_l, FF // 2)
    up_send = jnp.where(c == 0, up_rows[:, :, 1], up_rows[:, :, 0]).reshape(rows_l, FF // 2)
    up_both = both_cores(up_mine, other_core(up_send), c, 0).reshape(2 * rows_l, FF // 2)
    down_mine = w_down.astype(BF16).reshape(down_l, D)
    out_mine = w_out.astype(BF16).reshape(rows_l, D)
    a, b, e = down_l, down_l + 2 * rows_l, down_l + 4 * rows_l
    pack = jnp.concatenate([down_mine, up_both[:, :D], up_both[:, D:]], axis=0)
    packed = lax.all_gather(pack, "pair", axis=0, tiled=False)
    packed, _ = lax.optimization_barrier((packed, w_same))
    out_mine, _ = lax.optimization_barrier((out_mine, w_same))
    packed = lax.all_gather(packed, "head", axis=0, tiled=False).reshape((same,) + pack.shape)
    out_same = spread(out_mine, SAME)
    tall = down_l
    if tall != 96:
        packed = jnp.concatenate(
            [
                packed[:, :a].reshape(16, 96, D),
                packed[:, a:b].reshape(16, 48, D),
                packed[:, b:e].reshape(16, 48, D),
            ],
            axis=1,
        )

    w_both = both_cores(w_same, other_core(w_same), c, 1).reshape(D, width)
    w_kv, w_q = w_both[:, :384], w_both[:, 384:576]
    gain_rows = w_both[:, 588:590].reshape(2, D).astype(F32)
    bias_rows = w_both[:, 590:600].reshape(10, D).astype(F32)
    ids_all = w_both[:, 600 : 600 + id_lanes].reshape(devices, rows_l * id_lanes)[:, :tok]
    ids_all = ids_all.astype(jnp.int32).reshape(groups, pairs, 2, tok)
    ids_all = ids_all.transpose(1, 2, 0, 3).reshape(total)

    x_low = jnp.concatenate(x_parts, axis=0)
    x_rows = x_low.astype(F32)
    unit_one, scale_one = normalize(x_rows)
    normed = (unit_one * gain_rows[0] + bias_rows[0]).astype(BF16)
    w_s = lax.dynamic_slice_in_dim(w_both[:, 576:588], 3 * h, 3, axis=1)
    w_s = jnp.pad(w_s, ((0, 0), (0, 5)))
    scores = lax.dot_general(
        w_s, normed, (((0,), (1,)), ((), ())), preferred_element_type=F32
    ).astype(BF16)
    s_sib = other_core(scores)
    s_prev = next_chip(jnp.stack([scores, s_sib]), 1)
    bias_v = lax.dynamic_slice_in_dim(bias_rows[2:3], 192 * h, 192, axis=1).reshape(1, 3, 1, HDIM)
    bias_kv = jnp.concatenate([jnp.zeros_like(bias_v), bias_v], axis=2).reshape(1, 384)
    kv = (dot_nn(normed, w_kv) + bias_kv).astype(BF16)
    bias_q = lax.dynamic_slice_in_dim(bias_rows[1:2], 192 * h, 192, axis=1).reshape(192, 1)
    q = lax.dot_general(w_q, normed, (((0,), (1,)), ((), ())), preferred_element_type=F32)
    q = (q + bias_q).astype(BF16)

    padded = jnp.concatenate([jnp.full((super_rows,), -1, jnp.int32), ids_all])
    ids_win = lax.dynamic_slice_in_dim(padded, p * super_rows, 2 * super_rows)
    k_of = h ^ jnp.arange(count)
    tile_of = k_of + count * ((c + k_of) & 1)
    ids_super = ids_win[super_rows:].reshape(1, 2 * count, TILE)
    picked = tile_of[:, None, None] == jnp.arange(2 * count)[None, :, None]
    ids_q = jnp.sum(jnp.where(picked, ids_super, 0), axis=1)
    starts = jnp.sum((ids_win[None, :, None] < ids_q[:, None, :]).astype(jnp.int32), axis=1)
    lows = jnp.min(starts, axis=1) // TILE
    scal = jnp.concatenate([jnp.stack([c, h]), jnp.min(lows)[None], lows]).astype(jnp.int32)
    ds = jnp.broadcast_to(starts[:, None, :], (count, 8, TILE))

    kv, s_prev, out_same, q, ds, scal = lax.optimization_barrier(
        (kv, s_prev, out_same, q, ds, scal)
    )
    m_out = both_cores(out_same, other_core(out_same), c, 1).reshape(D, D)
    kv_prev = next_chip(kv, 1)
    kv_sib = other_core(kv)

    own_kvs, own_ss = (kv, kv_sib), (scores, s_sib)
    prev_ss = (s_prev[0], s_prev[1])
    acc, ml, pr = forward_own(count, scal, q, own_kvs, own_ss + prev_ss, ds)
    dy_mine = jnp.where(swaps, dy_other, cotangent)
    dy_sib = jnp.where(swaps, cotangent, dy_other)
    stripes = bias_rows[5:9].reshape(same, 2, down_l)
    up_half = jnp.where(c == 0, stripes[:, 0], stripes[:, 1]).reshape(1, FF // 2)
    up_half = jnp.broadcast_to(up_half, (8, FF // 2))
    kv_prev, acc, dy_mine, dy_sib, up_half = lax.optimization_barrier(
        (kv_prev, acc, dy_mine, dy_sib, up_half)
    )
    prev_kvs = (kv_prev, other_core(kv_prev))
    o, of, lse = forward_prev(count, scal, q, prev_kvs, prev_ss, ds, acc, ml, pr)

    attn = lax.all_to_all(o, "head", 0, 0).reshape(D, tok)
    middle = x_mine.astype(F32) + dot_tn(attn, m_out) + bias_rows[3]
    unit_two, scale_two = normalize(middle)
    n_two = (unit_two * gain_rows[1] + bias_rows[4]).astype(BF16)
    n_sib = other_core(n_two)
    y0, y1, d_two_0, d_two_1, g_pack, g_up_bias = hidden_passes(
        n_two, n_sib, dy_mine, dy_sib, up_half, packed
    )
    d_two = d_two_0 + other_core(d_two_1).astype(F32)
    y = y0 + other_core(y1)
    result_mine = (middle + y + bias_rows[9]).astype(BF16)
    result = jnp.where(swaps, other_core(result_mine), result_mine)

    g_up_bias = g_up_bias[0]
    g_gain_two = jnp.sum(d_two * unit_two, axis=0)
    g_shift_two = jnp.sum(d_two, axis=0)
    dy_f = dy_mine.astype(F32)
    g_down_bias = jnp.sum(dy_f, axis=0)

    d_middle = dy_f + norm_pull(d_two, unit_two, scale_two, gain_rows[1])
    d_branch = d_middle.astype(BF16)
    g_out_bias = jnp.sum(d_branch.astype(F32), axis=0)
    d_sent = dot_nt(m_out, d_branch).astype(BF16)
    d_branch, d_sent = lax.optimization_barrier((d_branch, d_sent))
    d_heads = lax.all_to_all(d_sent.reshape(groups, 192, tok), "head", 0, 0)
    g_out = dot_nn(attn, d_branch)

    g_out_rows = g_out.reshape(same, 2, rows_l, D)
    g_out_keep = jnp.where(c == 0, g_out_rows[:, 0], g_out_rows[:, 1])
    g_out_send = jnp.where(c == 0, g_out_rows[:, 1], g_out_rows[:, 0]).astype(BF16)
    g_out_same = (g_out_keep + other_core(g_out_send).astype(F32)).astype(BF16)
    if tall == 96:
        g_pack = lax.dynamic_update_slice(g_pack, g_out_same, (0, e, 0))
    else:
        g_parts = [
            g_pack[:, :96].reshape(same, a, D),
            g_pack[:, 96:144].reshape(same, b - a, D),
            g_pack[:, 144:192].reshape(same, e - b, D),
        ]
        g_pack = jnp.concatenate(g_parts + [g_out_same], axis=1)
    g_half = lax.psum_scatter(
        g_pack.reshape(groups, pairs, e + rows_l, D), "head", scatter_dimension=0, tiled=False
    )

    rows = (q, d_heads, of, lse, pr)
    dq_part, tau, prev, to_cross, s_prev_part, s_to_cross = backward_prev(
        count, scal, *rows, prev_kvs, prev_ss, ds
    )
    to_prev = (prev + other_core(to_cross).astype(F32)).astype(BF16)
    to_prev, tau = lax.optimization_barrier((to_prev, tau))
    back = next_chip(to_prev, -1)
    s_back = next_chip((s_prev_part + other_core(s_to_cross).astype(F32)).astype(BF16), -1)
    dq, own, to_sib, s_own, s_to_sib, carry = backward_own(
        count, scal, *rows, own_kvs, own_ss, ds, dq_part, tau
    )
    carry = next_chip(carry + other_core(carry), -1)
    back, s_back, to_sib, s_to_sib = lax.optimization_barrier((back, s_back, to_sib, s_to_sib))
    sib_kv, sib_s = other_core(to_sib), other_core(s_to_sib)

    sib_kv, g_half = lax.optimization_barrier((sib_kv, g_half))

    continued = (ids_q == ids_win[-1]).astype(jnp.int32).reshape(1, block)
    continued = jnp.broadcast_to(continued, (8, block))
    cat, d_norm_sum, *d_norm_low, sums, cols = project_back(
        count, scal, own, sib_kv, back, dq, s_own, sib_s, s_back, scores, continued, carry, x_low, w_both[:, :640]
    )
    cat, d_norm_low = lax.optimization_barrier((cat, d_norm_low))
    for r in range(1, groups):
        d_norm_sum = d_norm_sum + across(d_norm_low[r - 1], r).astype(F32)

    mine = jnp.arange(D) // 192 == h
    g_q_bias = jnp.where(mine, jnp.tile(cols[0, 384:576], groups), 0.0)
    g_v_bias = cols[0, :384].reshape(3, 2, HDIM)[:, 1].reshape(192)
    g_v_bias = jnp.where(mine, jnp.tile(g_v_bias, groups), 0.0)
    halves = jnp.stack([g_up_bias.reshape(same, down_l)] * 2, axis=1)
    halves = jnp.where(jnp.arange(2)[None, :, None] == c, halves, 0.0).reshape(4, D)
    g_bias_rows = jnp.concatenate(
        [
            jnp.stack([sums[1], g_q_bias, g_v_bias, g_out_bias, g_shift_two]),
            halves,
            g_down_bias[None],
        ],
        axis=0,
    )
    small = jnp.concatenate(
        [jnp.stack([sums[0], g_gain_two]).reshape(D, 2), g_bias_rows.reshape(D, 10)], axis=1
    )
    g_all = dot_tn(normed, cat) + jnp.pad(small, ((0, 0), (588, 40)))
    g_all = g_all.astype(BF16)
    came = lax.all_to_all(g_all, ALL, 0, 0, tiled=True)
    g_pack = lax.psum_scatter(g_half, "pair", scatter_dimension=0, tiled=False).astype(F32)
    grad_w_down = g_pack[:a].reshape(-1)
    grad_w_out = g_pack[e:].reshape(-1)
    g_up_rows = jnp.concatenate([g_pack[a:b], g_pack[b:e]], axis=1).reshape(2, rows_l, FF // 2)
    g_up_keep = jnp.where(c == 0, g_up_rows[0], g_up_rows[1])
    g_up_came = other_core(jnp.where(c == 0, g_up_rows[1], g_up_rows[0]))
    grad_w_up = both_cores(
        g_up_keep.reshape(rows_l, same, down_l), g_up_came.reshape(rows_l, same, down_l), c, 2
    ).reshape(-1)
    came, grad_w_down, grad_w_out, grad_w_up = lax.optimization_barrier(
        (came, grad_w_down, grad_w_out, grad_w_up)
    )
    came = came.astype(F32)
    came = jnp.sum(came.reshape(groups, 2 * pairs, rows_l, 640), axis=1)
    grad_kv = came[:, :, :384].reshape(groups, rows_l, 3, 2, HDIM)
    grad_kv = grad_kv.transpose(1, 3, 0, 2, 4).reshape(rows_l, 2, D)
    grad_q = came[:, :, 384:576].transpose(1, 0, 2).reshape(rows_l, 1, D)
    grad_w_qkv = jnp.concatenate([grad_q, grad_kv], axis=1).reshape(-1)
    small_sum = jnp.sum(came[:, :, 576:600], axis=0)
    grad_w_score = small_sum[:, :12].reshape(-1)
    grad_gains = small_sum[:, 12:14].reshape(-1)
    grad_biases = small_sum[:, 14:24].reshape(-1)

    unit_mine, scale_mine = unit_one[:tok], scale_one[:tok]
    grad_mine = d_middle + norm_pull(d_norm_sum, unit_mine, scale_mine, gain_rows[0])
    grad_mine = grad_mine.astype(BF16)
    grad_tokens = jnp.where(swaps, other_core(grad_mine), grad_mine)
    return (
        result,
        grad_tokens,
        grad_gains,
        grad_biases,
        grad_w_qkv,
        grad_w_score,
        grad_w_out,
        grad_w_up,
        grad_w_down,
    )


def solution(mesh):
    groups = mesh.devices.shape[0]
    fine = Mesh(mesh.devices.reshape(groups, -1, 2), ALL)
    rows = P(("pair", "core", "head"), None)
    flat = P(ALL)
    in_specs = (rows, P(("pair", "core", "head"))) + (flat,) * 7 + (rows,)
    out_specs = (rows, rows) + (flat,) * 7
    return jax.shard_map(shards, mesh=fine, in_specs=in_specs, out_specs=out_specs, check_vma=False)
```

```python
import functools
import math

import jax
import jax.numpy as jnp
from jax import lax
from jax.experimental import pallas as pl
from jax.experimental.pallas import tpu as pltpu
from jax.sharding import Mesh
from jax.sharding import PartitionSpec as P

D = 768
HEADS = 12
HDIM = 64
FF = 3072
WINDOW = 64
KEEP = 64
MOST = 2000

EPS = 1e-05
NEGATIVE = -1e30
TINY = 1e-37
TILE = 256
ROOT = 1.0 / math.sqrt(HDIM)
F32 = jnp.float32
BF16 = jnp.bfloat16
ALL = ("head", "pair", "core")
SAME = ("head", "pair")


def dot_nn(a, b):
    return lax.dot_general(a, b, (((1,), (0,)), ((), ())), preferred_element_type=F32)


def dot_nt(a, b):
    return lax.dot_general(a, b, (((1,), (1,)), ((), ())), preferred_element_type=F32)


def dot_tn(a, b):
    return lax.dot_general(a, b, (((0,), (0,)), ((), ())), preferred_element_type=F32)


def tile_place(sc, r, rel, count):
    k = sc[1] ^ r
    return k + count * ((sc[0] + rel + k) & 1)


def fill_window(sc, count, base, kv_refs, s_refs, kvw, kvt, ew):
    eye = (
        lax.broadcasted_iota(jnp.int32, (128, 128), 0)
        == lax.broadcasted_iota(jnp.int32, (128, 128), 1)
    ).astype(BF16)
    for rel in range(2):
        for r in range(count):
            place = tile_place(sc, r, rel, count)

            @pl.when(base + place >= sc[2])
            def _(rel=rel, r=r, place=place):
                block = kv_refs[rel][r * TILE : (r + 1) * TILE, :]
                kvw[place] = block
                rows = s_refs[rel][:, r * TILE : (r + 1) * TILE]
                for h in range(3):
                    kvt[place, h * 128 : (h + 1) * 128, :] = dot_nt(
                        eye, block[:, h * 128 : (h + 1) * 128]
                    ).astype(BF16)
                    pick = (lax.broadcasted_iota(jnp.int32, (8, 128), 0) == h).astype(BF16)
                    ew[place * 3 + h] = jnp.exp(dot_tn(rows, pick))


def twice(x):
    return jnp.concatenate([x, x], axis=1)


def key_iota():
    return lax.broadcasted_iota(jnp.int32, (TILE, TILE), 0)


def query_iota():
    return lax.broadcasted_iota(jnp.int32, (1, TILE), 1)


def column(r):
    return pl.ds(pl.multiple_of(r * TILE, TILE), TILE)


def padded_queries(q_ref, r):
    zero = jnp.zeros((64, TILE), BF16)
    q_all = q_ref[:, column(r)] * BF16(ROOT)
    return [
        jnp.concatenate([q_all[64 * h : 64 * h + 64, :], zero], axis=0) for h in range(3)
    ]


def chunk_masks(ds_row, place, j, edge):
    k_io = key_iota()
    mask = k_io >= ds_row - j * TILE
    near = None
    if edge:
        ahead = query_iota() + (place - j) * TILE
        mask = mask & (k_io <= ahead)
        near = k_io > ahead - WINDOW
    return mask, near


def fwd_chunk(state, j, slot, edge, place, ds_row, q_pad, p_rows, kvw, kvt, ew, acc):
    mask, near = chunk_masks(ds_row, place, j, edge)
    zs = [dot_nn(kvw[slot, :, h * 128 : (h + 1) * 128], q_pad[h]) for h in range(3)]
    out, probs, alphas = [], [], []
    for h in range(3):
        m_old, l_old = state[2 * h], state[2 * h + 1]
        z = jnp.where(mask, zs[h], NEGATIVE)
        m_new = jnp.maximum(m_old, jnp.max(z, axis=0, keepdims=True))
        e = twice(ew[slot * 3 + h])
        sig = e / (e + p_rows[h])
        if edge:
            sig = jnp.where(near, 1.0, sig)
        prob = jnp.exp(z - m_new) * sig
        alphas.append(jnp.exp(m_old - m_new))
        out += [m_new, l_old * alphas[h] + jnp.sum(prob, axis=0, keepdims=True)]
        probs.append(prob.astype(BF16))
    for h in range(3):
        acc[h] = acc[h] * alphas[h] + dot_nn(kvt[slot, h * 128 + 64 : (h + 1) * 128, :], probs[h])
    return tuple(out)


def fwd_own_kernel(count, sc, q_ref, kv0, kv1, s0, s1, s2, s3, ds_ref, acc_ref, ml_ref, p_ref,
                   kvw, kvt, ew, er, acc):
    base = 2 * count
    fill_window(sc, count, base, (kv0, kv1), (s0, s1), kvw, kvt, ew)
    for part, refs in enumerate(((s2, s3), (s0, s1))):
        for rel in range(2):
            for r in range(count):
                place = part * base + tile_place(sc, r, rel, count)
                er[place] = jnp.exp(refs[rel][:, r * TILE : (r + 1) * TILE].astype(F32))

    def one_tile(r, unused):
        place = base + tile_place(sc, r, 0, count)
        low = sc[3 + r]
        ds_row = ds_ref[r][0:1, :]
        tile_start = place * TILE
        q_pad = padded_queries(q_ref, r)
        k_io = key_iota()
        inside = (k_io >= ds_row - tile_start) & (k_io <= query_iota())
        ds_first = jnp.min(ds_row, axis=1, keepdims=True)
        lane = lax.broadcasted_iota(jnp.int32, (8, TILE), 1)

        def carry_step(j, sums):
            return sums + jnp.where(lane >= ds_first - j * TILE, er[j], 0.0)

        carried = lax.fori_loop(low, place, carry_step, jnp.zeros((8, TILE), F32))
        carried = jnp.sum(carried, axis=1, keepdims=True)
        starts_before = ds_row < tile_start
        p_rows = []
        for h in range(3):
            local = jnp.sum(
                jnp.where(inside, twice(ew[(place - base) * 3 + h]), 0.0), axis=0, keepdims=True
            )
            prefix = local + jnp.where(starts_before, carried[h : h + 1, :], 0.0)
            p_rows.append(jnp.maximum(prefix * (1.0 / KEEP), TINY))
        acc[...] = jnp.zeros_like(acc)

        def chunk(j, state, edge):
            return fwd_chunk(
                state, j, j - base, edge, place, ds_row, q_pad, p_rows, kvw, kvt, ew, acc
            )

        state = (jnp.full((1, TILE), NEGATIVE, F32), jnp.zeros((1, TILE), F32)) * 3
        low = jnp.maximum(low, base)
        edge_low = jnp.maximum(place - 1, low)
        state = lax.fori_loop(low, edge_low, lambda j, s: chunk(j, s, False), state)
        state = lax.fori_loop(edge_low, place + 1, lambda j, s: chunk(j, s, True), state)
        zero = jnp.zeros((2, TILE), F32)
        acc_ref[r] = jnp.concatenate([acc[0], acc[1], acc[2]], axis=0)
        ml_ref[r] = jnp.concatenate(list(state[0::2]) + list(state[1::2]) + [zero], axis=0)
        p_ref[r] = jnp.concatenate(p_rows + p_rows + [zero], axis=0)
        return unused

    lax.fori_loop(0, count, one_tile, 0)


def fwd_prev_kernel(count, sc, q_ref, kv0, kv1, s0, s1, ds_ref, acc_ref, ml_ref, p_ref,
                    o_ref, of_ref, lse_ref, kvw, kvt, ew, acc):
    base = 2 * count
    fill_window(sc, count, 0, (kv0, kv1), (s0, s1), kvw, kvt, ew)

    def one_tile(r, unused):
        place = base + tile_place(sc, r, 0, count)
        low = sc[3 + r]
        ds_row = ds_ref[r][0:1, :]
        q_pad = padded_queries(q_ref, r)
        ml = ml_ref[r]
        p_all = p_ref[r]
        p_rows = [p_all[h : h + 1, :] for h in range(3)]
        before = acc_ref[r]
        for h in range(3):
            acc[h] = before[64 * h : 64 * h + 64, :]

        def chunk(j, state, edge):
            return fwd_chunk(state, j, j, edge, place, ds_row, q_pad, p_rows, kvw, kvt, ew, acc)

        state = ()
        for h in range(3):
            state += (ml[h : h + 1, :], ml[3 + h : 4 + h, :])
        edge_low = jnp.maximum(place - 1, low)
        state = lax.fori_loop(
            low, jnp.minimum(edge_low, base), lambda j, s: chunk(j, s, False), state
        )
        state = lax.fori_loop(edge_low, base, lambda j, s: chunk(j, s, True), state)
        stacked = jnp.concatenate([acc[h] / state[2 * h + 1] for h in range(3)], axis=0)
        of_ref[r] = stacked
        o_ref[sc[1] ^ r] = stacked.astype(BF16)
        lse = [state[2 * h] + jnp.log(state[2 * h + 1]) for h in range(3)]
        lse_ref[r] = jnp.concatenate(lse + lse + [jnp.zeros((2, TILE), F32)], axis=0)
        return unused

    lax.fori_loop(0, count, one_tile, 0)


def bwd_chunk(state, j, slot, edge, place, ds_row, q_pad, do_pad, both, lse, p_rows, delta,
              kvw, kvt, ew, dkv, dsl, dqt):
    mask, near = chunk_masks(ds_row, place, j, edge)
    kv = [kvw[slot, :, h * 128 : (h + 1) * 128] for h in range(3)]
    zds = [dot_nn(kv[h], both[h]) for h in range(3)]
    zs = [zd[:, :TILE] for zd in zds]
    dps = [zd[:, TILE:] for zd in zds]
    out, lows, pairs, fars = [], [], [], []
    for h in range(3):
        e = twice(ew[slot * 3 + h])
        r = 1.0 / (e + p_rows[h])
        sig = e * r
        if edge:
            sig = jnp.where(near, 1.0, sig)
        prob = jnp.exp(jnp.where(mask, zs[h] - lse[h], NEGATIVE)) * sig
        dz = prob * (dps[h] - delta[h])
        far = dz * (p_rows[h] * r)
        if edge:
            far = jnp.where(near, 0.0, far)
        out.append(state[h] - jnp.sum(far, axis=0, keepdims=True))
        fars.append(far[:, :128] + far[:, 128:])
        lows.append(dz.astype(BF16))
        pairs.append(jnp.concatenate([lows[h], prob.astype(BF16)], axis=1))
    grads = [dot_nt(pairs[h], both[h]) for h in range(3)]
    for h in range(3):
        dqt[h] += dot_nn(kvt[slot, h * 128 : h * 128 + 64, :], lows[h])
    dkv[slot] += jnp.concatenate(grads, axis=1)
    for h in range(3):
        dsl[slot * 3 + h] += fars[h]
    return tuple(out)


def bwd_rows(r, sc, q_ref, do_ref, of_ref, lse_ref, p_ref):
    q_pad = padded_queries(q_ref, r)
    do_all = do_ref[sc[1] ^ r]
    lse_all, p_all, of = lse_ref[r], p_ref[r], of_ref[r]
    zero = jnp.zeros((64, TILE), BF16)
    do_pad, both, lse, p_rows, delta = [], [], [], [], []
    for h in range(3):
        dh = do_all[64 * h : 64 * h + 64, :]
        do_pad.append(jnp.concatenate([zero, dh], axis=0))
        both.append(jnp.concatenate([q_pad[h], do_pad[h]], axis=1))
        lse.append(lse_all[h : h + 1, :])
        p_rows.append(p_all[h : h + 1, :])
        delta.append(
            jnp.sum(dh.astype(F32) * of[64 * h : 64 * h + 64, :], axis=0, keepdims=True)
        )
    return q_pad, do_pad, both, lse, p_rows, delta


def write_keys(sc, count, dkv, dsl, outs):
    for rel in range(2):
        big, small = outs[rel]
        for r in range(count):
            place = tile_place(sc, r, rel, count)
            big[r * TILE : (r + 1) * TILE, :] = dkv[place].astype(big.dtype)
            rows = []
            for h in range(3):
                summed = jnp.sum(dsl[place * 3 + h], axis=1, keepdims=True)
                rows.append(jnp.transpose(jnp.broadcast_to(summed, (TILE, 128)))[0:1, :])
            rows = jnp.concatenate(rows + [jnp.zeros((5, TILE), F32)], axis=0)
            small[:, r * TILE : (r + 1) * TILE] = rows.astype(small.dtype)


def bwd_prev_kernel(count, sc, q_ref, do_ref, of_ref, lse_ref, p_ref, kv0, kv1, s0, s1, ds_ref,
                    dq_ref, tau_ref, big0, big1, small0, small1, kvw, kvt, ew, dkv, dsl, dqt):
    base = 2 * count
    fill_window(sc, count, 0, (kv0, kv1), (s0, s1), kvw, kvt, ew)
    dkv[...] = jnp.zeros_like(dkv)
    dsl[...] = jnp.zeros_like(dsl)

    def one_tile(r, unused):
        place = base + tile_place(sc, r, 0, count)
        low = sc[3 + r]
        ds_row = ds_ref[r][0:1, :]
        dqt[...] = jnp.zeros_like(dqt)

        @pl.when(low >= base)
        def _():
            tau_ref[r] = jnp.zeros((8, TILE), F32)

        @pl.when(low < base)
        def _():
            rows = bwd_rows(r, sc, q_ref, do_ref, of_ref, lse_ref, p_ref)

            def chunk(j, state, edge):
                return bwd_chunk(
                    state, j, j, edge, place, ds_row, *rows, kvw, kvt, ew, dkv, dsl, dqt
                )

            state = (jnp.zeros((1, TILE), F32),) * 3
            edge_low = jnp.maximum(place - 1, low)
            state = lax.fori_loop(
                low, jnp.minimum(edge_low, base), lambda j, s: chunk(j, s, False), state
            )
            state = lax.fori_loop(edge_low, base, lambda j, s: chunk(j, s, True), state)
            tau_ref[r] = jnp.concatenate(list(state) + [jnp.zeros((5, TILE), F32)], axis=0)

        dq_ref[r] = jnp.concatenate([dqt[0], dqt[1], dqt[2]], axis=0)
        return unused

    lax.fori_loop(0, count, one_tile, 0)
    write_keys(sc, count, dkv, dsl, ((big0, small0), (big1, small1)))


def bwd_own_kernel(count, sc, q_ref, do_ref, of_ref, lse_ref, p_ref, kv0, kv1, s0, s1, ds_ref,
                   dqp_ref, tau_ref, dq_ref, big0, big1, small0, small1, carry_ref,
                   kvw, kvt, ew, dkv, dsl, dqt):
    base = 2 * count
    fill_window(sc, count, base, (kv0, kv1), (s0, s1), kvw, kvt, ew)
    dkv[...] = jnp.zeros_like(dkv)
    dsl[...] = jnp.zeros_like(dsl)
    carry_ref[...] = jnp.zeros_like(carry_ref)

    def one_tile(r, unused):
        place = base + tile_place(sc, r, 0, count)
        low = sc[3 + r]
        ds_row = ds_ref[r][0:1, :]
        tile_start = place * TILE
        rows = bwd_rows(r, sc, q_ref, do_ref, of_ref, lse_ref, p_ref)
        p_rows = rows[4]
        before = dqp_ref[r]
        for h in range(3):
            dqt[h] = before[64 * h : 64 * h + 64, :]

        def chunk(j, state, edge):
            return bwd_chunk(
                state, j, j - base, edge, place, ds_row, *rows, kvw, kvt, ew, dkv, dsl, dqt
            )

        tau = tau_ref[r]
        state = tuple(tau[h : h + 1, :] for h in range(3))
        low = jnp.maximum(low, base)
        edge_low = jnp.maximum(place - 1, low)
        state = lax.fori_loop(low, edge_low, lambda j, s: chunk(j, s, False), state)
        state = lax.fori_loop(edge_low, place + 1, lambda j, s: chunk(j, s, True), state)
        dq_ref[:, column(r)] = (
            jnp.concatenate([dqt[0], dqt[1], dqt[2]], axis=0) * ROOT
        ).astype(BF16)

        k_io = key_iota()
        inside = (k_io >= ds_row - tile_start) & (k_io <= query_iota())
        ds_first = jnp.min(ds_row, axis=1, keepdims=True)
        slot = place - base
        w_lane = []
        for h in range(3):
            w = state[h] / (p_rows[h] * float(KEEP))
            earlier = jnp.where(ds_row < tile_start, w, 0.0)
            w_lane.append(earlier[:, :128] + earlier[:, 128:])
            here = jnp.where(inside, w, 0.0)
            dsl[slot * 3 + h] += ew[slot * 3 + h] * (here[:, :128] + here[:, 128:])
            further = jnp.where(ds_row < base * TILE, w, 0.0)
            carry_ref[h : h + 1, :] += further[:, :128] + further[:, 128:]

        def later(j, unused):
            keep = lax.broadcasted_iota(jnp.int32, (TILE, 128), 0) >= ds_first - j * TILE
            for h in range(3):
                dsl[(j - base) * 3 + h] += jnp.where(keep, ew[(j - base) * 3 + h] * w_lane[h], 0.0)
            return unused

        lax.fori_loop(low, place, later, 0)
        return unused

    lax.fori_loop(0, count, one_tile, 0)
    write_keys(sc, count, dkv, dsl, ((big0, small0), (big1, small1)))


VM = pl.BlockSpec(memory_space=pltpu.VMEM)
SM = pl.BlockSpec(memory_space=pltpu.SMEM)
MIB = 1024 * 1024


def window_scratch(count):
    return [
        pltpu.VMEM((2 * count, TILE, 384), BF16),
        pltpu.VMEM((2 * count, 384, TILE), BF16),
        pltpu.VMEM((2 * count * 3, TILE, 128), F32),
    ]


def grad_scratch(count):
    return [
        pltpu.VMEM((2 * count, TILE, 384), F32),
        pltpu.VMEM((2 * count * 3, TILE, 128), F32),
        pltpu.VMEM((3, 64, TILE), F32),
    ]


def call(body, count, name, args, outs, scratch, work, room):
    return pl.pallas_call(
        functools.partial(body, count),
        out_shape=tuple(jax.ShapeDtypeStruct(s, t) for s, t in outs),
        in_specs=[SM] + [VM] * (len(args) - 1),
        out_specs=(VM,) * len(outs),
        scratch_shapes=scratch,
        compiler_params=pltpu.CompilerParams(vmem_limit_bytes=room * MIB),
        cost_estimate=pl.CostEstimate(flops=work, bytes_accessed=work // 400, transcendentals=0),
        name=name,
    )(*args)


def forward_own(count, scal, q, kvs, ss, ds):
    outs = (((count, 192, TILE), F32), ((count, 8, TILE), F32), ((count, 8, TILE), F32))
    scratch = window_scratch(count) + [
        pltpu.VMEM((4 * count, 8, TILE), F32),
        pltpu.VMEM((3, 64, TILE), F32),
    ]
    return call(fwd_own_kernel, count, "forward_own", (scal, q, *kvs, *ss, ds), outs, scratch, 20 * 10**9, 24)


def forward_prev(count, scal, q, kvs, ss, ds, acc, ml, p):
    outs = (((count, 192, TILE), BF16), ((count, 192, TILE), F32), ((count, 8, TILE), F32))
    scratch = window_scratch(count) + [pltpu.VMEM((3, 64, TILE), F32)]
    args = (scal, q, *kvs, *ss, ds, acc, ml, p)
    return call(fwd_prev_kernel, count, "forward_prev", args, outs, scratch, 8 * 10**9, 24)


def key_outs(count):
    rows = count * TILE
    return (((rows, 384), F32), ((rows, 384), BF16), ((8, rows), F32), ((8, rows), BF16))


def backward_prev(count, scal, q, do, of, lse, p, kvs, ss, ds):
    outs = (((count, 192, TILE), F32), ((count, 8, TILE), F32)) + key_outs(count)
    scratch = window_scratch(count) + grad_scratch(count)
    args = (scal, q, do, of, lse, p, *kvs, *ss, ds)
    return call(bwd_prev_kernel, count, "backward_prev", args, outs, scratch, 12 * 10**9, 32)


def backward_own(count, scal, q, do, of, lse, p, kvs, ss, ds, dq, tau):
    outs = (((192, count * TILE), BF16),) + key_outs(count) + (((8, 128), F32),)
    scratch = window_scratch(count) + grad_scratch(count)
    args = (scal, q, do, of, lse, p, *kvs, *ss, ds, dq, tau)
    return call(bwd_own_kernel, count, "backward_own", args, outs, scratch, 24 * 10**9, 32)


def hidden_kernel(n0, n1, dy0, dy1, bias, down, up, y0, y1, dt0, dt1, g_ref, gb_ref,
                  n_all, dy_all, y_acc, d_acc, n_t, gd, gu, sem):
    step = pl.program_id(0)
    tok = n0.shape[0]

    @pl.when(step == 0)
    def _():
        n_all[:tok, :] = n0[...]
        n_all[tok:, :] = n1[...]
        n_t[:, :tok] = jnp.transpose(n0[...].astype(F32)).astype(BF16)
        n_t[:, tok:] = jnp.transpose(n1[...].astype(F32)).astype(BF16)
        dy_all[:tok, :] = dy0[...]
        dy_all[tok:, :] = dy1[...]
        y_acc[...] = jnp.zeros_like(y_acc)
        d_acc[...] = jnp.zeros_like(d_acc)

    n = n_all[...]
    dy = dy_all[...]
    c0 = math.sqrt(2.0 / math.pi)
    ways, wide = 2, 384
    w_up = [up[:, :, i * wide : (i + 1) * wide].reshape(D, wide) for i in range(ways)]
    w_down = [down[4 * i : 4 * i + 4].reshape(wide, D) for i in range(ways)]
    pres = [dot_nn(n, w_up[i]) + bias[0:1, i * wide : (i + 1) * wide] for i in range(ways)]
    backs = [dot_nt(dy, w_down[i]) for i in range(ways)]
    hiddens, d_ups = [], []
    for i in range(ways):
        pre = pres[i]
        squared = pre * pre
        th = jnp.tanh(c0 * pre * (1.0 + 0.044715 * squared))
        half = 0.5 * (1.0 + th)
        hiddens.append((pre * half).astype(BF16))
        slope = half + 0.5 * pre * (1.0 - th * th) * c0 * (1.0 + 3 * 0.044715 * squared)
        d_ups.append((backs[i] * slope).astype(BF16))
        gb_ref[:, i * wide : (i + 1) * wide] = jnp.broadcast_to(
            jnp.sum(d_ups[i].astype(F32), axis=0, keepdims=True), (8, wide)
        )
    hid, dup = jnp.concatenate(hiddens, axis=1), jnp.concatenate(d_ups, axis=1)
    y_acc[...] += dot_nn(hid, down[...].reshape(-1, D))
    d_acc[...] += dot_nt(dup, up[...].reshape(D, -1))
    g_down = dot_tn(hid, dy).astype(BF16).reshape(8, 96, D)
    g_up = dot_nn(n_t[...], dup).astype(BF16).reshape(16, 48, D)
    for k in range(2):

        @pl.when(step == k)
        def _(k=k):
            gd[k] = g_down
            gu[k] = g_up
            pltpu.make_async_copy(gd.at[k], g_ref.at[8 * k : 8 * k + 8, 0:96, :], sem.at[k]).start()
            pltpu.make_async_copy(
                gu.at[k], g_ref.at[:, 96 + 48 * k : 144 + 48 * k, :], sem.at[2 + k]
            ).start()


    @pl.when(step == pl.num_programs(0) - 1)
    def _():
        y0[...] = y_acc[:tok, :]
        y1[...] = y_acc[tok:, :]
        dt0[...] = d_acc[:tok, :]
        dt1[...] = d_acc[tok:, :].astype(BF16)
        for k in range(2):
            pltpu.make_async_copy(gd.at[k], g_ref.at[8 * k : 8 * k + 8, 0:96, :], sem.at[k]).wait()
            pltpu.make_async_copy(
                gu.at[k], g_ref.at[:, 96 + 48 * k : 144 + 48 * k, :], sem.at[2 + k]
            ).wait()


def hidden_passes(n0, n1, dy0, dy1, bias, packed):
    tok = n0.shape[0]
    whole = pl.BlockSpec((tok, D), lambda i: (0, 0))
    lanes = pl.BlockSpec((8, D), lambda i: (0, i))
    outs = (
        jax.ShapeDtypeStruct((tok, D), F32),
        jax.ShapeDtypeStruct((tok, D), F32),
        jax.ShapeDtypeStruct((tok, D), F32),
        jax.ShapeDtypeStruct((tok, D), BF16),
        jax.ShapeDtypeStruct((16, 216, D), BF16),
        jax.ShapeDtypeStruct((8, FF // 2), F32),
    )
    return pl.pallas_call(
        hidden_kernel,
        grid=(2,),
        out_shape=outs,
        in_specs=[
            whole,
            whole,
            whole,
            whole,
            lanes,
            pl.BlockSpec((8, 96, D), lambda i: (i, 0, 0)),
            pl.BlockSpec((16, 48, D), lambda i: (0, 2 + i, 0)),
        ],
        out_specs=(
            whole,
            whole,
            whole,
            whole,
            pl.BlockSpec(memory_space=pl.ANY),
            lanes,
        ),
        scratch_shapes=[
            pltpu.VMEM((2 * tok, D), BF16),
            pltpu.VMEM((2 * tok, D), BF16),
            pltpu.VMEM((2 * tok, D), F32),
            pltpu.VMEM((2 * tok, D), F32),
            pltpu.VMEM((D, 2 * tok), BF16),
            pltpu.VMEM((2, 8, 96, D), BF16),
            pltpu.VMEM((2, 16, 48, D), BF16),
            pltpu.SemaphoreType.DMA((4,)),
        ],
        compiler_params=pltpu.CompilerParams(vmem_limit_bytes=50 * MIB),
        cost_estimate=pl.CostEstimate(flops=7 * 10**9, bytes_accessed=10**7, transcendentals=0),
        name="hidden_passes",
    )(n0, n1, dy0, dy1, bias, packed, packed)


def project_kernel(count, sc, own, sib, back, dq, s0, s1, s2, scores, cond, carry, x, w,
                   cat_ref, dn0_ref, dn1_ref, dn2_ref, dn3_ref, sums_ref, cols_ref):
    place = (
        lax.broadcasted_iota(jnp.int32, (8, 64), 1)
        == lax.broadcasted_iota(jnp.int32, (8, 64), 0) + 3 * sc[1]
    ).astype(BF16)
    real = lax.broadcasted_iota(jnp.int32, (8, TILE), 0) < 3
    sums_ref[...] = jnp.zeros_like(sums_ref)
    cols_ref[...] = jnp.zeros_like(cols_ref)
    weights = w[...]
    for r in range(count):
        at = slice(r * TILE, (r + 1) * TILE)
        d_kv = own[at, :] + sib[at, :].astype(F32) + back[at, :].astype(F32)
        d_q = jnp.transpose(dq[:, at].astype(F32))
        after = jnp.exp(scores[:, at].astype(F32)) * jnp.sum(carry[...], axis=1, keepdims=True)
        d_s = s0[:, at] + s1[:, at].astype(F32) + s2[:, at].astype(F32)
        d_s = d_s + jnp.where(cond[0:1, at] > 0, after, 0.0)
        d_s = jnp.transpose(jnp.where(real, d_s, 0.0)).astype(BF16)
        d_s = dot_nn(d_s, place)
        cat = jnp.concatenate([d_kv, d_q, d_s], axis=1).astype(BF16)
        cat_ref[at, :] = cat
        d_n = dot_nt(cat, weights)
        if r == 0:
            dn0_ref[...] = d_n
        else:
            (dn1_ref, dn2_ref, dn3_ref)[r - 1][...] = d_n.astype(BF16)
        unit, _ = normalize(x[at, :].astype(F32))
        sums_ref[0:1, :] += jnp.sum(d_n * unit, axis=0, keepdims=True)
        sums_ref[1:2, :] += jnp.sum(d_n, axis=0, keepdims=True)
        cols_ref[0:1, :] += jnp.sum(cat.astype(F32), axis=0, keepdims=True)


def project_back(count, *args):
    rows = count * TILE
    outs = (
        ((rows, 640), BF16),
        ((TILE, D), F32),
        ((TILE, D), BF16),
        ((TILE, D), BF16),
        ((TILE, D), BF16),
        ((8, D), F32),
        ((8, 640), F32),
    )
    return call(project_kernel, count, "project_back", args, outs, [], 10**9, 50)


def other_core(x):
    return lax.ppermute(x, "core", [(0, 1), (1, 0)])


def next_chip(x, step):
    n = lax.axis_size("pair")
    return lax.ppermute(x, "pair", [(i, i + step) for i in range(n) if 0 <= i + step < n])


def spread(x, axes):
    n = lax.axis_size(axes)
    return lax.all_to_all(jnp.broadcast_to(x[None], (n,) + x.shape), axes, 0, 0)


def both_cores(mine, theirs, core, axis):
    return jnp.where(
        core == 0, jnp.stack([mine, theirs], axis), jnp.stack([theirs, mine], axis)
    )


def normalize(rows):
    centred = rows - jnp.mean(rows, axis=-1, keepdims=True)
    scale = lax.rsqrt(jnp.mean(centred * centred, axis=-1, keepdims=True) + EPS)
    return centred * scale, scale


def norm_pull(grad, unit, scale, gain):
    inner = grad * gain
    return scale * (
        inner
        - jnp.mean(inner, axis=-1, keepdims=True)
        - unit * jnp.mean(inner * unit, axis=-1, keepdims=True)
    )


def across(x, r):
    return lax.ppermute(x, "head", [(i, i ^ r) for i in range(lax.axis_size("head"))])


def shards(tokens, segment_ids, gains, biases, w_qkv, w_score, w_out, w_up, w_down, cotangent):
    groups = lax.axis_size("head")
    pairs = lax.axis_size("pair")
    devices = groups * pairs * 2
    same = groups * pairs
    h = lax.axis_index("head")
    p = lax.axis_index("pair")
    c = lax.axis_index("core")
    tok = tokens.shape[0]
    block = groups * tok
    count = groups
    super_rows = 2 * block
    total = super_rows * pairs
    rows_l = D // devices
    down_l = FF // devices
    swaps = (h & 1) == 1

    x_other = other_core(tokens)
    dy_other = other_core(cotangent)
    x_mine = jnp.where(swaps, x_other, tokens)
    x_parts = [x_mine] + [across(x_mine, r) for r in range(1, groups)]

    part = w_qkv.astype(BF16).reshape(rows_l, 3, groups, 3, HDIM)
    part_q = part[:, 0].reshape(rows_l, groups, 192)
    part_kv = part[:, 1:].transpose(0, 2, 3, 1, 4).reshape(rows_l, groups, 384)
    id_lanes = -(-tok // rows_l)
    own_ids = jnp.pad(segment_ids.astype(BF16), (0, id_lanes * rows_l - tok))
    small = jnp.concatenate(
        [
            w_score.astype(BF16).reshape(rows_l, HEADS),
            gains.astype(BF16).reshape(rows_l, 2),
            biases.astype(BF16).reshape(rows_l, 10),
            own_ids.reshape(rows_l, id_lanes),
        ],
        axis=1,
    )
    small = jnp.broadcast_to(small[:, None], (rows_l, groups, small.shape[1]))
    part = jnp.concatenate([part_kv, part_q, small], axis=-1).transpose(1, 0, 2)
    filled = part.shape[2]
    width = -(-filled // 128) * 128
    part = jnp.pad(part, ((0, 0), (0, 0), (0, width - filled)))
    part = jnp.broadcast_to(part[:, None], (groups, pairs, rows_l, width))
    w_same = lax.all_to_all(part.reshape(same, rows_l, width), SAME, 0, 0)
    up_rows = w_up.astype(BF16).reshape(rows_l, same, 2, down_l)
    up_mine = jnp.where(c == 0, up_rows[:, :, 0], up_rows[:, :, 1]).reshape(rows_l, FF // 2)
    up_send = jnp.where(c == 0, up_rows[:, :, 1], up_rows[:, :, 0]).reshape(rows_l, FF // 2)
    up_both = both_cores(up_mine, other_core(up_send), c, 0).reshape(2 * rows_l, FF // 2)
    down_mine = w_down.astype(BF16).reshape(down_l, D)
    out_mine = w_out.astype(BF16).reshape(rows_l, D)
    a, b, e = down_l, down_l + 2 * rows_l, down_l + 4 * rows_l
    pack = jnp.concatenate([down_mine, up_both[:, :D], up_both[:, D:]], axis=0)
    packed = lax.all_gather(pack, "pair", axis=0, tiled=False)
    packed, _ = lax.optimization_barrier((packed, w_same))
    out_mine, _ = lax.optimization_barrier((out_mine, w_same))
    packed = lax.all_gather(packed, "head", axis=0, tiled=False).reshape((same,) + pack.shape)
    out_same = spread(out_mine, SAME)
    tall = down_l
    if tall != 96:
        packed = jnp.concatenate(
            [
                packed[:, :a].reshape(16, 96, D),
                packed[:, a:b].reshape(16, 48, D),
                packed[:, b:e].reshape(16, 48, D),
            ],
            axis=1,
        )

    w_sib = other_core(w_same)
    w_both = both_cores(w_same, w_sib, c, 1).reshape(D, width)
    w_tail = both_cores(w_same[:, :, 576:], w_sib[:, :, 576:], c, 1).reshape(D, width - 576)
    w_kv, w_q = w_both[:, :384], w_both[:, 384:576]
    gain_rows = w_tail[:, 12:14].reshape(2, D).astype(F32)
    bias_rows = w_tail[:, 14:24].reshape(10, D).astype(F32)
    ids_all = w_tail[:, 24 : 24 + id_lanes].reshape(devices, rows_l * id_lanes)[:, :tok]
    ids_all = ids_all.astype(jnp.int32).reshape(groups, pairs, 2, tok)
    ids_all = ids_all.transpose(1, 2, 0, 3).reshape(total)

    x_low = jnp.concatenate(x_parts, axis=0)
    x_rows = x_low.astype(F32)
    unit_one, scale_one = normalize(x_rows)
    normed = (unit_one * gain_rows[0] + bias_rows[0]).astype(BF16)
    w_s = lax.dynamic_slice_in_dim(w_tail[:, :12], 3 * h, 3, axis=1)
    w_s = jnp.pad(w_s, ((0, 0), (0, 5)))
    scores = lax.dot_general(
        w_s, normed, (((0,), (1,)), ((), ())), preferred_element_type=F32
    ).astype(BF16)
    s_sib = other_core(scores)
    s_prev = next_chip(jnp.stack([scores, s_sib]), 1)
    bias_v = lax.dynamic_slice_in_dim(bias_rows[2:3], 192 * h, 192, axis=1).reshape(1, 3, 1, HDIM)
    bias_kv = jnp.concatenate([jnp.zeros_like(bias_v), bias_v], axis=2).reshape(1, 384)
    kv = (dot_nn(normed, w_kv) + bias_kv).astype(BF16)
    bias_q = lax.dynamic_slice_in_dim(bias_rows[1:2], 192 * h, 192, axis=1).reshape(192, 1)
    q = lax.dot_general(w_q, normed, (((0,), (1,)), ((), ())), preferred_element_type=F32)
    q = (q + bias_q).astype(BF16)

    padded = jnp.concatenate([jnp.full((super_rows,), -1, jnp.int32), ids_all])
    ids_win = lax.dynamic_slice_in_dim(padded, p * super_rows, 2 * super_rows)
    k_of = h ^ jnp.arange(count)
    tile_of = k_of + count * ((c + k_of) & 1)
    ids_super = ids_win[super_rows:].reshape(1, 2 * count, TILE)
    picked = tile_of[:, None, None] == jnp.arange(2 * count)[None, :, None]
    ids_q = jnp.sum(jnp.where(picked, ids_super, 0), axis=1)
    starts = jnp.sum((ids_win[None, :, None] < ids_q[:, None, :]).astype(jnp.int32), axis=1)
    lows = jnp.min(starts, axis=1) // TILE
    scal = jnp.concatenate([jnp.stack([c, h]), jnp.min(lows)[None], lows]).astype(jnp.int32)
    ds = jnp.broadcast_to(starts[:, None, :], (count, 8, TILE))

    kv, s_prev, out_same, q, ds, scal = lax.optimization_barrier(
        (kv, s_prev, out_same, q, ds, scal)
    )
    m_out = both_cores(out_same, other_core(out_same), c, 1).reshape(D, D)
    kv_prev = next_chip(kv, 1)
    kv_sib = other_core(kv)

    own_kvs, own_ss = (kv, kv_sib), (scores, s_sib)
    prev_ss = (s_prev[0], s_prev[1])
    acc, ml, pr = forward_own(count, scal, q, own_kvs, own_ss + prev_ss, ds)
    dy_mine = jnp.where(swaps, dy_other, cotangent)
    dy_sib = jnp.where(swaps, cotangent, dy_other)
    stripes = bias_rows[5:9].reshape(same, 2, down_l)
    up_half = jnp.where(c == 0, stripes[:, 0], stripes[:, 1]).reshape(1, FF // 2)
    up_half = jnp.broadcast_to(up_half, (8, FF // 2))
    kv_prev, acc, dy_mine, dy_sib, up_half = lax.optimization_barrier(
        (kv_prev, acc, dy_mine, dy_sib, up_half)
    )
    prev_kvs = (kv_prev, other_core(kv_prev))
    o, of, lse = forward_prev(count, scal, q, prev_kvs, prev_ss, ds, acc, ml, pr)

    attn = lax.all_to_all(o, "head", 0, 0).reshape(D, tok)
    middle = x_mine.astype(F32) + dot_tn(attn, m_out) + bias_rows[3]
    unit_two, scale_two = normalize(middle)
    n_two = (unit_two * gain_rows[1] + bias_rows[4]).astype(BF16)
    n_sib = other_core(n_two)
    y0, y1, d_two_0, d_two_1, g_pack, g_up_bias = hidden_passes(
        n_two, n_sib, dy_mine, dy_sib, up_half, packed
    )
    d_two = d_two_0 + other_core(d_two_1).astype(F32)
    y = y0 + other_core(y1)
    result_mine = (middle + y + bias_rows[9]).astype(BF16)
    result = jnp.where(swaps, other_core(result_mine), result_mine)

    g_up_bias = g_up_bias[0]
    g_gain_two = jnp.sum(d_two * unit_two, axis=0)
    g_shift_two = jnp.sum(d_two, axis=0)
    dy_f = dy_mine.astype(F32)
    g_down_bias = jnp.sum(dy_f, axis=0)

    d_middle = dy_f + norm_pull(d_two, unit_two, scale_two, gain_rows[1])
    d_branch = d_middle.astype(BF16)
    g_out_bias = jnp.sum(d_branch.astype(F32), axis=0)
    d_sent = dot_nt(m_out, d_branch).astype(BF16)
    d_branch, d_sent = lax.optimization_barrier((d_branch, d_sent))
    d_heads = lax.all_to_all(d_sent.reshape(groups, 192, tok), "head", 0, 0)
    g_out = dot_nn(attn, d_branch)

    g_out_rows = g_out.reshape(same, 2, rows_l, D)
    g_out_keep = jnp.where(c == 0, g_out_rows[:, 0], g_out_rows[:, 1])
    g_out_send = jnp.where(c == 0, g_out_rows[:, 1], g_out_rows[:, 0]).astype(BF16)
    g_out_same = (g_out_keep + other_core(g_out_send).astype(F32)).astype(BF16)
    if tall == 96:
        g_pack = lax.dynamic_update_slice(g_pack, g_out_same, (0, e, 0))
    else:
        g_parts = [
            g_pack[:, :96].reshape(same, a, D),
            g_pack[:, 96:144].reshape(same, b - a, D),
            g_pack[:, 144:192].reshape(same, e - b, D),
        ]
        g_pack = jnp.concatenate(g_parts + [g_out_same], axis=1)
    g_half = lax.psum_scatter(
        g_pack.reshape(groups, pairs, e + rows_l, D), "head", scatter_dimension=0, tiled=False
    )

    rows = (q, d_heads, of, lse, pr)
    dq_part, tau, prev, to_cross, s_prev_part, s_to_cross = backward_prev(
        count, scal, *rows, prev_kvs, prev_ss, ds
    )
    to_prev = (prev + other_core(to_cross).astype(F32)).astype(BF16)
    to_prev, tau = lax.optimization_barrier((to_prev, tau))
    back = next_chip(to_prev, -1)
    s_back = next_chip((s_prev_part + other_core(s_to_cross).astype(F32)).astype(BF16), -1)
    dq, own, to_sib, s_own, s_to_sib, carry = backward_own(
        count, scal, *rows, own_kvs, own_ss, ds, dq_part, tau
    )
    carry = next_chip(carry + other_core(carry), -1)
    back, s_back, to_sib, s_to_sib = lax.optimization_barrier((back, s_back, to_sib, s_to_sib))
    sib_kv, sib_s = other_core(to_sib), other_core(s_to_sib)

    sib_kv, g_half = lax.optimization_barrier((sib_kv, g_half))

    continued = (ids_q == ids_win[-1]).astype(jnp.int32).reshape(1, block)
    continued = jnp.broadcast_to(continued, (8, block))
    cat, d_norm_sum, *d_norm_low, sums, cols = project_back(
        count, scal, own, sib_kv, back, dq, s_own, sib_s, s_back, scores, continued, carry, x_low, w_both[:, :640]
    )
    cat, d_norm_low = lax.optimization_barrier((cat, d_norm_low))
    for r in range(1, groups):
        d_norm_sum = d_norm_sum + across(d_norm_low[r - 1], r).astype(F32)

    mine = jnp.arange(D) // 192 == h
    g_q_bias = jnp.where(mine, jnp.tile(cols[0, 384:576], groups), 0.0)
    g_v_bias = cols[0, :384].reshape(3, 2, HDIM)[:, 1].reshape(192)
    g_v_bias = jnp.where(mine, jnp.tile(g_v_bias, groups), 0.0)
    halves = jnp.stack([g_up_bias.reshape(same, down_l)] * 2, axis=1)
    halves = jnp.where(jnp.arange(2)[None, :, None] == c, halves, 0.0).reshape(4, D)
    g_bias_rows = jnp.concatenate(
        [
            jnp.stack([sums[1], g_q_bias, g_v_bias, g_out_bias, g_shift_two]),
            halves,
            g_down_bias[None],
        ],
        axis=0,
    )
    small = jnp.concatenate(
        [jnp.stack([sums[0], g_gain_two]).reshape(D, 2), g_bias_rows.reshape(D, 10)], axis=1
    )
    g_all = dot_tn(normed, cat) + jnp.pad(small, ((0, 0), (588, 40)))
    g_all = g_all.astype(BF16)
    came = lax.all_to_all(g_all, ALL, 0, 0, tiled=True)
    g_pack = lax.psum_scatter(g_half, "pair", scatter_dimension=0, tiled=False).astype(F32)
    grad_w_down = g_pack[:a].reshape(-1)
    grad_w_out = g_pack[e:].reshape(-1)
    g_up_rows = jnp.concatenate([g_pack[a:b], g_pack[b:e]], axis=1).reshape(2, rows_l, FF // 2)
    g_up_keep = jnp.where(c == 0, g_up_rows[0], g_up_rows[1])
    g_up_came = other_core(jnp.where(c == 0, g_up_rows[1], g_up_rows[0]))
    grad_w_up = both_cores(
        g_up_keep.reshape(rows_l, same, down_l), g_up_came.reshape(rows_l, same, down_l), c, 2
    ).reshape(-1)
    came, grad_w_down, grad_w_out, grad_w_up = lax.optimization_barrier(
        (came, grad_w_down, grad_w_out, grad_w_up)
    )
    came = came.astype(F32)
    came = jnp.sum(came.reshape(groups, 2 * pairs, rows_l, 640), axis=1)
    grad_kv = came[:, :, :384].reshape(groups, rows_l, 3, 2, HDIM)
    grad_kv = grad_kv.transpose(1, 3, 0, 2, 4).reshape(rows_l, 2, D)
    grad_q = came[:, :, 384:576].transpose(1, 0, 2).reshape(rows_l, 1, D)
    grad_w_qkv = jnp.concatenate([grad_q, grad_kv], axis=1).reshape(-1)
    small_sum = jnp.sum(came[:, :, 576:600], axis=0)
    grad_w_score = small_sum[:, :12].reshape(-1)
    grad_gains = small_sum[:, 12:14].reshape(-1)
    grad_biases = small_sum[:, 14:24].reshape(-1)

    unit_mine, scale_mine = unit_one[:tok], scale_one[:tok]
    grad_mine = d_middle + norm_pull(d_norm_sum, unit_mine, scale_mine, gain_rows[0])
    grad_mine = grad_mine.astype(BF16)
    grad_tokens = jnp.where(swaps, other_core(grad_mine), grad_mine)
    return (
        result,
        grad_tokens,
        grad_gains,
        grad_biases,
        grad_w_qkv,
        grad_w_score,
        grad_w_out,
        grad_w_up,
        grad_w_down,
    )


def solution(mesh):
    groups = mesh.devices.shape[0]
    fine = Mesh(mesh.devices.reshape(groups, -1, 2), ALL)
    rows = P(("pair", "core", "head"), None)
    flat = P(ALL)
    in_specs = (rows, P(("pair", "core", "head"))) + (flat,) * 7 + (rows,)
    out_specs = (rows, rows) + (flat,) * 7
    return jax.shard_map(shards, mesh=fine, in_specs=in_specs, out_specs=out_specs, check_vma=False)
```

```python
import functools
import math

import jax
import jax.numpy as jnp
from jax import lax
from jax.experimental import pallas as pl
from jax.experimental.pallas import tpu as pltpu
from jax.sharding import Mesh
from jax.sharding import PartitionSpec as P

D = 768
HEADS = 12
HDIM = 64
FF = 3072
WINDOW = 64
KEEP = 64
MOST = 2000

EPS = 1e-05
NEGATIVE = -1e30
TINY = 1e-37
TILE = 256
ROOT = 1.0 / math.sqrt(HDIM)
F32 = jnp.float32
BF16 = jnp.bfloat16
ALL = ("head", "pair", "core")
SAME = ("head", "pair")


def dot_nn(a, b):
    return lax.dot_general(a, b, (((1,), (0,)), ((), ())), preferred_element_type=F32)


def dot_nt(a, b):
    return lax.dot_general(a, b, (((1,), (1,)), ((), ())), preferred_element_type=F32)


def dot_tn(a, b):
    return lax.dot_general(a, b, (((0,), (0,)), ((), ())), preferred_element_type=F32)


def tile_place(sc, r, rel, count):
    k = sc[1] ^ r
    return k + count * ((sc[0] + rel + k) & 1)


def fill_window(sc, count, base, kv_refs, s_refs, kvw, kvt, ew):
    eye = (
        lax.broadcasted_iota(jnp.int32, (128, 128), 0)
        == lax.broadcasted_iota(jnp.int32, (128, 128), 1)
    ).astype(BF16)
    for rel in range(2):
        for r in range(count):
            place = tile_place(sc, r, rel, count)

            @pl.when(base + place >= sc[2])
            def _(rel=rel, r=r, place=place):
                block = kv_refs[rel][r * TILE : (r + 1) * TILE, :]
                kvw[place] = block
                rows = s_refs[rel][:, r * TILE : (r + 1) * TILE]
                for h in range(3):
                    kvt[place, h * 128 : (h + 1) * 128, :] = dot_nt(
                        eye, block[:, h * 128 : (h + 1) * 128]
                    ).astype(BF16)
                    pick = (lax.broadcasted_iota(jnp.int32, (8, 128), 0) == h).astype(BF16)
                    ew[place * 3 + h] = jnp.exp(dot_tn(rows, pick))


def twice(x):
    return jnp.concatenate([x, x], axis=1)


def key_iota():
    return lax.broadcasted_iota(jnp.int32, (TILE, TILE), 0)


def query_iota():
    return lax.broadcasted_iota(jnp.int32, (1, TILE), 1)


def column(r):
    return pl.ds(pl.multiple_of(r * TILE, TILE), TILE)


def padded_queries(q_ref, r):
    zero = jnp.zeros((64, TILE), BF16)
    q_all = q_ref[:, column(r)] * BF16(ROOT)
    return [
        jnp.concatenate([q_all[64 * h : 64 * h + 64, :], zero], axis=0) for h in range(3)
    ]


def chunk_masks(ds_row, place, j, edge):
    k_io = key_iota()
    mask = k_io >= ds_row - j * TILE
    near = None
    if edge:
        ahead = query_iota() + (place - j) * TILE
        mask = mask & (k_io <= ahead)
        near = k_io > ahead - WINDOW
    return mask, near


def fwd_chunk(state, j, slot, edge, place, ds_row, q_pad, p_rows, kvw, kvt, ew, acc):
    mask, near = chunk_masks(ds_row, place, j, edge)
    zs = [dot_nn(kvw[slot, :, h * 128 : (h + 1) * 128], q_pad[h]) for h in range(3)]
    out, probs, alphas = [], [], []
    for h in range(3):
        m_old, l_old = state[2 * h], state[2 * h + 1]
        z = jnp.where(mask, zs[h], NEGATIVE)
        m_new = jnp.maximum(m_old, jnp.max(z, axis=0, keepdims=True))
        e = twice(ew[slot * 3 + h])
        sig = e / (e + p_rows[h])
        if edge:
            sig = jnp.where(near, 1.0, sig)
        prob = jnp.exp(z - m_new) * sig
        alphas.append(jnp.exp(m_old - m_new))
        out += [m_new, l_old * alphas[h] + jnp.sum(prob, axis=0, keepdims=True)]
        probs.append(prob.astype(BF16))
    for h in range(3):
        acc[h] = acc[h] * alphas[h] + dot_nn(kvt[slot, h * 128 + 64 : (h + 1) * 128, :], probs[h])
    return tuple(out)


def fwd_own_kernel(count, sc, q_ref, kv0, kv1, s0, s1, s2, s3, ds_ref, acc_ref, ml_ref, p_ref,
                   kvw, kvt, ew, er, acc):
    base = 2 * count
    fill_window(sc, count, base, (kv0, kv1), (s0, s1), kvw, kvt, ew)
    for part, refs in enumerate(((s2, s3), (s0, s1))):
        for rel in range(2):
            for r in range(count):
                place = part * base + tile_place(sc, r, rel, count)
                er[place] = jnp.exp(refs[rel][:, r * TILE : (r + 1) * TILE].astype(F32))

    def one_tile(r, unused):
        place = base + tile_place(sc, r, 0, count)
        low = sc[3 + r]
        ds_row = ds_ref[r][0:1, :]
        tile_start = place * TILE
        q_pad = padded_queries(q_ref, r)
        k_io = key_iota()
        inside = (k_io >= ds_row - tile_start) & (k_io <= query_iota())
        ds_first = jnp.min(ds_row, axis=1, keepdims=True)
        lane = lax.broadcasted_iota(jnp.int32, (8, TILE), 1)

        def carry_step(j, sums):
            return sums + jnp.where(lane >= ds_first - j * TILE, er[j], 0.0)

        carried = lax.fori_loop(low, place, carry_step, jnp.zeros((8, TILE), F32))
        carried = jnp.sum(carried, axis=1, keepdims=True)
        starts_before = ds_row < tile_start
        p_rows = []
        for h in range(3):
            local = jnp.sum(
                jnp.where(inside, twice(ew[(place - base) * 3 + h]), 0.0), axis=0, keepdims=True
            )
            prefix = local + jnp.where(starts_before, carried[h : h + 1, :], 0.0)
            p_rows.append(jnp.maximum(prefix * (1.0 / KEEP), TINY))
        acc[...] = jnp.zeros_like(acc)

        def chunk(j, state, edge):
            return fwd_chunk(
                state, j, j - base, edge, place, ds_row, q_pad, p_rows, kvw, kvt, ew, acc
            )

        state = (jnp.full((1, TILE), NEGATIVE, F32), jnp.zeros((1, TILE), F32)) * 3
        low = jnp.maximum(low, base)
        edge_low = jnp.maximum(place - 1, low)
        state = lax.fori_loop(low, edge_low, lambda j, s: chunk(j, s, False), state)
        state = lax.fori_loop(edge_low, place + 1, lambda j, s: chunk(j, s, True), state)
        zero = jnp.zeros((2, TILE), F32)
        acc_ref[r] = jnp.concatenate([acc[0], acc[1], acc[2]], axis=0)
        ml_ref[r] = jnp.concatenate(list(state[0::2]) + list(state[1::2]) + [zero], axis=0)
        p_ref[r] = jnp.concatenate(p_rows + p_rows + [zero], axis=0)
        return unused

    lax.fori_loop(0, count, one_tile, 0)


def fwd_prev_kernel(count, sc, q_ref, kv0, kv1, s0, s1, ds_ref, acc_ref, ml_ref, p_ref,
                    o_ref, of_ref, lse_ref, kvw, kvt, ew, acc):
    base = 2 * count
    fill_window(sc, count, 0, (kv0, kv1), (s0, s1), kvw, kvt, ew)

    def one_tile(r, unused):
        place = base + tile_place(sc, r, 0, count)
        low = sc[3 + r]
        ds_row = ds_ref[r][0:1, :]
        q_pad = padded_queries(q_ref, r)
        ml = ml_ref[r]
        p_all = p_ref[r]
        p_rows = [p_all[h : h + 1, :] for h in range(3)]
        before = acc_ref[r]
        for h in range(3):
            acc[h] = before[64 * h : 64 * h + 64, :]

        def chunk(j, state, edge):
            return fwd_chunk(state, j, j, edge, place, ds_row, q_pad, p_rows, kvw, kvt, ew, acc)

        state = ()
        for h in range(3):
            state += (ml[h : h + 1, :], ml[3 + h : 4 + h, :])
        edge_low = jnp.maximum(place - 1, low)
        state = lax.fori_loop(
            low, jnp.minimum(edge_low, base), lambda j, s: chunk(j, s, False), state
        )
        state = lax.fori_loop(edge_low, base, lambda j, s: chunk(j, s, True), state)
        stacked = jnp.concatenate([acc[h] / state[2 * h + 1] for h in range(3)], axis=0)
        of_ref[r] = stacked
        o_ref[sc[1] ^ r] = stacked.astype(BF16)
        lse = [state[2 * h] + jnp.log(state[2 * h + 1]) for h in range(3)]
        lse_ref[r] = jnp.concatenate(lse + lse + [jnp.zeros((2, TILE), F32)], axis=0)
        return unused

    lax.fori_loop(0, count, one_tile, 0)


def bwd_chunk(state, j, slot, edge, place, ds_row, q_pad, do_pad, both, lse, p_rows, delta,
              kvw, kvt, ew, dkv, dsl, dqt):
    mask, near = chunk_masks(ds_row, place, j, edge)
    kv = [kvw[slot, :, h * 128 : (h + 1) * 128] for h in range(3)]
    zds = [dot_nn(kv[h], both[h]) for h in range(3)]
    zs = [zd[:, :TILE] for zd in zds]
    dps = [zd[:, TILE:] for zd in zds]
    out, lows, pairs, fars = [], [], [], []
    for h in range(3):
        e = twice(ew[slot * 3 + h])
        r = 1.0 / (e + p_rows[h])
        sig = e * r
        if edge:
            sig = jnp.where(near, 1.0, sig)
        prob = jnp.exp(jnp.where(mask, zs[h] - lse[h], NEGATIVE)) * sig
        dz = prob * (dps[h] - delta[h])
        far = dz * (p_rows[h] * r)
        if edge:
            far = jnp.where(near, 0.0, far)
        out.append(state[h] - jnp.sum(far, axis=0, keepdims=True))
        fars.append(far[:, :128] + far[:, 128:])
        lows.append(dz.astype(BF16))
        pairs.append(jnp.concatenate([lows[h], prob.astype(BF16)], axis=1))
    grads = [dot_nt(pairs[h], both[h]) for h in range(3)]
    for h in range(3):
        dqt[h] += dot_nn(kvt[slot, h * 128 : h * 128 + 64, :], lows[h])
    dkv[slot] += jnp.concatenate(grads, axis=1)
    for h in range(3):
        dsl[slot * 3 + h] += fars[h]
    return tuple(out)


def bwd_rows(r, sc, q_ref, do_ref, of_ref, lse_ref, p_ref):
    q_pad = padded_queries(q_ref, r)
    do_all = do_ref[sc[1] ^ r]
    lse_all, p_all, of = lse_ref[r], p_ref[r], of_ref[r]
    zero = jnp.zeros((64, TILE), BF16)
    do_pad, both, lse, p_rows, delta = [], [], [], [], []
    for h in range(3):
        dh = do_all[64 * h : 64 * h + 64, :]
        do_pad.append(jnp.concatenate([zero, dh], axis=0))
        both.append(jnp.concatenate([q_pad[h], do_pad[h]], axis=1))
        lse.append(lse_all[h : h + 1, :])
        p_rows.append(p_all[h : h + 1, :])
        delta.append(
            jnp.sum(dh.astype(F32) * of[64 * h : 64 * h + 64, :], axis=0, keepdims=True)
        )
    return q_pad, do_pad, both, lse, p_rows, delta


def write_keys(sc, count, dkv, dsl, outs):
    for rel in range(2):
        big, small = outs[rel]
        for r in range(count):
            place = tile_place(sc, r, rel, count)
            big[r * TILE : (r + 1) * TILE, :] = dkv[place].astype(big.dtype)
            rows = []
            for h in range(3):
                summed = jnp.sum(dsl[place * 3 + h], axis=1, keepdims=True)
                rows.append(jnp.transpose(jnp.broadcast_to(summed, (TILE, 128)))[0:1, :])
            rows = jnp.concatenate(rows + [jnp.zeros((5, TILE), F32)], axis=0)
            small[:, r * TILE : (r + 1) * TILE] = rows.astype(small.dtype)


def bwd_prev_kernel(count, sc, q_ref, do_ref, of_ref, lse_ref, p_ref, kv0, kv1, s0, s1, ds_ref,
                    dq_ref, tau_ref, big0, big1, small0, small1, kvw, kvt, ew, dkv, dsl, dqt):
    base = 2 * count
    fill_window(sc, count, 0, (kv0, kv1), (s0, s1), kvw, kvt, ew)
    dkv[...] = jnp.zeros_like(dkv)
    dsl[...] = jnp.zeros_like(dsl)

    def one_tile(r, unused):
        place = base + tile_place(sc, r, 0, count)
        low = sc[3 + r]
        ds_row = ds_ref[r][0:1, :]
        dqt[...] = jnp.zeros_like(dqt)

        @pl.when(low >= base)
        def _():
            tau_ref[r] = jnp.zeros((8, TILE), F32)

        @pl.when(low < base)
        def _():
            rows = bwd_rows(r, sc, q_ref, do_ref, of_ref, lse_ref, p_ref)

            def chunk(j, state, edge):
                return bwd_chunk(
                    state, j, j, edge, place, ds_row, *rows, kvw, kvt, ew, dkv, dsl, dqt
                )

            state = (jnp.zeros((1, TILE), F32),) * 3
            edge_low = jnp.maximum(place - 1, low)
            state = lax.fori_loop(
                low, jnp.minimum(edge_low, base), lambda j, s: chunk(j, s, False), state
            )
            state = lax.fori_loop(edge_low, base, lambda j, s: chunk(j, s, True), state)
            tau_ref[r] = jnp.concatenate(list(state) + [jnp.zeros((5, TILE), F32)], axis=0)

        dq_ref[r] = jnp.concatenate([dqt[0], dqt[1], dqt[2]], axis=0)
        return unused

    lax.fori_loop(0, count, one_tile, 0)
    write_keys(sc, count, dkv, dsl, ((big0, small0), (big1, small1)))


def bwd_own_kernel(count, sc, q_ref, do_ref, of_ref, lse_ref, p_ref, kv0, kv1, s0, s1, ds_ref,
                   dqp_ref, tau_ref, dq_ref, big0, big1, small0, small1, carry_ref,
                   kvw, kvt, ew, dkv, dsl, dqt):
    base = 2 * count
    fill_window(sc, count, base, (kv0, kv1), (s0, s1), kvw, kvt, ew)
    dkv[...] = jnp.zeros_like(dkv)
    dsl[...] = jnp.zeros_like(dsl)
    carry_ref[...] = jnp.zeros_like(carry_ref)

    def one_tile(r, unused):
        place = base + tile_place(sc, r, 0, count)
        low = sc[3 + r]
        ds_row = ds_ref[r][0:1, :]
        tile_start = place * TILE
        rows = bwd_rows(r, sc, q_ref, do_ref, of_ref, lse_ref, p_ref)
        p_rows = rows[4]
        before = dqp_ref[r]
        for h in range(3):
            dqt[h] = before[64 * h : 64 * h + 64, :]

        def chunk(j, state, edge):
            return bwd_chunk(
                state, j, j - base, edge, place, ds_row, *rows, kvw, kvt, ew, dkv, dsl, dqt
            )

        tau = tau_ref[r]
        state = tuple(tau[h : h + 1, :] for h in range(3))
        low = jnp.maximum(low, base)
        edge_low = jnp.maximum(place - 1, low)
        state = lax.fori_loop(low, edge_low, lambda j, s: chunk(j, s, False), state)
        state = lax.fori_loop(edge_low, place + 1, lambda j, s: chunk(j, s, True), state)
        dq_ref[:, column(r)] = (
            jnp.concatenate([dqt[0], dqt[1], dqt[2]], axis=0) * ROOT
        ).astype(BF16)

        k_io = key_iota()
        inside = (k_io >= ds_row - tile_start) & (k_io <= query_iota())
        ds_first = jnp.min(ds_row, axis=1, keepdims=True)
        slot = place - base
        w_lane = []
        for h in range(3):
            w = state[h] / (p_rows[h] * float(KEEP))
            earlier = jnp.where(ds_row < tile_start, w, 0.0)
            w_lane.append(earlier[:, :128] + earlier[:, 128:])
            here = jnp.where(inside, w, 0.0)
            dsl[slot * 3 + h] += ew[slot * 3 + h] * (here[:, :128] + here[:, 128:])
            further = jnp.where(ds_row < base * TILE, w, 0.0)
            carry_ref[h : h + 1, :] += further[:, :128] + further[:, 128:]

        def later(j, unused):
            keep = lax.broadcasted_iota(jnp.int32, (TILE, 128), 0) >= ds_first - j * TILE
            for h in range(3):
                dsl[(j - base) * 3 + h] += jnp.where(keep, ew[(j - base) * 3 + h] * w_lane[h], 0.0)
            return unused

        lax.fori_loop(low, place, later, 0)
        return unused

    lax.fori_loop(0, count, one_tile, 0)
    write_keys(sc, count, dkv, dsl, ((big0, small0), (big1, small1)))


VM = pl.BlockSpec(memory_space=pltpu.VMEM)
SM = pl.BlockSpec(memory_space=pltpu.SMEM)
MIB = 1024 * 1024


def window_scratch(count):
    return [
        pltpu.VMEM((2 * count, TILE, 384), BF16),
        pltpu.VMEM((2 * count, 384, TILE), BF16),
        pltpu.VMEM((2 * count * 3, TILE, 128), F32),
    ]


def grad_scratch(count):
    return [
        pltpu.VMEM((2 * count, TILE, 384), F32),
        pltpu.VMEM((2 * count * 3, TILE, 128), F32),
        pltpu.VMEM((3, 64, TILE), F32),
    ]


def call(body, count, name, args, outs, scratch, work, room):
    return pl.pallas_call(
        functools.partial(body, count),
        out_shape=tuple(jax.ShapeDtypeStruct(s, t) for s, t in outs),
        in_specs=[SM] + [VM] * (len(args) - 1),
        out_specs=(VM,) * len(outs),
        scratch_shapes=scratch,
        compiler_params=pltpu.CompilerParams(vmem_limit_bytes=room * MIB),
        cost_estimate=pl.CostEstimate(flops=work, bytes_accessed=work // 400, transcendentals=0),
        name=name,
    )(*args)


def forward_own(count, scal, q, kvs, ss, ds):
    outs = (((count, 192, TILE), F32), ((count, 8, TILE), F32), ((count, 8, TILE), F32))
    scratch = window_scratch(count) + [
        pltpu.VMEM((4 * count, 8, TILE), F32),
        pltpu.VMEM((3, 64, TILE), F32),
    ]
    return call(fwd_own_kernel, count, "forward_own", (scal, q, *kvs, *ss, ds), outs, scratch, 20 * 10**9, 18)


def forward_prev(count, scal, q, kvs, ss, ds, acc, ml, p):
    outs = (((count, 192, TILE), BF16), ((count, 192, TILE), F32), ((count, 8, TILE), F32))
    scratch = window_scratch(count) + [pltpu.VMEM((3, 64, TILE), F32)]
    args = (scal, q, *kvs, *ss, ds, acc, ml, p)
    return call(fwd_prev_kernel, count, "forward_prev", args, outs, scratch, 8 * 10**9, 18)


def key_outs(count):
    rows = count * TILE
    return (((rows, 384), F32), ((rows, 384), BF16), ((8, rows), F32), ((8, rows), BF16))


def backward_prev(count, scal, q, do, of, lse, p, kvs, ss, ds):
    outs = (((count, 192, TILE), F32), ((count, 8, TILE), F32)) + key_outs(count)
    scratch = window_scratch(count) + grad_scratch(count)
    args = (scal, q, do, of, lse, p, *kvs, *ss, ds)
    return call(bwd_prev_kernel, count, "backward_prev", args, outs, scratch, 12 * 10**9, 26)


def backward_own(count, scal, q, do, of, lse, p, kvs, ss, ds, dq, tau):
    outs = (((192, count * TILE), BF16),) + key_outs(count) + (((8, 128), F32),)
    scratch = window_scratch(count) + grad_scratch(count)
    args = (scal, q, do, of, lse, p, *kvs, *ss, ds, dq, tau)
    return call(bwd_own_kernel, count, "backward_own", args, outs, scratch, 24 * 10**9, 26)


def hidden_kernel(n0, n1, dy0, dy1, bias, down, up, y0, y1, dt0, dt1, g_ref, gb_ref,
                  n_all, dy_all, y_acc, d_acc, n_t, gd, gu, sem):
    step = pl.program_id(0)
    tok = n0.shape[0]

    @pl.when(step == 0)
    def _():
        n_all[:tok, :] = n0[...]
        n_all[tok:, :] = n1[...]
        n_t[:, :tok] = jnp.transpose(n0[...].astype(F32)).astype(BF16)
        n_t[:, tok:] = jnp.transpose(n1[...].astype(F32)).astype(BF16)
        dy_all[:tok, :] = dy0[...]
        dy_all[tok:, :] = dy1[...]
        y_acc[...] = jnp.zeros_like(y_acc)
        d_acc[...] = jnp.zeros_like(d_acc)

    n = n_all[...]
    dy = dy_all[...]
    c0 = math.sqrt(2.0 / math.pi)
    ways, wide = 2, 384
    w_up = [up[:, :, i * wide : (i + 1) * wide].reshape(D, wide) for i in range(ways)]
    w_down = [down[4 * i : 4 * i + 4].reshape(wide, D) for i in range(ways)]
    pres = [dot_nn(n, w_up[i]) + bias[0:1, i * wide : (i + 1) * wide] for i in range(ways)]
    backs = [dot_nt(dy, w_down[i]) for i in range(ways)]
    hiddens, d_ups = [], []
    for i in range(ways):
        pre = pres[i]
        squared = pre * pre
        th = jnp.tanh(c0 * pre * (1.0 + 0.044715 * squared))
        half = 0.5 * (1.0 + th)
        hiddens.append((pre * half).astype(BF16))
        slope = half + 0.5 * pre * (1.0 - th * th) * c0 * (1.0 + 3 * 0.044715 * squared)
        d_ups.append((backs[i] * slope).astype(BF16))
        gb_ref[:, i * wide : (i + 1) * wide] = jnp.broadcast_to(
            jnp.sum(d_ups[i].astype(F32), axis=0, keepdims=True), (8, wide)
        )
    hid, dup = jnp.concatenate(hiddens, axis=1), jnp.concatenate(d_ups, axis=1)
    y_acc[...] += dot_nn(hid, down[...].reshape(-1, D))
    d_acc[...] += dot_nt(dup, up[...].reshape(D, -1))
    g_down = dot_tn(hid, dy).astype(BF16).reshape(8, 96, D)
    g_up = dot_nn(n_t[...], dup).astype(BF16).reshape(16, 48, D)
    for k in range(2):

        @pl.when(step == k)
        def _(k=k):
            gd[k] = g_down
            gu[k] = g_up
            pltpu.make_async_copy(gd.at[k], g_ref.at[8 * k : 8 * k + 8, 0:96, :], sem.at[k]).start()
            pltpu.make_async_copy(
                gu.at[k], g_ref.at[:, 96 + 48 * k : 144 + 48 * k, :], sem.at[2 + k]
            ).start()


    @pl.when(step == pl.num_programs(0) - 1)
    def _():
        y0[...] = y_acc[:tok, :]
        y1[...] = y_acc[tok:, :]
        dt0[...] = d_acc[:tok, :]
        dt1[...] = d_acc[tok:, :].astype(BF16)
        for k in range(2):
            pltpu.make_async_copy(gd.at[k], g_ref.at[8 * k : 8 * k + 8, 0:96, :], sem.at[k]).wait()
            pltpu.make_async_copy(
                gu.at[k], g_ref.at[:, 96 + 48 * k : 144 + 48 * k, :], sem.at[2 + k]
            ).wait()


def hidden_passes(n0, n1, dy0, dy1, bias, packed):
    tok = n0.shape[0]
    whole = pl.BlockSpec((tok, D), lambda i: (0, 0))
    lanes = pl.BlockSpec((8, D), lambda i: (0, i))
    outs = (
        jax.ShapeDtypeStruct((tok, D), F32),
        jax.ShapeDtypeStruct((tok, D), F32),
        jax.ShapeDtypeStruct((tok, D), F32),
        jax.ShapeDtypeStruct((tok, D), BF16),
        jax.ShapeDtypeStruct((16, 216, D), BF16),
        jax.ShapeDtypeStruct((8, FF // 2), F32),
    )
    return pl.pallas_call(
        hidden_kernel,
        grid=(2,),
        out_shape=outs,
        in_specs=[
            whole,
            whole,
            whole,
            whole,
            lanes,
            pl.BlockSpec((8, 96, D), lambda i: (i, 0, 0)),
            pl.BlockSpec((16, 48, D), lambda i: (0, 2 + i, 0)),
        ],
        out_specs=(
            whole,
            whole,
            whole,
            whole,
            pl.BlockSpec(memory_space=pl.ANY),
            lanes,
        ),
        scratch_shapes=[
            pltpu.VMEM((2 * tok, D), BF16),
            pltpu.VMEM((2 * tok, D), BF16),
            pltpu.VMEM((2 * tok, D), F32),
            pltpu.VMEM((2 * tok, D), F32),
            pltpu.VMEM((D, 2 * tok), BF16),
            pltpu.VMEM((2, 8, 96, D), BF16),
            pltpu.VMEM((2, 16, 48, D), BF16),
            pltpu.SemaphoreType.DMA((4,)),
        ],
        compiler_params=pltpu.CompilerParams(vmem_limit_bytes=50 * MIB),
        cost_estimate=pl.CostEstimate(flops=7 * 10**9, bytes_accessed=10**7, transcendentals=0),
        name="hidden_passes",
    )(n0, n1, dy0, dy1, bias, packed, packed)


def project_kernel(count, sc, own, sib, back, dq, s0, s1, s2, scores, cond, carry, x, w,
                   cat_ref, dn0_ref, dn1_ref, dn2_ref, dn3_ref, sums_ref, cols_ref):
    place = (
        lax.broadcasted_iota(jnp.int32, (8, 64), 1)
        == lax.broadcasted_iota(jnp.int32, (8, 64), 0) + 3 * sc[1]
    ).astype(BF16)
    real = lax.broadcasted_iota(jnp.int32, (8, TILE), 0) < 3
    sums_ref[...] = jnp.zeros_like(sums_ref)
    cols_ref[...] = jnp.zeros_like(cols_ref)
    weights = w[...]
    for r in range(count):
        at = slice(r * TILE, (r + 1) * TILE)
        d_kv = own[at, :] + sib[at, :].astype(F32) + back[at, :].astype(F32)
        d_q = jnp.transpose(dq[:, at].astype(F32))
        after = jnp.exp(scores[:, at].astype(F32)) * jnp.sum(carry[...], axis=1, keepdims=True)
        d_s = s0[:, at] + s1[:, at].astype(F32) + s2[:, at].astype(F32)
        d_s = d_s + jnp.where(cond[0:1, at] > 0, after, 0.0)
        d_s = jnp.transpose(jnp.where(real, d_s, 0.0)).astype(BF16)
        d_s = dot_nn(d_s, place)
        cat = jnp.concatenate([d_kv, d_q, d_s], axis=1).astype(BF16)
        cat_ref[at, :] = cat
        d_n = dot_nt(cat, weights)
        if r == 0:
            dn0_ref[...] = d_n
        else:
            (dn1_ref, dn2_ref, dn3_ref)[r - 1][...] = d_n.astype(BF16)
        unit, _ = normalize(x[at, :].astype(F32))
        sums_ref[0:1, :] += jnp.sum(d_n * unit, axis=0, keepdims=True)
        sums_ref[1:2, :] += jnp.sum(d_n, axis=0, keepdims=True)
        cols_ref[0:1, :] += jnp.sum(cat.astype(F32), axis=0, keepdims=True)


def project_back(count, *args):
    rows = count * TILE
    outs = (
        ((rows, 640), BF16),
        ((TILE, D), F32),
        ((TILE, D), BF16),
        ((TILE, D), BF16),
        ((TILE, D), BF16),
        ((8, D), F32),
        ((8, 640), F32),
    )
    return call(project_kernel, count, "project_back", args, outs, [], 10**9, 50)


def other_core(x):
    return lax.ppermute(x, "core", [(0, 1), (1, 0)])


def next_chip(x, step):
    n = lax.axis_size("pair")
    return lax.ppermute(x, "pair", [(i, i + step) for i in range(n) if 0 <= i + step < n])


def spread(x, axes):
    n = lax.axis_size(axes)
    return lax.all_to_all(jnp.broadcast_to(x[None], (n,) + x.shape), axes, 0, 0)


def both_cores(mine, theirs, core, axis):
    return jnp.where(
        core == 0, jnp.stack([mine, theirs], axis), jnp.stack([theirs, mine], axis)
    )


def normalize(rows):
    centred = rows - jnp.mean(rows, axis=-1, keepdims=True)
    scale = lax.rsqrt(jnp.mean(centred * centred, axis=-1, keepdims=True) + EPS)
    return centred * scale, scale


def norm_pull(grad, unit, scale, gain):
    inner = grad * gain
    return scale * (
        inner
        - jnp.mean(inner, axis=-1, keepdims=True)
        - unit * jnp.mean(inner * unit, axis=-1, keepdims=True)
    )


def across(x, r):
    return lax.ppermute(x, "head", [(i, i ^ r) for i in range(lax.axis_size("head"))])


def shards(tokens, segment_ids, gains, biases, w_qkv, w_score, w_out, w_up, w_down, cotangent):
    groups = lax.axis_size("head")
    pairs = lax.axis_size("pair")
    devices = groups * pairs * 2
    same = groups * pairs
    h = lax.axis_index("head")
    p = lax.axis_index("pair")
    c = lax.axis_index("core")
    tok = tokens.shape[0]
    block = groups * tok
    count = groups
    super_rows = 2 * block
    total = super_rows * pairs
    rows_l = D // devices
    down_l = FF // devices
    swaps = (h & 1) == 1

    x_other = other_core(tokens)
    dy_other = other_core(cotangent)
    x_mine = jnp.where(swaps, x_other, tokens)
    x_parts = [x_mine] + [across(x_mine, r) for r in range(1, groups)]

    part = w_qkv.astype(BF16).reshape(rows_l, 3, groups, 3, HDIM)
    part_q = part[:, 0].reshape(rows_l, groups, 192)
    part_kv = part[:, 1:].transpose(0, 2, 3, 1, 4).reshape(rows_l, groups, 384)
    id_lanes = -(-tok // rows_l)
    own_ids = jnp.pad(segment_ids.astype(BF16), (0, id_lanes * rows_l - tok))
    small = jnp.concatenate(
        [
            w_score.astype(BF16).reshape(rows_l, HEADS),
            gains.astype(BF16).reshape(rows_l, 2),
            biases.astype(BF16).reshape(rows_l, 10),
            own_ids.reshape(rows_l, id_lanes),
        ],
        axis=1,
    )
    small = jnp.broadcast_to(small[:, None], (rows_l, groups, small.shape[1]))
    part = jnp.concatenate([part_kv, part_q, small], axis=-1).transpose(1, 0, 2)
    filled = part.shape[2]
    width = -(-filled // 128) * 128
    part = jnp.pad(part, ((0, 0), (0, 0), (0, width - filled)))
    part = jnp.broadcast_to(part[:, None], (groups, pairs, rows_l, width))
    w_same = lax.all_to_all(part.reshape(same, rows_l, width), SAME, 0, 0)
    up_rows = w_up.astype(BF16).reshape(rows_l, same, 2, down_l)
    up_mine = jnp.where(c == 0, up_rows[:, :, 0], up_rows[:, :, 1]).reshape(rows_l, FF // 2)
    up_send = jnp.where(c == 0, up_rows[:, :, 1], up_rows[:, :, 0]).reshape(rows_l, FF // 2)
    up_both = both_cores(up_mine, other_core(up_send), c, 0).reshape(2 * rows_l, FF // 2)
    down_mine = w_down.astype(BF16).reshape(down_l, D)
    out_mine = w_out.astype(BF16).reshape(rows_l, D)
    a, b, e = down_l, down_l + 2 * rows_l, down_l + 4 * rows_l
    pack = jnp.concatenate([down_mine, up_both[:, :D], up_both[:, D:]], axis=0)
    packed = lax.all_gather(pack, "pair", axis=0, tiled=False)
    packed, _ = lax.optimization_barrier((packed, w_same))
    out_mine, _ = lax.optimization_barrier((out_mine, w_same))
    packed = lax.all_gather(packed, "head", axis=0, tiled=False).reshape((same,) + pack.shape)
    out_same = spread(out_mine, SAME)
    tall = down_l
    if tall != 96:
        packed = jnp.concatenate(
            [
                packed[:, :a].reshape(16, 96, D),
                packed[:, a:b].reshape(16, 48, D),
                packed[:, b:e].reshape(16, 48, D),
            ],
            axis=1,
        )

    w_sib = other_core(w_same)
    w_both = both_cores(w_same, w_sib, c, 1).reshape(D, width)
    w_tail = both_cores(w_same[:, :, 576:], w_sib[:, :, 576:], c, 1).reshape(D, width - 576)
    w_kv, w_q = w_both[:, :384], w_both[:, 384:576]
    gain_rows = w_tail[:, 12:14].reshape(2, D).astype(F32)
    bias_rows = w_tail[:, 14:24].reshape(10, D).astype(F32)
    ids_all = w_tail[:, 24 : 24 + id_lanes].reshape(devices, rows_l * id_lanes)[:, :tok]
    ids_all = ids_all.astype(jnp.int32).reshape(groups, pairs, 2, tok)
    ids_all = ids_all.transpose(1, 2, 0, 3).reshape(total)

    x_low = jnp.concatenate(x_parts, axis=0)
    x_rows = x_low.astype(F32)
    unit_one, scale_one = normalize(x_rows)
    normed = (unit_one * gain_rows[0] + bias_rows[0]).astype(BF16)
    w_s = lax.dynamic_slice_in_dim(w_tail[:, :12], 3 * h, 3, axis=1)
    w_s = jnp.pad(w_s, ((0, 0), (0, 5)))
    scores = lax.dot_general(
        w_s, normed, (((0,), (1,)), ((), ())), preferred_element_type=F32
    ).astype(BF16)
    s_sib = other_core(scores)
    s_prev = next_chip(jnp.stack([scores, s_sib]), 1)
    bias_v = lax.dynamic_slice_in_dim(bias_rows[2:3], 192 * h, 192, axis=1).reshape(1, 3, 1, HDIM)
    bias_kv = jnp.concatenate([jnp.zeros_like(bias_v), bias_v], axis=2).reshape(1, 384)
    kv = (dot_nn(normed, w_kv) + bias_kv).astype(BF16)
    bias_q = lax.dynamic_slice_in_dim(bias_rows[1:2], 192 * h, 192, axis=1).reshape(192, 1)
    q = lax.dot_general(w_q, normed, (((0,), (1,)), ((), ())), preferred_element_type=F32)
    q = (q + bias_q).astype(BF16)

    padded = jnp.concatenate([jnp.full((super_rows,), -1, jnp.int32), ids_all])
    ids_win = lax.dynamic_slice_in_dim(padded, p * super_rows, 2 * super_rows)
    k_of = h ^ jnp.arange(count)
    tile_of = k_of + count * ((c + k_of) & 1)
    ids_super = ids_win[super_rows:].reshape(1, 2 * count, TILE)
    picked = tile_of[:, None, None] == jnp.arange(2 * count)[None, :, None]
    ids_q = jnp.sum(jnp.where(picked, ids_super, 0), axis=1)
    starts = jnp.sum((ids_win[None, :, None] < ids_q[:, None, :]).astype(jnp.int32), axis=1)
    lows = jnp.min(starts, axis=1) // TILE
    scal = jnp.concatenate([jnp.stack([c, h]), jnp.min(lows)[None], lows]).astype(jnp.int32)
    ds = jnp.broadcast_to(starts[:, None, :], (count, 8, TILE))

    kv, s_prev, out_same, q, ds, scal = lax.optimization_barrier(
        (kv, s_prev, out_same, q, ds, scal)
    )
    m_out = both_cores(out_same, other_core(out_same), c, 1).reshape(D, D)
    kv_prev = next_chip(kv, 1)
    kv_sib = other_core(kv)

    own_kvs, own_ss = (kv, kv_sib), (scores, s_sib)
    prev_ss = (s_prev[0], s_prev[1])
    acc, ml, pr = forward_own(count, scal, q, own_kvs, own_ss + prev_ss, ds)
    dy_mine = jnp.where(swaps, dy_other, cotangent)
    dy_sib = jnp.where(swaps, cotangent, dy_other)
    stripes = bias_rows[5:9].reshape(same, 2, down_l)
    up_half = jnp.where(c == 0, stripes[:, 0], stripes[:, 1]).reshape(1, FF // 2)
    up_half = jnp.broadcast_to(up_half, (8, FF // 2))
    kv_prev, acc, dy_mine, dy_sib, up_half = lax.optimization_barrier(
        (kv_prev, acc, dy_mine, dy_sib, up_half)
    )
    prev_kvs = (kv_prev, other_core(kv_prev))
    o, of, lse = forward_prev(count, scal, q, prev_kvs, prev_ss, ds, acc, ml, pr)

    attn = lax.all_to_all(o, "head", 0, 0).reshape(D, tok)
    middle = x_mine.astype(F32) + dot_tn(attn, m_out) + bias_rows[3]
    unit_two, scale_two = normalize(middle)
    n_two = (unit_two * gain_rows[1] + bias_rows[4]).astype(BF16)
    n_sib = other_core(n_two)
    y0, y1, d_two_0, d_two_1, g_pack, g_up_bias = hidden_passes(
        n_two, n_sib, dy_mine, dy_sib, up_half, packed
    )
    d_two = d_two_0 + other_core(d_two_1).astype(F32)
    y = y0 + other_core(y1)
    result_mine = (middle + y + bias_rows[9]).astype(BF16)
    result = jnp.where(swaps, other_core(result_mine), result_mine)

    g_up_bias = g_up_bias[0]
    g_gain_two = jnp.sum(d_two * unit_two, axis=0)
    g_shift_two = jnp.sum(d_two, axis=0)
    dy_f = dy_mine.astype(F32)
    g_down_bias = jnp.sum(dy_f, axis=0)

    d_middle = dy_f + norm_pull(d_two, unit_two, scale_two, gain_rows[1])
    d_branch = d_middle.astype(BF16)
    g_out_bias = jnp.sum(d_branch.astype(F32), axis=0)
    d_sent = dot_nt(m_out, d_branch).astype(BF16)
    d_branch, d_sent = lax.optimization_barrier((d_branch, d_sent))
    d_heads = lax.all_to_all(d_sent.reshape(groups, 192, tok), "head", 0, 0)
    g_out = dot_nn(attn, d_branch)

    g_out_rows = g_out.reshape(same, 2, rows_l, D)
    g_out_keep = jnp.where(c == 0, g_out_rows[:, 0], g_out_rows[:, 1])
    g_out_send = jnp.where(c == 0, g_out_rows[:, 1], g_out_rows[:, 0]).astype(BF16)
    g_out_same = (g_out_keep + other_core(g_out_send).astype(F32)).astype(BF16)
    if tall == 96:
        g_pack = lax.dynamic_update_slice(g_pack, g_out_same, (0, e, 0))
    else:
        g_parts = [
            g_pack[:, :96].reshape(same, a, D),
            g_pack[:, 96:144].reshape(same, b - a, D),
            g_pack[:, 144:192].reshape(same, e - b, D),
        ]
        g_pack = jnp.concatenate(g_parts + [g_out_same], axis=1)
    g_half = lax.psum_scatter(
        g_pack.reshape(groups, pairs, e + rows_l, D), "head", scatter_dimension=0, tiled=False
    )

    rows = (q, d_heads, of, lse, pr)
    dq_part, tau, prev, to_cross, s_prev_part, s_to_cross = backward_prev(
        count, scal, *rows, prev_kvs, prev_ss, ds
    )
    to_prev = (prev + other_core(to_cross).astype(F32)).astype(BF16)
    to_prev, tau = lax.optimization_barrier((to_prev, tau))
    back = next_chip(to_prev, -1)
    s_back = next_chip((s_prev_part + other_core(s_to_cross).astype(F32)).astype(BF16), -1)
    dq, own, to_sib, s_own, s_to_sib, carry = backward_own(
        count, scal, *rows, own_kvs, own_ss, ds, dq_part, tau
    )
    carry = next_chip(carry + other_core(carry), -1)
    back, s_back, to_sib, s_to_sib = lax.optimization_barrier((back, s_back, to_sib, s_to_sib))
    sib_kv, sib_s = other_core(to_sib), other_core(s_to_sib)

    sib_kv, g_half = lax.optimization_barrier((sib_kv, g_half))

    continued = (ids_q == ids_win[-1]).astype(jnp.int32).reshape(1, block)
    continued = jnp.broadcast_to(continued, (8, block))
    cat, d_norm_sum, *d_norm_low, sums, cols = project_back(
        count, scal, own, sib_kv, back, dq, s_own, sib_s, s_back, scores, continued, carry, x_low, w_both[:, :640]
    )
    cat, d_norm_low = lax.optimization_barrier((cat, d_norm_low))
    for r in range(1, groups):
        d_norm_sum = d_norm_sum + across(d_norm_low[r - 1], r).astype(F32)

    mine = jnp.arange(D) // 192 == h
    g_q_bias = jnp.where(mine, jnp.tile(cols[0, 384:576], groups), 0.0)
    g_v_bias = cols[0, :384].reshape(3, 2, HDIM)[:, 1].reshape(192)
    g_v_bias = jnp.where(mine, jnp.tile(g_v_bias, groups), 0.0)
    halves = jnp.stack([g_up_bias.reshape(same, down_l)] * 2, axis=1)
    halves = jnp.where(jnp.arange(2)[None, :, None] == c, halves, 0.0).reshape(4, D)
    g_bias_rows = jnp.concatenate(
        [
            jnp.stack([sums[1], g_q_bias, g_v_bias, g_out_bias, g_shift_two]),
            halves,
            g_down_bias[None],
        ],
        axis=0,
    )
    small = jnp.concatenate(
        [jnp.stack([sums[0], g_gain_two]).reshape(D, 2), g_bias_rows.reshape(D, 10)], axis=1
    )
    g_all = dot_tn(normed, cat) + jnp.pad(small, ((0, 0), (588, 40)))
    g_all = g_all.astype(BF16)
    came = lax.all_to_all(g_all, ALL, 0, 0, tiled=True)
    g_pack = lax.psum_scatter(g_half, "pair", scatter_dimension=0, tiled=False).astype(F32)
    grad_w_down = g_pack[:a].reshape(-1)
    grad_w_out = g_pack[e:].reshape(-1)
    g_up_rows = jnp.concatenate([g_pack[a:b], g_pack[b:e]], axis=1).reshape(2, rows_l, FF // 2)
    g_up_keep = jnp.where(c == 0, g_up_rows[0], g_up_rows[1])
    g_up_came = other_core(jnp.where(c == 0, g_up_rows[1], g_up_rows[0]))
    grad_w_up = both_cores(
        g_up_keep.reshape(rows_l, same, down_l), g_up_came.reshape(rows_l, same, down_l), c, 2
    ).reshape(-1)
    came, grad_w_down, grad_w_out, grad_w_up = lax.optimization_barrier(
        (came, grad_w_down, grad_w_out, grad_w_up)
    )
    came = came.astype(F32)
    came = jnp.sum(came.reshape(groups, 2 * pairs, rows_l, 640), axis=1)
    grad_kv = came[:, :, :384].reshape(groups, rows_l, 3, 2, HDIM)
    grad_kv = grad_kv.transpose(1, 3, 0, 2, 4).reshape(rows_l, 2, D)
    grad_q = came[:, :, 384:576].transpose(1, 0, 2).reshape(rows_l, 1, D)
    grad_w_qkv = jnp.concatenate([grad_q, grad_kv], axis=1).reshape(-1)
    small_sum = jnp.sum(came[:, :, 576:600], axis=0)
    grad_w_score = small_sum[:, :12].reshape(-1)
    grad_gains = small_sum[:, 12:14].reshape(-1)
    grad_biases = small_sum[:, 14:24].reshape(-1)

    unit_mine, scale_mine = unit_one[:tok], scale_one[:tok]
    grad_mine = d_middle + norm_pull(d_norm_sum, unit_mine, scale_mine, gain_rows[0])
    grad_mine = grad_mine.astype(BF16)
    grad_tokens = jnp.where(swaps, other_core(grad_mine), grad_mine)
    return (
        result,
        grad_tokens,
        grad_gains,
        grad_biases,
        grad_w_qkv,
        grad_w_score,
        grad_w_out,
        grad_w_up,
        grad_w_down,
    )


def solution(mesh):
    groups = mesh.devices.shape[0]
    fine = Mesh(mesh.devices.reshape(groups, -1, 2), ALL)
    rows = P(("pair", "core", "head"), None)
    flat = P(ALL)
    in_specs = (rows, P(("pair", "core", "head"))) + (flat,) * 7 + (rows,)
    out_specs = (rows, rows) + (flat,) * 7
    return jax.shard_map(shards, mesh=fine, in_specs=in_specs, out_specs=out_specs, check_vma=False)
```
